32 devices in a mesh: frame: 2 (over x), pix: 16 (over z, y, core).
Axes of the slice: x: 2, y: 2, z: 4, core: 2. Of those that a mesh axis runs over, the one named last changes fastest.
Arguments:
- features: bfloat16 [2, 73728, 128], P('frame', 'pix'), may hold values from -6 to 6
- cotangent: bfloat16 [2, 73728, 128], P('frame', 'pix'), may hold values from -6 to 6
- slot_pair: int32 [16], P('pix'), may hold values from 0 to 15, each once
- crop_size: int32 [16, 2], replicated, may hold values from 40 to 112, as said below
- self_query: bfloat16 [128, 128], replicated, may hold values from -0.75 to 0.75
- self_key: bfloat16 [128, 128], replicated, may hold values from -0.5 to 0.5
- self_value: bfloat16 [128, 128], replicated, may hold values from -0.5 to 0.5
- self_merge: bfloat16 [128, 128], replicated, may hold values from -0.5 to 0.5
- self_gain: float32 [128], replicated, may hold values from 0.25 to 1.75
- self_bias: float32 [128], replicated, may hold values from -3 to 3
- cross_query: bfloat16 [128, 128], replicated, may hold values from -0.5 to 0.5
- cross_key: bfloat16 [128, 128], replicated, may hold values from -0.5 to 0.5
- cross_value: bfloat16 [128, 128], replicated, may hold values from -0.5 to 0.5
- cross_merge: bfloat16 [128, 128], replicated, may hold values from -0.5 to 0.5
- cross_gain: float32 [128], replicated, may hold values from 0.25 to 1.75
- cross_bias: float32 [128], replicated, may hold values from -3 to 3
- expand_weight: bfloat16 [256, 1024], replicated, may hold values from -0.375 to 0.375
- shrink_weight: bfloat16 [1024, 128], replicated, may hold values from -0.1875 to 0.1875
- final_gain: float32 [128], replicated, may hold values from 0.25 to 1.75
- final_bias: float32 [128], replicated, may hold values from -3 to 3
Outputs:
- features_out: bfloat16 [2, 73728, 128], P('frame', 'pix')
- input_grad: float32 [2, 73728, 128], P('frame', 'pix')
- grad_self_query: float32 [128, 128], replicated
- grad_self_key: float32 [128, 128], replicated
- grad_self_value: float32 [128, 128], replicated
- grad_self_merge: float32 [128, 128], replicated
- grad_self_gain: float32 [128], replicated
- grad_self_bias: float32 [128], replicated
- grad_cross_query: float32 [128, 128], replicated
- grad_cross_key: float32 [128, 128], replicated
- grad_cross_value: float32 [128, 128], replicated
- grad_cross_merge: float32 [128, 128], replicated
- grad_cross_gain: float32 [128], replicated
- grad_cross_bias: float32 [128], replicated
- grad_expand: float32 [256, 1024], replicated
- grad_shrink: float32 [1024, 128], replicated
- grad_final_gain: float32 [128], replicated
- grad_final_bias: float32 [128], replicated
The draws below stay inside these ranges and needn't reach their ends.
Inputs may be any that keep to these rules, and one draw needn't show every extreme that they name: `slot_pair`: each pair is held by exactly one slot; pix index i holds slot i. `crop_size`: row p is the feature height and width of pair p: (46, 62) for half of the pairs and (40, 112) for the other half.
All inputs are finite; a program needn't handle non-finite values.
Results may differ from the reference program's by a relative error of at most 0.019.
The reference program's roundings to bfloat16 on the way count: a program that leaves them out, or rounds other values in their place, can miss the bound.
Values may be sent and summed in bfloat16 or wider, within the bound.
A program may use at most 192 MiB of HBM per device.

```python
import math
import jax
import jax.numpy as jnp
from jax import lax

D = 128
FF = 1024
HA = 46
WA = 62
HB = 40
WB = 112
WSLOT = 1152
PAIRS = 16
TOKENS = 73728


def draw_crop_size(key, part):
    key = jax.random.fold_in(key, 11)
    shuffled = jax.random.permutation(key, PAIRS)
    second = (shuffled % 2).astype(jnp.int32)
    heights = HA + (HB - HA) * second
    widths = WA + (WB - WA) * second
    return jnp.stack([heights, widths], axis=1).astype(jnp.int32)


def block_scale(rng, dims, cuts, least, high):
    loudness = 1.0
    for position, shards_of in cuts:
        steps = jax.random.uniform(jax.random.fold_in(jax.random.fold_in(rng, 6), position), (shards_of,), jnp.float32, least / len(cuts), high / len(cuts))
        loudness = loudness * jnp.repeat(jnp.exp(steps), dims[position] // shards_of).reshape((-1,) + (1,) * (len(dims) - 1 - position))
    return loudness


def centred(own_key, shape, deviation, most, pieces=(), kind=jnp.bfloat16):
    array = jax.random.normal(own_key, shape, jnp.float32) * deviation
    if len(pieces) > 0:
        array = block_scale(own_key, shape, pieces, -0.22, 0.18) * array
    return jnp.clip(array, min=-most, max=most).astype(kind)


def setup_inputs(seed: int = 0) -> dict:
    keys = jax.random.split(jax.random.key(seed), 21)
    return {
        "features": centred(keys[0], (2, TOKENS, D), 1.0, 6.0, ((0, 2), (1, 16))),
        "cotangent": centred(keys[1], (2, TOKENS, D), 1.0, 6.0, ((0, 2), (1, 16))),
        "slot_pair": jax.random.permutation(keys[2], PAIRS).astype(jnp.int32),
        "crop_size": draw_crop_size(jax.random.fold_in(keys[20], 71), 0),
        "self_query": centred(keys[4], (D, D), (D // 2) ** -0.5, 0.75),
        "self_key": centred(keys[5], (D, D), D ** -0.5, 0.5),
        "self_value": centred(keys[6], (D, D), D ** -0.5, 0.5),
        "self_merge": centred(keys[7], (D, D), D ** -0.5, 0.5),
        "self_gain": jnp.clip(1.0 + 0.15 * jax.random.normal(keys[8], (D,), jnp.float32), 0.25, 1.75),
        "self_bias": centred(keys[9], (D,), 0.3, 3.0, (), jnp.float32),
        "cross_query": centred(keys[10], (D, D), D ** -0.5, 0.5),
        "cross_key": centred(keys[11], (D, D), D ** -0.5, 0.5),
        "cross_value": centred(keys[12], (D, D), D ** -0.5, 0.5),
        "cross_merge": centred(keys[13], (D, D), D ** -0.5, 0.5),
        "cross_gain": jnp.clip(1.0 + 0.15 * jax.random.normal(keys[14], (D,), jnp.float32), 0.25, 1.75),
        "cross_bias": centred(keys[15], (D,), 0.3, 3.0, (), jnp.float32),
        "expand_weight": centred(keys[16], (2 * D, FF), (2 * D) ** -0.5, 0.375),
        "shrink_weight": centred(keys[17], (FF, D), FF ** -0.5, 0.1875),
        "final_gain": jnp.clip(1.0 + 0.15 * jax.random.normal(keys[18], (D,), jnp.float32), 0.25, 1.75),
        "final_bias": centred(keys[19], (D,), 0.3, 3.0, (), jnp.float32),
    }


HIGHEST = lax.Precision.HIGHEST
NEGATIVE = -1e+30
EPSILON = 1e-05

@jax.custom_vjp
def low(v):
    return lax.optimization_barrier(v.astype(jnp.bfloat16)).astype(jnp.float32)

@jax.custom_vjp
def low_back(v):
    return v

def low_keep(v):
    return (low(v), None)

def low_pass(kept, grad):
    return (grad,)

def back_keep(v):
    return (v, None)

def back_low(kept, grad):
    return (low(grad),)
low.defvjp(low_keep, low_pass)
low_back.defvjp(back_keep, back_low)

def layer_norm(values, gain_vec, bias_vec):
    centre = lax.optimization_barrier(jnp.mean(values, axis=-1, keepdims=True))
    shifted = values - centre
    spread = lax.optimization_barrier(jnp.mean(shifted * shifted, axis=-1, keepdims=True))
    return shifted * lax.rsqrt(spread + EPSILON) * gain_vec + bias_vec

def gelu_exact(values):
    return jax.nn.gelu(values, approximate=False)

def rounded(values):
    return low(low_back(values))

def matmul(left_side, right_side):
    return jnp.dot(left_side, right_side, precision=HIGHEST)

def attend(queries, keys_all, values_all, valid_key):
    factor = 1.0 / math.sqrt(D)
    scores = low_back(jnp.einsum('fwqd,fwkd->fwqk', queries, keys_all, precision=HIGHEST) * factor)
    scores = jnp.where(valid_key, scores, NEGATIVE)
    probability = jax.nn.softmax(scores, axis=-1)
    return jnp.einsum('fwqk,fwkd->fwqd', low(probability), values_all, precision=HIGHEST)

def pair_layer(pair_rows, length, weights):
    self_query, self_key, self_value, self_merge, self_gain, self_bias, cross_query, cross_key, cross_value, cross_merge, cross_gain, cross_bias, expand_weight, shrink_weight, final_gain, final_bias = weights
    valid_key = jnp.arange(WSLOT, dtype=jnp.int32) < length.astype(jnp.int32)
    query_one = rounded(matmul(pair_rows, self_query))
    key_one = rounded(matmul(pair_rows, self_key))
    value_one = rounded(matmul(pair_rows, self_value))
    attended_one = rounded(attend(query_one, key_one, value_one, valid_key))
    merged_one = low_back(matmul(attended_one, self_merge))
    residual_one = pair_rows + layer_norm(merged_one, self_gain, self_bias)
    residual_low = low(residual_one)
    query_two = rounded(matmul(residual_low, cross_query))
    key_two = rounded(matmul(residual_low, cross_key))
    value_two = rounded(matmul(residual_low, cross_value))
    attended_two = rounded(attend(query_two, key_two[::-1], value_two[::-1], valid_key))
    merged_two = low_back(matmul(attended_two, cross_merge))
    normed_two = low(layer_norm(merged_two, cross_gain, cross_bias))
    concat_input = jnp.concatenate([residual_low, normed_two], axis=-1)
    hidden_pre = low_back(matmul(concat_input, expand_weight))
    activated = low(gelu_exact(hidden_pre))
    branch_out = low_back(matmul(activated, shrink_weight))
    result = residual_one + layer_norm(branch_out, final_gain, final_bias)
    return jnp.where(valid_key[:, None], result, jnp.zeros_like(result))

def forward_all(features_all, lengths, weights):
    stacked = jnp.transpose(features_all.reshape(2, PAIRS, 4, WSLOT, D), (1, 0, 2, 3, 4))

    def per_pair(operands):
        return pair_layer(operands[0], operands[1], weights)
    outputs = lax.map(jax.checkpoint(per_pair), (stacked, lengths))
    return jnp.transpose(outputs, (1, 0, 2, 3, 4)).reshape(2, TOKENS, D)

def reference(features, cotangent, slot_pair, crop_size, self_query, self_key, self_value, self_merge, self_gain, self_bias, cross_query, cross_key, cross_value, cross_merge, cross_gain, cross_bias, expand_weight, shrink_weight, final_gain, final_bias):
    dims_pair = crop_size[slot_pair.astype(jnp.int32)].astype(jnp.int32)
    lengths = (dims_pair[:, 0] // 2 * (dims_pair[:, 1] // 2)).astype(jnp.int32)
    weights = tuple((tensor.astype(jnp.float32) for tensor in (self_query, self_key, self_value, self_merge, self_gain, self_bias, cross_query, cross_key, cross_value, cross_merge, cross_gain, cross_bias, expand_weight, shrink_weight, final_gain, final_bias)))

    def run_layer(features_all, weight_set):
        return forward_all(features_all, lengths, weight_set)
    outputs, pullback = jax.vjp(run_layer, features.astype(jnp.float32), weights)
    grad_features, grad_weights = pullback(cotangent.astype(jnp.float32))
    factor = 1.0 / math.sqrt(2.0 * TOKENS)
    scaled = [item * factor for item in grad_weights]
    return (outputs.astype(jnp.bfloat16), grad_features, scaled[0], scaled[1], scaled[2], scaled[3], scaled[4], scaled[5], scaled[6], scaled[7], scaled[8], scaled[9], scaled[10], scaled[11], scaled[12], scaled[13], scaled[14], scaled[15])
```

```python
import functools
import math

import jax
import jax.numpy as jnp
from jax import lax
from jax.experimental import pallas as pl
from jax.experimental.pallas import tpu as pltpu
from jax.sharding import PartitionSpec as P

WSLOT = 1152
FEWEST = 704
NEGATIVE = -1e30
EPSILON = 1e-05
LOG2E = 1.4426950408889634
F32 = jnp.float32
BF16 = jnp.bfloat16
TAIL_SCALE = 0.305
TAIL_POLY = (
    0.12163973599672318,
    0.12246681749820709,
    0.10342086106538773,
    0.12102170288562775,
    -0.037976883351802826,
    0.18571697175502777,
    -0.15298834443092346,
    0.03669919818639755,
)
TILES = ((0, 256), (256, 256), (512, 256), (768, 256), (1024, 128))


def nn(left, right):
    return jnp.dot(left, right, preferred_element_type=F32)


def nt(left, right):
    return lax.dot_general(left, right, (((1,), (1,)), ((), ())), preferred_element_type=F32)


def norm_stats(values):
    centre = jnp.mean(values, axis=0, keepdims=True)
    shifted = values - centre
    spread = jnp.mean(shifted * shifted, axis=0, keepdims=True)
    inverse = lax.rsqrt(spread + EPSILON)
    return shifted * inverse, inverse


def norm_back(hat, inverse, gain, upstream):
    scaled = upstream * gain
    first = jnp.mean(scaled, axis=0, keepdims=True)
    second = jnp.mean(scaled * hat, axis=0, keepdims=True)
    return inverse * (scaled - first - hat * second)


def attend(keys, queries_t, values_t, live, exps_ref, factor):
    scale = factor * LOG2E
    stacked = jnp.concatenate([values_t, jnp.ones((16, values_t.shape[1]), BF16)], axis=0)
    outs = []
    inverses = []
    for start, size in TILES:
        part = queries_t[:, start : start + size]
        sure = nn(keys[:FEWEST], part)
        rest = nn(keys[FEWEST:], part)
        row = lax.broadcasted_iota(jnp.int32, rest.shape, 0) + FEWEST
        rest = jnp.where(row < live, rest, NEGATIVE)
        top = jnp.maximum(
            jnp.max(sure, axis=0, keepdims=True), jnp.max(rest, axis=0, keepdims=True)
        )
        top = top * scale
        exps_ref[:FEWEST, start : start + size] = jnp.exp2(sure * scale - top).astype(BF16)
        exps_ref[FEWEST:, start : start + size] = jnp.exp2(rest * scale - top).astype(BF16)
        both = nn(stacked, exps_ref[:, start : start + size])
        inverse = 1.0 / both[values_t.shape[0] : values_t.shape[0] + 1]
        outs.append(both[: values_t.shape[0]] * inverse)
        inverses.append(inverse)
    return jnp.concatenate(outs, axis=1), jnp.concatenate(inverses, axis=1)


def attend_back(exps_ref, values, keys_t, queries_t, upstream_t, inner, factor, diff_ref):
    grads = []
    for start, size in TILES:
        cols = slice(start, start + size)
        grad = nn(values, upstream_t[:, cols]) - inner[:, cols]
        diff_ref[:, cols] = (exps_ref[:, cols].astype(F32) * grad).astype(BF16)
        grads.append(nn(keys_t, diff_ref[:, cols]))
    grad_query = (jnp.concatenate(grads, axis=1) * factor).astype(BF16)
    grad_key = (nt(diff_ref[...], queries_t) * factor).astype(BF16)
    grad_value = nt(exps_ref[...], upstream_t).astype(BF16)
    return grad_query, grad_key, grad_value


def accumulate(ref, value):
    first = pl.program_id(0) == 0

    @pl.when(first)
    def _():
        ref[...] = value

    @pl.when(jnp.logical_not(first))
    def _():
        ref[...] += value


def self_forward(
    live_ref, x_ref, qvi_ref, key_ref, merge_ref, gain_ref, bias_ref,
    x1_ref, x1b_ref, out_ref, inverse_ref, exps_ref,
):
    factor = 1.0 / math.sqrt(x_ref.shape[1])
    width = x_ref.shape[1]
    x = x_ref[...]
    stacked = nt(qvi_ref[...], x)
    keys = nn(x, key_ref[...]).astype(BF16)
    out, inverse = attend(
        keys, stacked[:width].astype(BF16), stacked[width : 2 * width].astype(BF16),
        live_ref[0], exps_ref, factor,
    )
    out = out.astype(BF16)
    out_ref[...] = out
    inverse_ref[...] = inverse
    hat, _ = norm_stats(nn(merge_ref[...], out))
    x1 = stacked[2 * width :] + hat * gain_ref[...] + bias_ref[...]
    x1_ref[...] = x1
    x1b_ref[...] = x1.astype(BF16)


def cross_both(
    live_ref, x1_ref, other_ref, cot_ref, eye_ref, query_t_ref, query_ref, kv_t_ref, kv_ref,
    merge_t_ref, merge_ref, cgain_ref, cbias_ref, expand_t_ref, expand_ref, shrink_t_ref, shrink_ref,
    fgain_ref, fbias_ref,
    result_ref, part_ref, send_ref, gq_ref, gkv_ref, gmerge_ref, gexpand_ref, gshrink_ref, gvec_ref,
    exps_ref, diff_ref, act_ref, hid_ref,
):
    width = x1_ref.shape[0]
    factor = 1.0 / math.sqrt(width)
    live = live_ref[0]
    x1 = x1_ref[...]
    x1b = x1.astype(BF16)
    other = other_ref[...]
    queries_t = nn(query_t_ref[...], x1b).astype(BF16)
    kv_t = nn(kv_t_ref[...], other)
    keys_t = kv_t[:width].astype(BF16)
    values_t = kv_t[width:].astype(BF16)
    keys = kv_t[:width].T.astype(BF16)
    values = kv_t[width:].T.astype(BF16)
    out, inverse = attend(keys, queries_t, values_t, live, exps_ref, factor)
    out = out.astype(BF16)
    hat2, inverse2 = norm_stats(nn(merge_t_ref[...], out))
    normed = (hat2 * cgain_ref[...] + cbias_ref[...]).astype(BF16)
    concat = jnp.concatenate([x1b, normed], axis=0)
    col = lax.broadcasted_iota(jnp.int32, (1, WSLOT), 1)
    alive = jnp.where(col < live, 1.0, 0.0)
    grad_out = nt(eye_ref[...], cot_ref[...]) * alive

    grad_branches = []
    grad_concats = []
    fgain_grad = jnp.zeros((width, 1), F32)
    fbias_grad = jnp.zeros((width, 1), F32)
    for start, size in TILES:
        cols = slice(start, start + size)
        hidden = nn(expand_t_ref[...], concat[:, cols])
        size_z = jnp.abs(hidden)
        bell = jnp.exp2(hidden * hidden * (-0.5 * LOG2E))
        t = 1.0 / (1.0 + TAIL_SCALE * size_z)
        poly = TAIL_POLY[-1]
        for coefficient in TAIL_POLY[-2::-1]:
            poly = poly * t + coefficient
        tail = poly * t * bell
        phi = jnp.where(hidden >= 0.0, 1.0 - tail, tail)
        act = (hidden * phi).astype(BF16)
        act_ref[:, cols] = act
        slope = phi + hidden * bell * (1.0 / math.sqrt(2.0 * math.pi))
        branch = nn(shrink_t_ref[...], act)
        hat3, inverse3 = norm_stats(branch)
        result = (x1[:, cols] + hat3 * fgain_ref[...] + fbias_ref[...]) * alive[:, cols]
        result_ref[cols, :] = result.T.astype(BF16)
        up = grad_out[:, cols]
        fgain_grad += jnp.sum(up * hat3, axis=1, keepdims=True)
        fbias_grad += jnp.sum(up, axis=1, keepdims=True)
        grad_branch = norm_back(hat3, inverse3, fgain_ref[...], up).astype(BF16)
        grad_branches.append(grad_branch)
        grad_act = nn(shrink_ref[...], grad_branch)
        grad_hidden = (slope * grad_act).astype(BF16)
        hid_ref[:, cols] = grad_hidden
        grad_concats.append(nn(expand_ref[...], grad_hidden))
    accumulate(gshrink_ref, nt(act_ref[...], jnp.concatenate(grad_branches, axis=1)))
    accumulate(gexpand_ref, nt(hid_ref[...], concat))
    grad_concat = jnp.concatenate(grad_concats, axis=1)
    up = grad_concat[width:]
    cgain_grad = jnp.sum(up * hat2, axis=1, keepdims=True)
    cbias_grad = jnp.sum(up, axis=1, keepdims=True)
    grad_merged = norm_back(hat2, inverse2, cgain_ref[...], up).astype(BF16)
    accumulate(gmerge_ref, nt(out, grad_merged))
    upstream = (nn(merge_ref[...], grad_merged) * inverse).astype(BF16)
    inner = jnp.sum(upstream.astype(F32) * out.astype(F32), axis=0, keepdims=True)
    grad_query, grad_key, grad_value = attend_back(
        exps_ref, values, keys_t, queries_t, upstream, inner, factor, diff_ref
    )
    accumulate(gq_ref, nt(x1b, grad_query))
    grad_kv = jnp.concatenate([grad_key, grad_value], axis=1)
    accumulate(gkv_ref, nn(other, grad_kv))
    send_ref[...] = nt(kv_ref[...], grad_kv).astype(BF16)
    part_ref[...] = grad_out + grad_concat[:width] + nn(query_ref[...], grad_query)
    accumulate(
        gvec_ref,
        jnp.concatenate(
            [cgain_grad, cbias_grad, fgain_grad, fbias_grad, jnp.zeros((width, 4), F32)], axis=1
        ),
    )


def self_back(
    x_ref, part_ref, received_ref, out_ref, inverse_ref, exps_ref,
    qki_ref, value_ref, merge_t_ref, merge_ref, gain_ref, query_ref, kv_ref,
    grad_ref, gq_ref, gkv_ref, gmerge_ref, gvec_ref,
    diff_ref,
):
    width = x_ref.shape[1]
    factor = 1.0 / math.sqrt(width)
    x = x_ref[...]
    stacked = nt(qki_ref[...], x).astype(BF16)
    queries_t = stacked[:width]
    keys_t = stacked[width : 2 * width]
    x_t = stacked[2 * width :]
    values = nn(x, value_ref[...]).astype(BF16)
    out = out_ref[...]
    up = part_ref[...] + received_ref[...].astype(F32)
    hat, inverse = norm_stats(nn(merge_t_ref[...], out))
    gain_grad = jnp.sum(up * hat, axis=1, keepdims=True)
    bias_grad = jnp.sum(up, axis=1, keepdims=True)
    grad_merged = norm_back(hat, inverse, gain_ref[...], up).astype(BF16)
    accumulate(gmerge_ref, nt(out, grad_merged))
    upstream = (nn(merge_ref[...], grad_merged) * inverse_ref[...]).astype(BF16)
    inner = jnp.sum(upstream.astype(F32) * out.astype(F32), axis=0, keepdims=True)
    grad_query, grad_key, grad_value = attend_back(
        exps_ref, values, keys_t, queries_t, upstream, inner, factor, diff_ref
    )
    accumulate(gq_ref, nt(x_t, grad_query))
    grad_kv = jnp.concatenate([grad_key, grad_value], axis=1)
    accumulate(gkv_ref, nn(x_t, grad_kv))
    total = up + nn(query_ref[...], grad_query) + nt(kv_ref[...], grad_kv)
    grad_ref[...] = total.T
    accumulate(
        gvec_ref, jnp.concatenate([gain_grad, bias_grad, jnp.zeros((width, 6), F32)], axis=1)
    )


def whole(shape):
    return pl.BlockSpec(shape, lambda w: (0,) * len(shape))


ROWS = lambda width: pl.BlockSpec((WSLOT, width), lambda w: (w, 0))
COLS = lambda height: pl.BlockSpec((height, WSLOT), lambda w: (0, w))
SCALAR = pl.BlockSpec(memory_space=pltpu.SMEM)
LIMIT = pltpu.CompilerParams(vmem_limit_bytes=56 * 2**20)


def local(
    features,
    cotangent,
    slot_pair,
    crop_size,
    self_query,
    self_key,
    self_value,
    self_merge,
    self_gain,
    self_bias,
    cross_query,
    cross_key,
    cross_value,
    cross_merge,
    cross_gain,
    cross_bias,
    expand_weight,
    shrink_weight,
    final_gain,
    final_bias,
):
    rows, width = features.shape[1:]
    hidden = expand_weight.shape[1]
    windows = rows // WSLOT
    grad_factor = 1.0 / math.sqrt(2.0 * rows * lax.axis_size("pix"))
    pair_index = jnp.arange(crop_size.shape[0], dtype=jnp.int32)
    matches = (slot_pair[:, None] == pair_index[None, :]).astype(jnp.int32)
    dims_local = jnp.sum(matches[:, :, None] * crop_size[None, :, :], axis=1)
    live = dims_local[:, 0] // 2 * (dims_local[:, 1] // 2)
    x = features[0]
    cot = cotangent[0]
    eye = jnp.eye(width, dtype=BF16)
    column = lambda vector: vector.reshape(width, 1)
    shape = jax.ShapeDtypeStruct

    x1, x1b, out_one, inverse_one, exps_one = pl.pallas_call(
        self_forward,
        grid=(windows,),
        in_specs=[SCALAR, ROWS(width), whole((3 * width, width)), whole((width, width)),
                  whole((width, width)), whole((width, 1)), whole((width, 1))],
        out_specs=[COLS(width), COLS(width), COLS(width), COLS(1), ROWS(WSLOT)],
        out_shape=[shape((width, rows), F32), shape((width, rows), BF16), shape((width, rows), BF16),
                   shape((1, rows), F32), shape((rows, WSLOT), BF16)],
        compiler_params=LIMIT,
        name="self_forward",
    )(live, x, jnp.concatenate([self_query.T, self_value.T, eye], axis=0), self_key, self_merge.T,
      column(self_gain), column(self_bias))

    partner = [(source, 1 - source) for source in range(2)]
    other = lax.ppermute(x1b, "frame", partner)

    cross_kv = jnp.concatenate([cross_key, cross_value], axis=1)
    (result, part, send, g_cq, g_ckv, g_cmerge, g_expand, g_shrink, g_cvec) = pl.pallas_call(
        cross_both,
        grid=(windows,),
        in_specs=[SCALAR, COLS(width), COLS(width), ROWS(width), whole((width, width)),
                  whole((width, width)), whole((width, width)), whole((2 * width, width)),
                  whole((width, 2 * width)), whole((width, width)), whole((width, width)),
                  whole((width, 1)), whole((width, 1)), whole((hidden, 2 * width)),
                  whole((2 * width, hidden)), whole((width, hidden)), whole((hidden, width)),
                  whole((width, 1)), whole((width, 1))],
        out_specs=[ROWS(width), COLS(width), COLS(width), whole((width, width)),
                   whole((width, 2 * width)), whole((width, width)), whole((hidden, 2 * width)),
                   whole((hidden, width)), whole((width, 8))],
        out_shape=[shape((rows, width), BF16), shape((width, rows), F32), shape((width, rows), BF16),
                   shape((width, width), F32), shape((width, 2 * width), F32), shape((width, width), F32),
                   shape((hidden, 2 * width), F32), shape((hidden, width), F32), shape((width, 8), F32)],
        scratch_shapes=[pltpu.VMEM((WSLOT, WSLOT), BF16), pltpu.VMEM((WSLOT, WSLOT), BF16),
                        pltpu.VMEM((hidden, WSLOT), BF16), pltpu.VMEM((hidden, WSLOT), BF16)],
        compiler_params=LIMIT,
        name="cross_both",
    )(live, x1, other, cot, eye, cross_query.T, cross_query, cross_kv.T, cross_kv, cross_merge.T,
      cross_merge, column(cross_gain), column(cross_bias), expand_weight.T, expand_weight,
      shrink_weight.T, shrink_weight, column(final_gain), column(final_bias))

    received = lax.ppermute(send, "frame", partner)

    grad_input, g_sq, g_skv, g_smerge, g_svec = pl.pallas_call(
        self_back,
        grid=(windows,),
        in_specs=[ROWS(width), COLS(width), COLS(width), COLS(width), COLS(1), ROWS(WSLOT),
                  whole((3 * width, width)), whole((width, width)), whole((width, width)),
                  whole((width, width)), whole((width, 1)), whole((width, width)), whole((width, 2 * width))],
        out_specs=[ROWS(width), whole((width, width)), whole((width, 2 * width)), whole((width, width)),
                   whole((width, 8))],
        out_shape=[shape((rows, width), F32), shape((width, width), F32), shape((width, 2 * width), F32),
                   shape((width, width), F32), shape((width, 8), F32)],
        scratch_shapes=[pltpu.VMEM((WSLOT, WSLOT), BF16)],
        compiler_params=LIMIT,
        name="self_back",
    )(x, part, received, out_one, inverse_one, exps_one,
      jnp.concatenate([self_query.T, self_key.T, eye], axis=0), self_value, self_merge.T, self_merge,
      column(self_gain), self_query, jnp.concatenate([self_key, self_value], axis=1))

    sums = lax.psum(
        (g_sq, g_skv, g_smerge, g_cq, g_ckv, g_cmerge, g_expand, g_shrink, g_cvec, g_svec),
        ("frame", "pix"),
    )
    g_sq, g_skv, g_smerge, g_cq, g_ckv, g_cmerge, g_expand, g_shrink, g_cvec, g_svec = [
        value * grad_factor for value in sums
    ]
    return (
        result[None],
        grad_input[None],
        g_sq,
        g_skv[:, :width],
        g_skv[:, width:],
        g_smerge,
        g_svec[:, 0],
        g_svec[:, 1],
        g_cq,
        g_ckv[:, :width],
        g_ckv[:, width:],
        g_cmerge,
        g_cvec[:, 0],
        g_cvec[:, 1],
        g_expand.T,
        g_shrink,
        g_cvec[:, 2],
        g_cvec[:, 3],
    )


def solution(mesh):
    split = P("frame", "pix", None)
    return jax.shard_map(
        local,
        mesh=mesh,
        in_specs=(split, split, P("pix")) + (P(),) * 17,
        out_specs=(split, split) + (P(),) * 16,
        check_vma=False,
    )
```

```python
import functools
import math
import types

import jax
import jax.numpy as jnp
from jax import lax
from jax.experimental import pallas as pl
from jax.experimental.pallas import tpu as pltpu
from jax.sharding import PartitionSpec as P

WSLOT = 1152
FEWEST = 704
NEGATIVE = -1e30
EPSILON = 1e-05
LOG2E = 1.4426950408889634
F32 = jnp.float32
BF16 = jnp.bfloat16
TAIL_SCALE = 0.305
TAIL_POLY = (
    0.12163973599672318,
    0.12246681749820709,
    0.10342086106538773,
    0.12102170288562775,
    -0.037976883351802826,
    0.18571697175502777,
    -0.15298834443092346,
    0.03669919818639755,
)
TILES = ((0, 256), (256, 256), (512, 256), (768, 256), (1024, 128))


def nn(left, right):
    return jnp.dot(left, right, preferred_element_type=F32)


def nt(left, right):
    return lax.dot_general(left, right, (((1,), (1,)), ((), ())), preferred_element_type=F32)


def norm_stats(values):
    centre = jnp.mean(values, axis=0, keepdims=True)
    shifted = values - centre
    spread = jnp.mean(shifted * shifted, axis=0, keepdims=True)
    inverse = lax.rsqrt(spread + EPSILON)
    return shifted * inverse, inverse


def norm_back(hat, inverse, gain, upstream):
    scaled = upstream * gain
    first = jnp.mean(scaled, axis=0, keepdims=True)
    second = jnp.mean(scaled * hat, axis=0, keepdims=True)
    return inverse * (scaled - first - hat * second)


def attend(keys, queries_t, values_t, live, exps_ref, factor):
    scale = factor * LOG2E
    stacked = jnp.concatenate([values_t, jnp.ones((16, values_t.shape[1]), BF16)], axis=0)
    outs = []
    inverses = []
    for start, size in TILES:
        part = queries_t[:, start : start + size]
        sure = nn(keys[:FEWEST], part)
        rest = nn(keys[FEWEST:], part)
        row = lax.broadcasted_iota(jnp.int32, rest.shape, 0) + FEWEST
        rest = jnp.where(row < live, rest, NEGATIVE)
        top = jnp.maximum(
            jnp.max(sure, axis=0, keepdims=True), jnp.max(rest, axis=0, keepdims=True)
        )
        top = top * scale
        exps_ref[:FEWEST, start : start + size] = jnp.exp2(sure * scale - top).astype(BF16)
        exps_ref[FEWEST:, start : start + size] = jnp.exp2(rest * scale - top).astype(BF16)
        both = nn(stacked, exps_ref[:, start : start + size])
        inverse = 1.0 / both[values_t.shape[0] : values_t.shape[0] + 1]
        outs.append(both[: values_t.shape[0]] * inverse)
        inverses.append(inverse)
    return jnp.concatenate(outs, axis=1), jnp.concatenate(inverses, axis=1)


def attend_back(exps_ref, values, keys_t, queries_t, upstream_t, inner, factor, diff_ref):
    grads = []
    for start, size in TILES:
        cols = slice(start, start + size)
        grad = nn(values, upstream_t[:, cols]) - inner[:, cols]
        diff_ref[:, cols] = (exps_ref[:, cols].astype(F32) * grad).astype(BF16)
        grads.append(nn(keys_t, diff_ref[:, cols]))
    grad_query = (jnp.concatenate(grads, axis=1) * factor).astype(BF16)
    grad_key = (nt(diff_ref[...], queries_t) * factor).astype(BF16)
    grad_value = nt(exps_ref[...], upstream_t).astype(BF16)
    return grad_query, grad_key, grad_value


def upper_tail(values):
    bell = jnp.exp2(values * values * (-0.5 * LOG2E))
    t = 1.0 / (1.0 + TAIL_SCALE * jnp.abs(values))
    poly = TAIL_POLY[-1]
    for coefficient in TAIL_POLY[-2::-1]:
        poly = poly * t + coefficient
    tail = poly * t * bell
    return bell, jnp.where(values >= 0.0, 1.0 - tail, tail)


def flip(values):
    return values.astype(F32).T.astype(BF16)


MESH = pl.DeviceIdType.MESH
INPUTS = (
    "x", "cot", "slot", "crop", "sq", "sk", "sv", "sm", "sgain", "sbias",
    "cq", "ck", "cv", "cm", "cgain", "cbias", "we", "ws", "fgain", "fbias",
)
MATRICES = ("sq", "sk", "sv", "sm", "cq", "ck", "cv", "cm", "we", "ws")
VECTORS = ("sgain", "sbias", "cgain", "cbias", "fgain", "fbias")


def layer_kernel(sizes, *refs):
    names = INPUTS + OUTPUTS + tuple(scratch_shapes(sizes))
    r = types.SimpleNamespace(**dict(zip(names, refs, strict=True)))
    width, hidden, windows, peers = sizes.width, sizes.hidden, sizes.windows, sizes.peers
    factor = 1.0 / math.sqrt(width)
    frame = lax.axis_index("frame")
    pix = lax.axis_index("pix")
    core = lax.rem(pix, 2)
    me = frame * (peers // 2) + lax.div(pix, 2)
    partner = (1 - frame, pix)
    sibling = (frame, pix + 1 - 2 * core)

    def peer(step):
        index = lax.rem(me + step, peers)
        return index, (lax.div(index, peers // 2), lax.rem(index, peers // 2) * 2 + core)

    barrier = pltpu.get_barrier_semaphore()
    pl.semaphore_signal(barrier, inc=1, device_id=sibling, device_id_type=MESH)

    def greet(step, carry):
        pl.semaphore_signal(barrier, inc=1, device_id=peer(step)[1], device_id_type=MESH)
        return carry

    lax.fori_loop(1, peers, greet, 0)

    slot = r.slot[0]
    live = lax.shift_right_logical(r.crop[slot, 0], 1) * lax.shift_right_logical(r.crop[slot, 1], 1)

    eye = jnp.where(
        lax.broadcasted_iota(jnp.int32, (width, width), 0)
        == lax.broadcasted_iota(jnp.int32, (width, width), 1),
        1.0, 0.0,
    ).astype(BF16)
    r.self_in[:width] = flip(r.sq[...])
    r.self_in[width : 2 * width] = flip(r.sv[...])
    r.self_in[2 * width : 3 * width] = eye
    r.self_in[3 * width :] = flip(r.sk[...])
    r.self_merge_t[...] = flip(r.sm[...])
    r.self_kv[:, :width] = r.sk[...]
    r.self_kv[:, width:] = r.sv[...]
    r.vectors[...] = jnp.concatenate(
        [getattr(r, name)[...] for name in VECTORS] + [jnp.zeros((2, width), F32)], axis=0
    ).T
    vector = {name: r.vectors[:, i : i + 1] for i, name in enumerate(VECTORS)}
    for name in ("g_sq", "g_skv", "g_sm", "g_cq", "g_ckv", "g_cm", "g_we", "g_ws", "g_vec"):
        getattr(r, name)[...] = jnp.zeros_like(getattr(r, name))

    pl.semaphore_wait(barrier, peers)

    def to_partner(source, target, sems, w):
        return pltpu.make_async_remote_copy(
            src_ref=source.at[w], dst_ref=target.at[w], send_sem=sems.at[0, w], recv_sem=sems.at[1, w],
            device_id=partner, device_id_type=MESH,
        )

    def forward(w, carry):
        rows = pl.ds(pl.multiple_of(w * WSLOT, WSLOT), WSLOT)
        x = r.x[rows, :]
        stacked = nt(r.self_in[: 3 * width], x)
        keys = nn(x, r.sk[...]).astype(BF16)
        out, inverse = attend(
            keys, stacked[:width].astype(BF16), stacked[width : 2 * width].astype(BF16),
            live, r.exps.at[w], factor,
        )
        out = out.astype(BF16)
        r.out_one[w] = out
        r.inverse_one[w] = inverse
        hat, _ = norm_stats(nn(r.self_merge_t[...], out))
        x1 = stacked[2 * width :] + hat * vector["sgain"] + vector["sbias"]
        r.x1[w] = x1
        r.x1b[w] = x1.astype(BF16)
        to_partner(r.x1b, r.other, r.sem_x, w).start()
        return carry

    lax.fori_loop(0, windows, forward, 0)

    r.cross_q_t[...] = flip(r.cq[...])
    r.cross_kv_t[:width] = flip(r.ck[...])
    r.cross_kv_t[width:] = flip(r.cv[...])
    r.cross_kv[:, :width] = r.ck[...]
    r.cross_kv[:, width:] = r.cv[...]
    r.cross_merge_t[...] = flip(r.cm[...])
    r.expand_t[...] = flip(r.we[...])
    r.shrink_t[...] = flip(r.ws[...])
    col = lax.broadcasted_iota(jnp.int32, (1, WSLOT), 1)
    alive = jnp.where(col < live, 1.0, 0.0)

    def store_rows(target, stage, w, sem):
        rows = pl.ds(pl.multiple_of(w * WSLOT, WSLOT), WSLOT)
        return pltpu.make_async_copy(stage.at[rows, :], target.at[rows, :], sem.at[w])

    def middle(w, carry):
        base = pl.multiple_of(w * WSLOT, WSLOT)
        rows = pl.ds(base, WSLOT)
        x1 = r.x1[w]
        x1b = r.x1b[w]
        queries_t = nn(r.cross_q_t[...], x1b).astype(BF16)
        to_partner(r.x1b, r.other, r.sem_x, w).wait()
        other = r.other[w]
        kv_t = nn(r.cross_kv_t[...], other)
        keys_t = kv_t[:width].astype(BF16)
        keys = kv_t[:width].T.astype(BF16)
        values = kv_t[width:].T.astype(BF16)
        out, inverse = attend(keys, queries_t, kv_t[width:].astype(BF16), live, r.exps_two, factor)
        out = out.astype(BF16)
        hat2, inverse2 = norm_stats(nn(r.cross_merge_t[...], out))
        normed = (hat2 * vector["cgain"] + vector["cbias"]).astype(BF16)
        concat = jnp.concatenate([x1b, normed], axis=0)
        grad_out = nt(eye, r.cot[rows, :]) * alive

        grad_branches = []
        grad_concats = []
        fgain_grad = jnp.zeros((width, 1), F32)
        fbias_grad = jnp.zeros((width, 1), F32)
        for start, size in TILES:
            cols = slice(start, start + size)
            pre = nn(r.expand_t[...], concat[:, cols])
            bell, phi = upper_tail(pre)
            act = (pre * phi).astype(BF16)
            r.act[:, cols] = act
            slope = phi + pre * bell * (1.0 / math.sqrt(2.0 * math.pi))
            branch = nn(r.shrink_t[...], act)
            hat3, inverse3 = norm_stats(branch)
            result = (x1[:, cols] + hat3 * vector["fgain"] + vector["fbias"]) * alive[:, cols]
            r.result_stage[pl.ds(base + start, size), :] = result.T.astype(BF16)
            up = grad_out[:, cols]
            fgain_grad += jnp.sum(up * hat3, axis=1, keepdims=True)
            fbias_grad += jnp.sum(up, axis=1, keepdims=True)
            grad_branch = norm_back(hat3, inverse3, vector["fgain"], up).astype(BF16)
            grad_branches.append(grad_branch)
            grad_hidden = (slope * nn(r.ws[...], grad_branch)).astype(BF16)
            r.hid[:, cols] = grad_hidden
            grad_concats.append(nn(r.we[...], grad_hidden))
        store_rows(r.result, r.result_stage, w, r.sem_result).start()
        r.g_ws[...] += nt(r.act[...], jnp.concatenate(grad_branches, axis=1))
        r.g_we[...] += nt(r.hid[...], concat)
        grad_concat = jnp.concatenate(grad_concats, axis=1)
        up = grad_concat[width:]
        cgain_grad = jnp.sum(up * hat2, axis=1, keepdims=True)
        cbias_grad = jnp.sum(up, axis=1, keepdims=True)
        r.g_vec[...] += jnp.concatenate(
            [jnp.zeros((width, 2), F32), cgain_grad, cbias_grad, fgain_grad, fbias_grad,
             jnp.zeros((width, 2), F32)], axis=1,
        )
        grad_merged = norm_back(hat2, inverse2, vector["cgain"], up).astype(BF16)
        r.g_cm[...] += nt(out, grad_merged)
        upstream = (nn(r.cm[...], grad_merged) * inverse).astype(BF16)
        inner = jnp.sum(upstream.astype(F32) * out.astype(F32), axis=0, keepdims=True)
        grad_query, grad_key, grad_value = attend_back(
            r.exps_two, values, keys_t, queries_t, upstream, inner, factor, r.diff
        )
        grad_kv = jnp.concatenate([grad_key, grad_value], axis=1)
        r.back[w] = nt(r.cross_kv[...], grad_kv).astype(BF16)
        to_partner(r.back, r.received, r.sem_b, w).start()
        r.g_cq[...] += nt(x1b, grad_query)
        r.g_ckv[...] += nn(other, grad_kv)
        r.part[w] = grad_out + grad_concat[:width] + nn(r.cq[...], grad_query)
        return carry

    lax.fori_loop(0, windows, middle, 0)

    early = Reduction(r, sizes, "early", sibling, peer, core, me)
    late = Reduction(r, sizes, "late", sibling, peer, core, me)
    pieces = ((r.g_we, 0), (r.g_we, width), (r.g_ws, 0), (r.g_cq, 0), (r.g_ckv, 0), (r.g_ckv, width), (r.g_cm, 0))
    early.begin([ref.at[:, pl.ds(start, width)] for ref, start in pieces])

    def backward(w, carry):
        rows = pl.ds(pl.multiple_of(w * WSLOT, WSLOT), WSLOT)

        @pl.when(w == 1)
        def _():
            early.scatter()

        @pl.when(w == 3)
        def _():
            early.gather()

        x = r.x[rows, :]
        queries_t = nt(r.self_in[:width], x).astype(BF16)
        stacked = nt(r.self_in[2 * width :], x).astype(BF16)
        x_t = stacked[:width]
        keys_t = stacked[width:]
        values = nn(x, r.sv[...]).astype(BF16)
        out = r.out_one[w]
        hat, inverse = norm_stats(nn(r.self_merge_t[...], out))
        to_partner(r.back, r.received, r.sem_b, w).wait()
        up = r.part[w] + r.received[w].astype(F32)
        gain_grad = jnp.sum(up * hat, axis=1, keepdims=True)
        bias_grad = jnp.sum(up, axis=1, keepdims=True)
        r.g_vec[...] += jnp.concatenate([gain_grad, bias_grad, jnp.zeros((width, 6), F32)], axis=1)
        grad_merged = norm_back(hat, inverse, vector["sgain"], up).astype(BF16)
        r.g_sm[...] += nt(out, grad_merged)
        upstream = (nn(r.sm[...], grad_merged) * r.inverse_one[w]).astype(BF16)
        inner = jnp.sum(upstream.astype(F32) * out.astype(F32), axis=0, keepdims=True)
        grad_query, grad_key, grad_value = attend_back(
            r.exps.at[w], values, keys_t, queries_t, upstream, inner, factor, r.diff
        )
        r.g_sq[...] += nt(x_t, grad_query)
        grad_kv = jnp.concatenate([grad_key, grad_value], axis=1)
        r.g_skv[...] += nn(x_t, grad_kv)
        total = up + nn(r.sq[...], grad_query) + nt(r.self_kv[...], grad_kv)
        r.grad_stage[rows, :] = total.T
        store_rows(r.grad, r.grad_stage, w, r.sem_grad).start()
        return carry

    lax.fori_loop(0, windows, backward, 0)

    pieces = ((r.g_sq, 0), (r.g_skv, 0), (r.g_skv, width), (r.g_sm, 0))
    late.begin([ref.at[:, pl.ds(start, width)] for ref, start in pieces], r.g_vec)
    early.share()
    late.scatter()
    early.finish()
    place = early.rows_of
    r.o_we[:width, :] = place(0, hidden).T
    r.o_we[width:, :] = place(hidden, hidden).T
    r.o_ws[...] = place(2 * hidden, hidden)
    for i, name in enumerate(("o_cq", "o_ck", "o_cv", "o_cm")):
        getattr(r, name)[...] = place(3 * hidden + i * width, width)
    late.gather()
    late.share()
    totals = late.vector_total()
    for i, name in enumerate(VECTORS):
        getattr(r, "o_" + name)[...] = totals[i : i + 1]
    late.finish()
    for i, name in enumerate(("o_sq", "o_sk", "o_sv", "o_sm")):
        getattr(r, name)[...] = late.rows_of(i * width, width)

    def drain(w, carry):
        store_rows(r.result, r.result_stage, w, r.sem_result).wait()
        store_rows(r.grad, r.grad_stage, w, r.sem_grad).wait()
        return carry

    lax.fori_loop(0, windows, drain, 0)


class Reduction:
    def __init__(self, r, sizes, name, sibling, peer, core, me):
        self.sizes = sizes
        self.sibling, self.peer, self.core, self.me = sibling, peer, core, me
        self.peers = sizes.peers
        self.scale = sizes.scale
        self.shard = sizes.shards[name]
        self.extra = sizes.extras[name]
        self.half = sizes.peers * self.shard
        for field in ("pack", "from_sibling", "parcels", "inbox", "total", "sems"):
            setattr(self, field, getattr(r, name + "_" + field))
        self.vec, self.vec_in = r.late_vec, r.late_vec_in

    def copy(self, source, target, number, device):
        return pltpu.make_async_remote_copy(
            src_ref=source, dst_ref=target, send_sem=self.sems.at[0, number],
            recv_sem=self.sems.at[1, number], device_id=device, device_id_type=MESH,
        )

    def halves(self):
        return self.copy(self.pack.at[1 - self.core], self.from_sibling, 0, self.sibling)

    def vectors(self):
        return self.copy(self.vec, self.vec_in, 4, self.sibling)

    def begin(self, pieces, vec=None):
        flat = sum(piece.shape[0] for piece in pieces)
        at = 0
        for piece in pieces:
            taken = 0
            while taken < piece.shape[0]:
                which, inside = divmod(at, self.half)
                count = min(piece.shape[0] - taken, self.half - inside)
                self.pack[which, inside : inside + count] = piece[taken : taken + count, :].astype(BF16)
                at += count
                taken += count
        while at < 2 * self.half:
            which, inside = divmod(at, self.half)
            count = self.half - inside
            self.pack[which, inside:] = jnp.zeros((count, self.pack.shape[2]), BF16)
            at += count
        self.halves().start()
        if self.extra:
            self.vec[...] = jnp.concatenate(
                [vec[...].T, jnp.zeros((8, vec.shape[0]), F32)], axis=0
            ).astype(BF16)
            self.vectors().start()

    def parcel(self, step, reverse=False):
        index, device = self.peer(step)
        return self.copy(self.parcels.at[index], self.inbox.at[self.me], 1, device)

    def arrivals(self, number, ref):
        few = ref.at[pl.ds(0, self.peers - 1)]
        return self.copy(few, few, number, self.sibling)

    def scatter(self):
        shape = (self.peers, self.shard, self.pack.shape[2])
        self.halves().wait()
        mine = self.pack[self.core].astype(F32) + self.from_sibling[...].astype(F32)
        mine = mine.astype(BF16).reshape(shape)
        self.parcels[:, : self.shard] = mine
        if self.extra:
            self.vectors().wait()
            both = (self.vec[...].astype(F32) + self.vec_in[...].astype(F32)).astype(BF16)
            self.parcels[:, self.shard :] = jnp.broadcast_to(
                both[None], (self.peers, self.extra, both.shape[1])
            )

        def send(step, carry):
            self.parcel(step).start()
            return carry

        lax.fori_loop(1, self.peers, send, 0)
        self.inbox[self.me] = self.parcels[self.me]

    def gather(self):
        arrivals = self.arrivals(1, self.inbox)
        arrivals.wait_send()
        arrivals.wait_recv()
        total = jnp.sum(self.inbox[:, : self.shard].astype(F32), axis=0) * self.scale
        self.total[self.core, self.me] = total.astype(BF16)

        def send(step, carry):
            _, device = self.peer(step)
            place = self.total.at[self.core, self.me]
            self.copy(place, place, 2, device).start()
            return carry

        lax.fori_loop(1, self.peers, send, 0)

    def vector_total(self):
        return jnp.sum(self.inbox[:, self.shard :].astype(F32), axis=0) * self.scale

    def share(self):
        arrivals = self.arrivals(2, self.total.at[self.core])
        arrivals.wait_send()
        arrivals.wait_recv()
        self.copy(self.total.at[self.core], self.total.at[self.core], 3, self.sibling).start()

    def finish(self):
        self.copy(self.total.at[self.core], self.total.at[self.core], 3, self.sibling).wait()

    def rows_of(self, start, count):
        at = start
        found = []
        while at < start + count:
            which, inside = divmod(at, self.half)
            index, offset = divmod(inside, self.shard)
            if offset or start + count - at < self.shard:
                take = min(self.shard - offset, start + count - at)
                found.append(self.total[which, index, offset : offset + take].astype(F32))
            else:
                blocks = min((start + count - at) // self.shard, self.peers - index)
                take = blocks * self.shard
                found.append(
                    self.total[which, index : index + blocks].astype(F32).reshape(take, self.total.shape[3])
                )
            at += take
        return found[0] if len(found) == 1 else jnp.concatenate(found, axis=0)


OUTPUTS = (
    "result", "grad", "o_sq", "o_sk", "o_sv", "o_sm", "o_sgain", "o_sbias",
    "o_cq", "o_ck", "o_cv", "o_cm", "o_cgain", "o_cbias", "o_we", "o_ws", "o_fgain", "o_fbias",
)


def scratch_shapes(sizes):
    width, hidden, windows, rows, peers = sizes.width, sizes.hidden, sizes.windows, sizes.rows, sizes.peers
    vmem = pltpu.VMEM
    dma = pltpu.SemaphoreType.DMA
    shapes = {
        "self_in": vmem((4 * width, width), BF16),
        "self_merge_t": vmem((width, width), BF16),
        "self_kv": vmem((width, 2 * width), BF16),
        "vectors": vmem((width, 8), F32),
        "cross_q_t": vmem((width, width), BF16),
        "cross_kv_t": vmem((2 * width, width), BF16),
        "cross_kv": vmem((width, 2 * width), BF16),
        "cross_merge_t": vmem((width, width), BF16),
        "expand_t": vmem((hidden, 2 * width), BF16),
        "shrink_t": vmem((width, hidden), BF16),
        "g_sq": vmem((width, width), F32),
        "g_skv": vmem((width, 2 * width), F32),
        "g_sm": vmem((width, width), F32),
        "g_cq": vmem((width, width), F32),
        "g_ckv": vmem((width, 2 * width), F32),
        "g_cm": vmem((width, width), F32),
        "g_we": vmem((hidden, 2 * width), F32),
        "g_ws": vmem((hidden, width), F32),
        "g_vec": vmem((width, 8), F32),
        "out_one": vmem((windows, width, WSLOT), BF16),
        "inverse_one": vmem((windows, 1, WSLOT), F32),
        "x1": vmem((windows, width, WSLOT), F32),
        "x1b": vmem((windows, width, WSLOT), BF16),
        "other": vmem((windows, width, WSLOT), BF16),
        "part": vmem((windows, width, WSLOT), F32),
        "back": vmem((windows, width, WSLOT), BF16),
        "received": vmem((windows, width, WSLOT), BF16),
        "exps": vmem((windows, WSLOT, WSLOT), BF16),
        "exps_two": vmem((WSLOT, WSLOT), BF16),
        "diff": vmem((WSLOT, WSLOT), BF16),
        "act": vmem((hidden, WSLOT), BF16),
        "hid": vmem((hidden, WSLOT), BF16),
        "result_stage": vmem((rows, width), BF16),
        "grad_stage": vmem((rows, width), F32),
        "sem_x": dma((2, windows)),
        "sem_b": dma((2, windows)),
        "sem_result": dma((windows,)),
        "sem_grad": dma((windows,)),
        "late_vec": vmem((16, width), BF16),
        "late_vec_in": vmem((16, width), BF16),
    }
    for name in ("early", "late"):
        shard, extra = sizes.shards[name], sizes.extras[name]
        shapes[name + "_pack"] = vmem((2, peers * shard, width), BF16)
        shapes[name + "_from_sibling"] = vmem((peers * shard, width), BF16)
        shapes[name + "_parcels"] = vmem((peers, shard + extra, width), BF16)
        shapes[name + "_inbox"] = vmem((peers, shard + extra, width), BF16)
        shapes[name + "_total"] = vmem((2, peers, shard, width), BF16)
        shapes[name + "_sems"] = dma((2, 5))
    return shapes


def local(features, cotangent, slot_pair, crop_size, *weights):
    rows, width = features.shape[1:]
    hidden = weights[12].shape[1]
    peers = lax.axis_size("pix")
    share = lambda count: -(-count // (2 * peers * 16)) * 16
    sizes = types.SimpleNamespace(
        rows=rows, width=width, hidden=hidden, windows=rows // WSLOT, peers=peers,
        scale=1.0 / math.sqrt(2.0 * rows * peers),
        shards={"early": share(3 * hidden + 4 * width), "late": share(4 * width)},
        extras={"early": 0, "late": 16},
    )
    flat = lambda value: value.reshape(1, -1) if value.ndim == 1 else value
    shape = jax.ShapeDtypeStruct
    small = pl.BlockSpec(memory_space=pltpu.VMEM)
    large = pl.BlockSpec(memory_space=pl.ANY)
    scalar = pl.BlockSpec(memory_space=pltpu.SMEM)
    square = shape((width, width), F32)
    row = shape((1, width), F32)
    outs = pl.pallas_call(
        functools.partial(layer_kernel, sizes),
        in_specs=[small, small, scalar, scalar] + [small] * 16,
        out_specs=[large, large] + [small] * 16,
        out_shape=[
            shape((rows, width), BF16), shape((rows, width), F32),
            square, square, square, square, row, row, square, square, square, square, row, row,
            shape((2 * width, hidden), F32), shape((hidden, width), F32), row, row,
        ],
        scratch_shapes=list(scratch_shapes(sizes).values()),
        compiler_params=pltpu.CompilerParams(
            collective_id=0, has_side_effects=True, vmem_limit_bytes=63 * 2**20
        ),
        name="layer",
    )(features[0], cotangent[0], slot_pair, crop_size, *[flat(weight) for weight in weights])
    result, grad = outs[:2]
    return (result[None], grad[None]) + tuple(
        out.reshape(-1) if out.shape[0] == 1 else out for out in outs[2:]
    )


def solution(mesh):
    split = P("frame", "pix", None)
    return jax.shard_map(
        local,
        mesh=mesh,
        in_specs=(split, split, P("pix")) + (P(),) * 17,
        out_specs=(split, split) + (P(),) * 16,
        check_vma=False,
    )
```

```python
import functools
import math
import types

import jax
import jax.numpy as jnp
from jax import lax
from jax.experimental import pallas as pl
from jax.experimental.pallas import tpu as pltpu
from jax.sharding import PartitionSpec as P

WSLOT = 1152
FEWEST = 704
NEGATIVE = -1e30
EPSILON = 1e-05
LOG2E = 1.4426950408889634
F32 = jnp.float32
BF16 = jnp.bfloat16
TAIL_SCALE = 0.305
TAIL_POLY = (
    0.12163973599672318,
    0.12246681749820709,
    0.10342086106538773,
    0.12102170288562775,
    -0.037976883351802826,
    0.18571697175502777,
    -0.15298834443092346,
    0.03669919818639755,
)
TILES = ((0, 256), (256, 256), (512, 256), (768, 256), (1024, 128))


def nn(left, right):
    return jnp.dot(left, right, preferred_element_type=F32)


def nt(left, right):
    return lax.dot_general(left, right, (((1,), (1,)), ((), ())), preferred_element_type=F32)


def norm_stats(values):
    centre = jnp.mean(values, axis=0, keepdims=True)
    shifted = values - centre
    spread = jnp.mean(shifted * shifted, axis=0, keepdims=True)
    inverse = lax.rsqrt(spread + EPSILON)
    return shifted * inverse, inverse


def norm_back(hat, inverse, gain, upstream):
    scaled = upstream * gain
    first = jnp.mean(scaled, axis=0, keepdims=True)
    second = jnp.mean(scaled * hat, axis=0, keepdims=True)
    return inverse * (scaled - first - hat * second)


def upper_tail(values):
    bell = jnp.exp2(values * values * (-0.5 * LOG2E))
    t = 1.0 / (1.0 + TAIL_SCALE * jnp.abs(values))
    poly = TAIL_POLY[-1]
    for coefficient in TAIL_POLY[-2::-1]:
        poly = poly * t + coefficient
    tail = poly * t * bell
    return bell, jnp.where(values >= 0.0, 1.0 - tail, tail)


def flip(values):
    return values.astype(F32).T.astype(BF16)


MESH = pl.DeviceIdType.MESH
INPUTS = (
    "x", "cot", "slot", "crop", "sq", "sk", "sv", "sm", "sgain", "sbias",
    "cq", "ck", "cv", "cm", "cgain", "cbias", "we", "ws", "fgain", "fbias",
)
OUTPUTS = ("result", "grad", "feed_out", "cross_out", "self_out", "totals")
VECTORS = ("sgain", "sbias", "cgain", "cbias", "fgain", "fbias")
SPAN = 256
ONES = 16


def pipeline(block, stages, steps):
    for now in range(steps + len(stages) - 1):

        @block
        def _():
            for depth, stage in enumerate(stages):
                if 0 <= now - depth < steps:
                    stage(now - depth)


def layer_kernel(sizes, *refs):
    names = INPUTS + OUTPUTS + tuple(scratch_shapes(sizes))
    r = types.SimpleNamespace(**dict(zip(names, refs, strict=True)))
    width, hidden, windows, peers = sizes.width, sizes.hidden, sizes.windows, sizes.peers
    factor = 1.0 / math.sqrt(width)
    scale = factor * LOG2E
    frame = lax.axis_index("frame")
    pix = lax.axis_index("pix")
    core = lax.rem(pix, 2)
    me = frame * (peers // 2) + lax.div(pix, 2)
    partner = (1 - frame, pix)
    sibling = (frame, pix + 1 - 2 * core)
    block = pl.when(pix < peers)

    def peer(step):
        index = lax.rem(me + step, peers)
        return index, (lax.div(index, peers // 2), lax.rem(index, peers // 2) * 2 + core)

    barrier = pltpu.get_barrier_semaphore()
    pl.semaphore_signal(barrier, inc=1, device_id=sibling, device_id_type=MESH)

    def greet(step, carry):
        pl.semaphore_signal(barrier, inc=1, device_id=peer(step)[1], device_id_type=MESH)
        return carry

    lax.fori_loop(1, peers, greet, 0)

    slot = r.slot[0]
    live = lax.shift_right_logical(r.crop[0, slot], 1) * lax.shift_right_logical(r.crop[1, slot], 1)

    eye = jnp.where(
        lax.broadcasted_iota(jnp.int32, (width, width), 0)
        == lax.broadcasted_iota(jnp.int32, (width, width), 1),
        1.0, 0.0,
    ).astype(BF16)
    r.eye[...] = eye
    r.self_t[:width] = flip(r.sq[...])
    r.self_t[width : 2 * width] = flip(r.sv[...])
    r.self_t[2 * width :] = flip(r.sk[...])
    r.self_merge_t[...] = flip(r.sm[...])
    r.self_kv_t[:width] = flip(r.sk[...])
    r.self_kv_t[width:] = flip(r.sv[...])
    r.vectors[...] = jnp.concatenate(
        [getattr(r, name)[...] for name in VECTORS] + [jnp.zeros((2, width), F32)], axis=0
    ).T
    vector = lambda name: r.vectors[:, VECTORS.index(name) : VECTORS.index(name) + 1]
    for name in ("g_sq", "g_skv", "g_sm", "g_cq", "g_ckv", "g_cm", "g_we", "g_ws", "g_vec"):
        getattr(r, name)[...] = jnp.zeros_like(getattr(r, name))
    r.v_aug[width:, :] = jnp.ones((ONES, WSLOT), BF16)
    col = lax.broadcasted_iota(jnp.int32, (1, WSLOT), 1)
    for w in range(windows):
        r.alive[:, w * WSLOT : (w + 1) * WSLOT] = jnp.where(col < live, 1.0, 0.0)

    def rows_at(w):
        return pl.ds(pl.multiple_of(w * WSLOT, WSLOT), WSLOT)

    def cols_at(w, t=None):
        start, size = (0, WSLOT) if t is None else TILES[t]
        return pl.ds(pl.multiple_of(w * WSLOT + start, 128), size)

    def to_partner(target, sems, w):
        return pltpu.make_async_remote_copy(
            src_ref=r.send.at[rows_at(w), :], dst_ref=target.at[rows_at(w), :],
            send_sem=sems.at[0, w], recv_sem=sems.at[1, w], device_id=partner, device_id_type=MESH,
        )

    def store_rows(target, stage, w, sem, back=None):
        place = w if back is None else lax.rem(w, 2)
        w = w if back is None else w + back
        return pltpu.make_async_copy(stage.at[rows_at(place), :], target.at[rows_at(w), :], sem.at[w])

    bufs = (r.buf_a, r.buf_b)
    tops = (r.top_a, r.top_b)

    def attend(w, exps, out, inverse):
        def scores(t):
            start, size = TILES[t]
            buf = bufs[t % 2]
            part = r.q_t[:, cols_at(w, t)]
            sure = nn(r.k[:FEWEST, :], part)
            buf[:FEWEST, :size] = sure
            rest = nn(r.k[FEWEST:, :], part)
            row = lax.broadcasted_iota(jnp.int32, rest.shape, 0) + FEWEST
            rest = jnp.where(row < live, rest, NEGATIVE)
            buf[FEWEST:WSLOT, :size] = rest
            top = jnp.maximum(
                jnp.max(sure, axis=0, keepdims=True), jnp.max(rest, axis=0, keepdims=True)
            )
            tops[t % 2][:, :size] = top * scale

        def soften(t):
            start, size = TILES[t]
            exps[w, :, start : start + size] = jnp.exp2(
                bufs[t % 2][:WSLOT, :size] * scale - tops[t % 2][:, :size]
            ).astype(BF16)

        def output(t):
            start, size = TILES[t]
            both = nn(r.v_aug[...], exps[w, :, start : start + size])
            share = 1.0 / both[width : width + 1]
            inverse[:, cols_at(w, t)] = share
            out[:, cols_at(w, t)] = (both[:width] * share).astype(BF16)

        pipeline(block, (scores, soften, output), len(TILES))

    def attend_back(w, exps):
        def grads(t):
            start, size = TILES[t]
            bufs[t % 2][:WSLOT, :size] = nn(r.v[...], r.up[:, start : start + size])

        def differ(t):
            start, size = TILES[t]
            cols = slice(start, start + size)
            grad = bufs[t % 2][:WSLOT, :size] - r.inner[:, cols]
            r.diff[:, cols] = (exps[w, :, cols].astype(F32) * grad).astype(BF16)

        def query(t):
            start, size = TILES[t]
            cols = slice(start, start + size)
            r.dq[:, cols] = (nn(r.k_t[...], r.diff[:, cols]) * factor).astype(BF16)

        pipeline(block, (grads, differ, query), len(TILES))

    def forward_self(w, carry):
        @block
        def _():
            x = r.x[rows_at(w), :]
            stacked = nt(r.self_t[: 2 * width], x).astype(BF16)
            r.q_t[:, cols_at(w)] = stacked[:width]
            r.v_aug[:width, :] = stacked[width:]
            r.k[...] = nn(x, r.sk[...]).astype(BF16)

        attend(w, r.exps, r.out_one, r.inverse_one)

        @block
        def _():
            hat, _ = norm_stats(nn(r.self_merge_t[...], r.out_one[:, cols_at(w)]))
            x1 = nt(r.eye[...], r.x[rows_at(w), :]) + hat * vector("sgain") + vector("sbias")
            r.x1[:, cols_at(w)] = x1
            r.concat[:width, cols_at(w)] = x1.astype(BF16)
            r.send[rows_at(w), :] = x1.T.astype(BF16)

        @pl.when(w == 0)
        def _():
            pl.semaphore_wait(barrier, peers)

        to_partner(r.other, r.sem_x, w).start()
        return carry

    lax.fori_loop(0, windows, forward_self, 0)

    r.cross_q_t[...] = flip(r.cq[...])
    r.cross_kv_t[:width] = flip(r.ck[...])
    r.cross_kv_t[width:] = flip(r.cv[...])
    r.cross_merge_t[...] = flip(r.cm[...])
    r.expand_t[...] = flip(r.we[...])
    r.shrink_t[...] = flip(r.ws[...])

    def forward_cross(w, carry):
        to_partner(r.other, r.sem_x, w).wait()

        @block
        def _():
            other = r.other[rows_at(w), :]
            r.q_t[:, cols_at(w)] = nn(r.cross_q_t[...], r.concat[:width, cols_at(w)]).astype(BF16)
            r.v_aug[:width, :] = nt(r.cross_kv_t[width:], other).astype(BF16)
            r.k[...] = nn(other, r.ck[...]).astype(BF16)

        attend(w, r.exps_two, r.out_two, r.inverse_two)

        @block
        def _():
            hat, _ = norm_stats(nn(r.cross_merge_t[...], r.out_two[:, cols_at(w)]))
            r.concat[width:, cols_at(w)] = (hat * vector("cgain") + vector("cbias")).astype(BF16)

        return carry

    lax.fori_loop(0, windows, forward_cross, 0)

    acts = (r.act_a, r.act_b)
    slopes = (r.slope_a, r.slope_b)

    def span(i):
        return pl.ds(pl.multiple_of(i * SPAN, SPAN), SPAN)

    def expand(i, b):
        bufs[b][:hidden, :] = nn(r.expand_t[...], r.concat[:, span(i)])

    def activate(b):
        pre = bufs[b][:hidden, :]
        bell, phi = upper_tail(pre)
        acts[b][...] = (pre * phi).astype(BF16)
        slopes[b][...] = (phi + pre * bell * (1.0 / math.sqrt(2.0 * math.pi))).astype(BF16)

    def finish_tile(i, b):
        cols = span(i)
        alive = r.alive[:, cols]
        act = acts[b][...]
        hat, inverse = norm_stats(nn(r.shrink_t[...], act))
        gain = vector("fgain")
        result = (r.x1[:, cols] + hat * gain + vector("fbias")) * alive
        r.result_stage[cols, :] = result.T.astype(BF16)
        up = nt(r.eye[...], r.cot[cols, :]) * alive
        r.g_vec[:, 4:5] += jnp.sum(up * hat, axis=1, keepdims=True)
        r.g_vec[:, 5:6] += jnp.sum(up, axis=1, keepdims=True)
        grad_branch = norm_back(hat, inverse, gain, up).astype(BF16)
        r.g_ws[...] += nt(act, grad_branch)
        grad_hidden = (slopes[b][...].astype(F32) * nn(r.ws[...], grad_branch)).astype(BF16)
        r.g_we[...] += nt(grad_hidden, r.concat[:, cols])
        grad_concat = nn(r.we[...], grad_hidden)
        r.x1[:, cols] = up + grad_concat[:width]
        r.grad_normed[:, cols] = grad_concat[width:]

    spans = sizes.rows // SPAN

    @block
    def _():
        expand(0, 0)

    @block
    def _():
        expand(1, 1)
        activate(0)

    def feed(j, carry):
        i = 2 * j

        @block
        def _():
            expand(i + 2, 0)
            activate(1)
            finish_tile(i, 0)

        @block
        def _():
            expand(i + 3, 1)
            activate(0)
            finish_tile(i + 1, 1)

        return carry

    lax.fori_loop(0, spans // 2 - 1, feed, 0)

    @block
    def _():
        activate(1)
        finish_tile(spans - 2, 0)

    @block
    def _():
        finish_tile(spans - 1, 1)

    def store_result(w, carry):
        store_rows(r.result, r.result_stage, w, r.sem_result).start()
        return carry

    lax.fori_loop(0, windows, store_result, 0)

    feed_sum = Reduction(r, sizes.plans["feed"], "feed", sizes.scale, sibling, peer, core, me)
    cross_sum = Reduction(r, sizes.plans["cross"], "cross", sizes.scale, sibling, peer, core, me)
    self_sum = Reduction(r, sizes.plans["self"], "self", sizes.scale, sibling, peer, core, me)

    def columns(*pieces):
        return [ref.at[:, pl.ds(start, width)] for ref, start in pieces]

    feed_sum.begin(columns((r.g_we, 0), (r.g_we, width), (r.g_ws, 0)))

    def backward_cross(w, carry):
        @pl.when(w == 1)
        def _():
            feed_sum.scatter()

        @pl.when(w == windows - 1)
        def _():
            feed_sum.gather()

        @block
        def _():
            out = r.out_two[:, cols_at(w)]
            hat, inverse = norm_stats(nn(r.cross_merge_t[...], out))
            grad = r.grad_normed[:, cols_at(w)]
            r.g_vec[:, 2:3] += jnp.sum(grad * hat, axis=1, keepdims=True)
            r.g_vec[:, 3:4] += jnp.sum(grad, axis=1, keepdims=True)
            grad_merged = norm_back(hat, inverse, vector("cgain"), grad).astype(BF16)
            r.g_cm[...] += nt(out, grad_merged)
            up = (nn(r.cm[...], grad_merged) * r.inverse_two[:, cols_at(w)]).astype(BF16)
            r.up[...] = up
            r.inner[...] = jnp.sum(up.astype(F32) * out.astype(F32), axis=0, keepdims=True)
            other = r.other[rows_at(w), :]
            r.k_t[...] = nt(r.cross_kv_t[:width], other).astype(BF16)
            r.v[...] = nn(other, r.cv[...]).astype(BF16)

        attend_back(w, r.exps_two)

        @block
        def _():
            grad_key = nt(r.diff[...], r.q_t[:, cols_at(w)]) * factor
            r.dkv[:, :width] = grad_key.astype(BF16)
            r.dkv[:, width:] = nt(r.exps_two[w], r.up[...]).astype(BF16)
            r.send[rows_at(w), :] = nn(r.dkv[...], r.cross_kv_t[...]).astype(BF16)

        to_partner(r.received, r.sem_b, w).start()

        @block
        def _():
            r.g_cq[...] += nt(r.concat[:width, cols_at(w)], r.dq[...])
            other_t = nt(r.eye[...], r.other[rows_at(w), :]).astype(BF16)
            r.g_ckv[...] += nn(other_t, r.dkv[...])
            r.x1[:, cols_at(w)] += nn(r.cq[...], r.dq[...])

        return carry

    lax.fori_loop(0, windows, backward_cross, 0)
    cross_sum.begin(columns((r.g_cq, 0), (r.g_ckv, 0), (r.g_ckv, width), (r.g_cm, 0)))

    def backward_self(w, carry):
        @pl.when(w == 1)
        def _():
            feed_sum.share()
            cross_sum.scatter()

        @pl.when(w == windows - 1)
        def _():
            feed_sum.finish()
            feed_sum.store(r.feed_out).start()
            cross_sum.gather()

        to_partner(r.received, r.sem_b, w).wait()

        @block
        def _():
            x = r.x[rows_at(w), :]
            r.q_t[:, cols_at(w)] = nt(r.self_t[:width], x).astype(BF16)
            r.k_t[...] = nt(r.self_t[2 * width :], x).astype(BF16)
            r.v[...] = nn(x, r.sv[...]).astype(BF16)
            out = r.out_one[:, cols_at(w)]
            hat, inverse = norm_stats(nn(r.self_merge_t[...], out))
            grad = r.x1[:, cols_at(w)] + nt(r.eye[...], r.received[rows_at(w), :])
            r.x1[:, cols_at(w)] = grad
            r.g_vec[:, 0:1] += jnp.sum(grad * hat, axis=1, keepdims=True)
            r.g_vec[:, 1:2] += jnp.sum(grad, axis=1, keepdims=True)
            grad_merged = norm_back(hat, inverse, vector("sgain"), grad).astype(BF16)
            r.g_sm[...] += nt(out, grad_merged)
            up = (nn(r.sm[...], grad_merged) * r.inverse_one[:, cols_at(w)]).astype(BF16)
            r.up[...] = up
            r.inner[...] = jnp.sum(up.astype(F32) * out.astype(F32), axis=0, keepdims=True)

        attend_back(w, r.exps)

        @block
        def _():
            grad_key = nt(r.diff[...], r.q_t[:, cols_at(w)]) * factor
            r.dkv[:, :width] = grad_key.astype(BF16)
            r.dkv[:, width:] = nt(r.exps[w], r.up[...]).astype(BF16)
            x_t = nt(r.eye[...], r.x[rows_at(w), :]).astype(BF16)
            r.g_sq[...] += nt(x_t, r.dq[...])
            r.g_skv[...] += nn(x_t, r.dkv[...])

        @pl.when(w >= 2)
        def _():
            store_rows(r.grad, r.grad_stage, w, r.sem_grad, -2).wait()

        @block
        def _():
            half = r.x1[:, cols_at(w)] + nn(r.sq[...], r.dq[...])
            r.grad_stage[pl.ds(pl.multiple_of(lax.rem(w, 2) * WSLOT, WSLOT), WSLOT), :] = half.T + nn(
                r.dkv[...], r.self_kv_t[...]
            )

        store_rows(r.grad, r.grad_stage, w, r.sem_grad, 0).start()
        return carry

    lax.fori_loop(0, windows, backward_self, 0)
    self_sum.begin(columns((r.g_sq, 0), (r.g_skv, 0), (r.g_skv, width), (r.g_sm, 0)), r.g_vec)
    cross_sum.share()
    self_sum.scatter()
    cross_sum.finish()
    cross_sum.store(r.cross_out).start()
    self_sum.gather()
    if self_sum.full:
        r.totals[...] = self_sum.vector_total()
    self_sum.share()
    self_sum.finish()
    self_sum.store(r.self_out).start()
    if not self_sum.full:
        r.totals[...] = self_sum.total[0, 0, self_sum.shard :].astype(F32)

    def drain(w, carry):
        store_rows(r.result, r.result_stage, w, r.sem_result).wait()

        @pl.when(w >= windows - 2)
        def _():
            store_rows(r.grad, r.grad_stage, w, r.sem_grad, 0).wait()

        return carry

    lax.fori_loop(0, windows, drain, 0)
    feed_sum.store(r.feed_out).wait()
    cross_sum.store(r.cross_out).wait()
    self_sum.store(r.self_out).wait()


class Reduction:
    def __init__(self, r, plan, name, scale, sibling, peer, core, me):
        self.sibling, self.peer, self.core, self.me = sibling, peer, core, me
        self.scale = scale
        self.peers, self.owners, self.shard, self.extra, self.kept = (
            plan.peers, plan.owners, plan.shard, plan.extra, plan.kept
        )
        self.half = self.owners * self.shard
        self.full = self.owners == self.peers
        for field in ("pack", "from_sibling", "inbox", "total", "sems"):
            setattr(self, field, getattr(r, name + "_" + field))

    def copy(self, source, target, number, device):
        return pltpu.make_async_remote_copy(
            src_ref=source, dst_ref=target, send_sem=self.sems.at[0, number],
            recv_sem=self.sems.at[1, number], device_id=device, device_id_type=MESH,
        )

    def owning(self, then, otherwise=None):
        if self.full:
            then()
        else:
            pl.when(self.me < self.owners)(then)
            if otherwise is not None:
                pl.when(self.me >= self.owners)(otherwise)

    def halves(self):
        return self.copy(self.pack.at[1 - self.core], self.from_sibling, 0, self.sibling)

    def begin(self, pieces, vec=None):
        at = 0
        width = self.pack.shape[3]
        for piece in pieces:
            taken = 0
            while taken < piece.shape[0]:
                which, inside = divmod(at, self.half)
                index, offset = divmod(inside, self.shard)
                left = piece.shape[0] - taken
                if offset or left < self.shard:
                    count = min(left, self.shard - offset)
                    self.pack[which, index, offset : offset + count] = piece[
                        taken : taken + count, :
                    ].astype(BF16)
                else:
                    blocks = min(left // self.shard, self.owners - index)
                    count = blocks * self.shard
                    self.pack[which, index : index + blocks, : self.shard] = (
                        piece[taken : taken + count, :].astype(BF16).reshape(blocks, self.shard, width)
                    )
                at += count
                taken += count
        while at < 2 * self.half:
            which, inside = divmod(at, self.half)
            index, offset = divmod(inside, self.shard)
            count = self.shard - offset
            self.pack[which, index, offset : self.shard] = jnp.zeros((count, width), BF16)
            at += count
        if self.extra:
            rows = jnp.concatenate([vec[...].T, jnp.zeros((8, width), F32)], axis=0).astype(BF16)
            for which in range(2):
                self.pack[which, :, self.shard :] = jnp.broadcast_to(
                    rows[None], (self.owners, self.extra, width)
                )
        self.halves().start()

    def wait(self, number, sent, received):
        if sent is not None:
            self.copy(sent, sent, number, self.sibling).wait_send()
        if received is not None:
            self.copy(received, received, number, self.sibling).wait_recv()

    def scatter(self):
        self.halves().wait()
        mine = self.pack[self.core].astype(F32) + self.from_sibling[...].astype(F32)
        self.pack[self.core] = mine.astype(BF16)

        def send(step, carry):
            index, device = self.peer(step)

            def go():
                place = self.pack.at[self.core, index]
                self.copy(place, self.inbox.at[self.me], 1, device).start()

            go() if self.full else pl.when(index < self.owners)(go)
            return carry

        lax.fori_loop(1, self.peers, send, 0)

        def own():
            self.inbox[self.me] = self.pack[self.core, self.me]

        self.owning(own)

    def gather(self):
        def own():
            self.wait(
                1, self.pack.at[0, pl.ds(0, self.owners - 1)], self.inbox.at[pl.ds(0, self.peers - 1)]
            )
            total = jnp.sum(self.inbox[:, : self.kept].astype(F32), axis=0) * self.scale
            self.total[self.core, self.me] = total.astype(BF16)

            def send(step, carry):
                place = self.total.at[self.core, self.me]
                self.copy(place, place, 2, self.peer(step)[1]).start()
                return carry

            lax.fori_loop(1, self.peers, send, 0)

        self.owning(own, lambda: self.wait(1, self.pack.at[0], None))

    def vector_total(self):
        return jnp.sum(self.inbox[:, self.shard :].astype(F32), axis=0) * self.scale

    def share(self):
        def own():
            for count in (self.owners - 1,) * ((self.peers - 1) // (self.owners - 1)) + (
                (self.peers - 1) % (self.owners - 1),
            ):
                if count:
                    self.wait(2, self.total.at[0, pl.ds(0, count)], None)
            self.wait(2, None, self.total.at[0, pl.ds(0, self.owners - 1)])

        self.owning(own, lambda: self.wait(2, None, self.total.at[0]))
        self.copy(self.total.at[self.core], self.total.at[self.core], 3, self.sibling).start()

    def finish(self):
        self.copy(self.total.at[self.core], self.total.at[self.core], 3, self.sibling).wait()

    def store(self, target):
        return pltpu.make_async_copy(self.total, target, self.sems.at[0, 4])


def scratch_shapes(sizes):
    width, hidden, windows, rows, peers = sizes.width, sizes.hidden, sizes.windows, sizes.rows, sizes.peers
    vmem = pltpu.VMEM
    dma = pltpu.SemaphoreType.DMA
    square = vmem((width, width), F32)
    shapes = {
        "eye": vmem((width, width), BF16),
        "self_t": vmem((3 * width, width), BF16),
        "self_kv_t": vmem((2 * width, width), BF16),
        "self_merge_t": vmem((width, width), BF16),
        "vectors": vmem((width, 8), F32),
        "cross_q_t": vmem((width, width), BF16),
        "cross_kv_t": vmem((2 * width, width), BF16),
        "cross_merge_t": vmem((width, width), BF16),
        "expand_t": vmem((hidden, 2 * width), BF16),
        "shrink_t": vmem((width, hidden), BF16),
        "g_sq": square, "g_sm": square, "g_cq": square, "g_cm": square,
        "g_skv": vmem((width, 2 * width), F32),
        "g_ckv": vmem((width, 2 * width), F32),
        "g_we": vmem((hidden, 2 * width), F32),
        "g_ws": vmem((hidden, width), F32),
        "g_vec": vmem((width, 8), F32),
        "alive": vmem((1, rows), F32),
        "q_t": vmem((width, rows), BF16),
        "k": vmem((WSLOT, width), BF16),
        "v_aug": vmem((width + ONES, WSLOT), BF16),
        "out_one": vmem((width, rows), BF16),
        "out_two": vmem((width, rows), BF16),
        "inverse_one": vmem((1, rows), F32),
        "inverse_two": vmem((1, rows), F32),
        "x1": vmem((width, rows), F32),
        "concat": vmem((2 * width, rows), BF16),
        "send": vmem((rows, width), BF16),
        "other": vmem((rows, width), BF16),
        "received": vmem((rows, width), BF16),
        "grad_normed": vmem((width, rows), F32),
        "exps": vmem((windows, WSLOT, WSLOT), BF16),
        "exps_two": vmem((windows, WSLOT, WSLOT), BF16),
        "diff": vmem((WSLOT, WSLOT), BF16),
        "buf_a": vmem((max(WSLOT, hidden), SPAN), F32),
        "buf_b": vmem((max(WSLOT, hidden), SPAN), F32),
        "top_a": vmem((1, SPAN), F32),
        "top_b": vmem((1, SPAN), F32),
        "act_a": vmem((hidden, SPAN), BF16),
        "act_b": vmem((hidden, SPAN), BF16),
        "slope_a": vmem((hidden, SPAN), BF16),
        "slope_b": vmem((hidden, SPAN), BF16),
        "k_t": vmem((width, WSLOT), BF16),
        "v": vmem((WSLOT, width), BF16),
        "up": vmem((width, WSLOT), BF16),
        "inner": vmem((1, WSLOT), F32),
        "dq": vmem((width, WSLOT), BF16),
        "dkv": vmem((WSLOT, 2 * width), BF16),
        "result_stage": vmem((rows, width), BF16),
        "grad_stage": vmem((2 * WSLOT, width), F32),
        "sem_x": dma((2, windows)),
        "sem_b": dma((2, windows)),
        "sem_result": dma((windows,)),
        "sem_grad": dma((windows,)),
    }
    for name, plan in sizes.plans.items():
        part = plan.shard + plan.extra
        shapes[name + "_pack"] = vmem((2, plan.owners, part, width), BF16)
        shapes[name + "_from_sibling"] = vmem((plan.owners, part, width), BF16)
        shapes[name + "_inbox"] = vmem((peers, part, width), BF16)
        shapes[name + "_total"] = vmem((2, plan.owners, plan.kept, width), BF16)
        shapes[name + "_sems"] = dma((2, 5))
    return shapes


def total_rows(total, shard, start, count):
    _, peers, _, width = total.shape
    at = start
    found = []
    while at < start + count:
        which, inside = divmod(at, peers * shard)
        index, offset = divmod(inside, shard)
        left = start + count - at
        if offset or left < shard:
            take = min(shard - offset, left)
            found.append(total[which, index, offset : offset + take])
        else:
            blocks = min(left // shard, peers - index)
            take = blocks * shard
            found.append(total[which, index : index + blocks, :shard].reshape(take, width))
        at += take
    return found[0] if len(found) == 1 else jnp.concatenate(found, axis=0)


def hand_out(sizes, *refs):
    result_in, grad_in, feed, cross, own, totals, result, grad = refs[:8]
    (o_sq, o_sk, o_sv, o_sm, o_sgain, o_sbias, o_cq, o_ck, o_cv, o_cm, o_cgain, o_cbias,
     o_we, o_ws, o_fgain, o_fbias) = refs[8:24]
    sems = refs[24]
    width, hidden = sizes.width, sizes.hidden
    shards = [plan.shard for plan in sizes.plans.values()]
    copies = []
    for source, target in ((result_in, result), (grad_in, grad)):
        for w in range(sizes.windows):
            rows = pl.ds(w * WSLOT, WSLOT)
            copies.append(
                pltpu.make_async_copy(source.at[rows, :], target.at[rows, :], sems.at[len(copies)])
            )
            copies[-1].start()
    o_we[:width, :] = total_rows(feed, shards[0], 0, hidden).astype(F32).T
    o_we[width:, :] = total_rows(feed, shards[0], hidden, hidden).astype(F32).T
    o_ws[...] = total_rows(feed, shards[0], 2 * hidden, hidden).astype(F32)
    for source, shard, group in (
        (cross, shards[1], (o_cq, o_ck, o_cv, o_cm)), (own, shards[2], (o_sq, o_sk, o_sv, o_sm))
    ):
        for i, ref in enumerate(group):
            ref[...] = total_rows(source, shard, i * width, width).astype(F32)
    for i, ref in enumerate((o_sgain, o_sbias, o_cgain, o_cbias, o_fgain, o_fbias)):
        ref[...] = totals[i : i + 1, :]
    for copy in copies:
        copy.wait()


def local(features, cotangent, slot_pair, crop_size, *weights):
    rows, width = features.shape[1:]
    hidden = weights[12].shape[1]
    peers = lax.axis_size("pix")

    def plan(count, extra=0):
        shard = -(-count // (2 * peers * 16)) * 16
        owners = min(peers, -(-count // (2 * shard)))
        kept = shard + (extra if owners < peers else 0)
        return types.SimpleNamespace(peers=peers, owners=owners, shard=shard, extra=extra, kept=kept)

    sizes = types.SimpleNamespace(
        rows=rows, width=width, hidden=hidden, windows=rows // WSLOT, peers=peers,
        scale=1.0 / math.sqrt(2.0 * rows * peers),
        plans={"feed": plan(3 * hidden), "cross": plan(4 * width), "self": plan(4 * width, 16)},
    )
    flat = lambda value: value.reshape(1, -1) if value.ndim == 1 else value
    shape = jax.ShapeDtypeStruct
    small = pl.BlockSpec(memory_space=pltpu.VMEM)
    large = pl.BlockSpec(memory_space=pl.ANY)
    scalar = pl.BlockSpec(memory_space=pltpu.SMEM)
    square = shape((width, width), F32)
    row = shape((1, width), F32)
    big = [shape((rows, width), BF16), shape((rows, width), F32)]
    middle = pl.pallas_call(
        functools.partial(layer_kernel, sizes),
        in_specs=[small, small, scalar, scalar] + [small] * 16,
        out_specs=[large] * 5 + [small],
        out_shape=big + [
            shape((2, plan.owners, plan.kept, width), BF16) for plan in sizes.plans.values()
        ] + [shape((16, width), F32)],
        scratch_shapes=list(scratch_shapes(sizes).values()),
        compiler_params=pltpu.CompilerParams(
            collective_id=0, has_side_effects=True, vmem_limit_bytes=63 * 2**20
        ),
        name="layer",
    )(features[0], cotangent[0], slot_pair, crop_size.T, *[flat(weight) for weight in weights])
    outs = pl.pallas_call(
        functools.partial(hand_out, sizes),
        in_specs=[large, large] + [small] * 4,
        out_specs=[large, large] + [small] * 16,
        out_shape=big + [
            square, square, square, square, row, row, square, square, square, square, row, row,
            shape((2 * width, hidden), F32), shape((hidden, width), F32), row, row,
        ],
        scratch_shapes=[pltpu.SemaphoreType.DMA((2 * sizes.windows,))],
        compiler_params=pltpu.CompilerParams(vmem_limit_bytes=16 * 2**20),
        name="hand_out",
    )(*middle)
    result, grad = outs[:2]
    return (result[None], grad[None]) + tuple(
        out.reshape(-1) if out.shape[0] == 1 else out for out in outs[2:]
    )


def solution(mesh):
    split = P("frame", "pix", None)
    return jax.shard_map(
        local,
        mesh=mesh,
        in_specs=(split, split, P("pix")) + (P(),) * 17,
        out_specs=(split, split) + (P(),) * 16,
        check_vma=False,
    )
```

```python
import functools
import math
import types

import jax
import jax.numpy as jnp
from jax import lax
from jax.experimental import pallas as pl
from jax.experimental.pallas import tpu as pltpu
from jax.sharding import PartitionSpec as P

WSLOT = 1152
FEWEST = 704
NEGATIVE = -1e30
EPSILON = 1e-05
LOG2E = 1.4426950408889634
F32 = jnp.float32
BF16 = jnp.bfloat16
MESH = pl.DeviceIdType.MESH
TAIL_SHIFT = 2.7777777777777777
TAIL_POLY = (0.39765776262463953, 1.1594294101832299, 1.9333185594349698, 10.032517622923805, -5.2492700447308085, -9.371923274701059)
SPAN = 256
CHUNK = 128
PART = 384
ONES = 16


def nn(left, right):
    return jnp.dot(left, right, preferred_element_type=F32)


def nt(left, right):
    return lax.dot_general(left, right, (((1,), (1,)), ((), ())), preferred_element_type=F32)


def norm_stats(values):
    centre = jnp.mean(values, axis=0, keepdims=True)
    shifted = values - centre
    spread = jnp.mean(shifted * shifted, axis=0, keepdims=True)
    inverse = lax.rsqrt(spread + EPSILON)
    return shifted * inverse, inverse


def norm_back(hat, inverse, gain, upstream):
    scaled = upstream * gain
    first = jnp.mean(scaled, axis=0, keepdims=True)
    second = jnp.mean(scaled * hat, axis=0, keepdims=True)
    return inverse * (scaled - first - hat * second)


def gelu_both(values):
    bell = jnp.exp2(values * (values * (-0.5 * LOG2E))).astype(BF16)
    t = (1.0 / (jnp.abs(values) + TAIL_SHIFT)).astype(BF16)
    low = values.astype(BF16)
    poly = t * BF16(TAIL_POLY[-1]) + BF16(TAIL_POLY[-2])
    for coefficient in TAIL_POLY[-3::-1]:
        poly = poly * t + BF16(coefficient)
    tail = poly * t * bell
    phi = jnp.where(low >= BF16(0.0), BF16(1.0) - tail, tail)
    return low * phi, phi + low * bell * BF16(1.0 / math.sqrt(2.0 * math.pi))


def flip(values):
    return values.astype(F32).T.astype(BF16)


INPUTS = (
    "x", "cot", "slot", "crop", "sq", "sk", "sv", "sm", "sgain", "sbias",
    "cq", "ck", "cv", "cm", "cgain", "cbias", "we", "ws", "fgain", "fbias",
)
OUTPUTS = ("result", "grad", "feed_out", "cross_out", "self_out", "totals")
VECTORS = ("sgain", "sbias", "cgain", "cbias", "fgain", "fbias")


def layer_kernel(sizes, *refs):
    names = INPUTS + OUTPUTS + tuple(scratch_shapes(sizes))
    r = types.SimpleNamespace(**dict(zip(names, refs, strict=True)))
    width, hidden, windows, peers = sizes.width, sizes.hidden, sizes.windows, sizes.peers
    factor = 1.0 / math.sqrt(width)
    scale = factor * LOG2E
    frame = lax.axis_index("frame")
    pix = lax.axis_index("pix")
    core = lax.rem(pix, 2)
    me = frame * (peers // 2) + lax.div(pix, 2)
    partner = (1 - frame, pix)
    sibling = (frame, pix + 1 - 2 * core)

    def peer(step):
        index = lax.rem(me + step, peers)
        return index, (lax.div(index, peers // 2), lax.rem(index, peers // 2) * 2 + core)

    barrier = pltpu.get_barrier_semaphore()
    pl.semaphore_signal(barrier, inc=1, device_id=sibling, device_id_type=MESH)

    def greet(step, carry):
        pl.semaphore_signal(barrier, inc=1, device_id=peer(step)[1], device_id_type=MESH)
        return carry

    lax.fori_loop(1, peers, greet, 0)

    slot = r.slot[0]
    live = lax.shift_right_logical(r.crop[0, slot], 1) * lax.shift_right_logical(r.crop[1, slot], 1)

    r.eye[...] = jnp.where(
        lax.broadcasted_iota(jnp.int32, (width, width), 0)
        == lax.broadcasted_iota(jnp.int32, (width, width), 1),
        1.0, 0.0,
    ).astype(BF16)
    r.self_qv_t[:width] = flip(r.sq[...])
    r.self_qv_t[width:] = flip(r.sv[...])
    r.self_k_t[...] = flip(r.sk[...])
    r.self_merge_t[...] = flip(r.sm[...])
    r.self_qkv[:, :width] = r.sq[...]
    r.self_qkv[:, width : 2 * width] = r.sk[...]
    r.self_qkv[:, 2 * width :] = r.sv[...]
    for i, name in enumerate(VECTORS):
        r.vectors[i] = jnp.broadcast_to(getattr(r, name)[...], (width, CHUNK)).T
    vector = lambda name: r.vectors[VECTORS.index(name)]
    for name in ("g_sqkv", "g_sm", "g_cqkv", "g_cm", "g_we", "g_ws", "g_vec"):
        getattr(r, name)[...] = jnp.zeros_like(getattr(r, name))
    r.v_aug[width:, :] = jnp.ones((ONES, WSLOT), BF16)

    def alive_at(start, size):
        token = lax.broadcasted_iota(jnp.int32, (1, size), 1) + lax.rem(start, WSLOT)
        return jnp.where(token < live, 1.0, 0.0)

    def rows_at(w):
        return pl.ds(pl.multiple_of(w * WSLOT, WSLOT), WSLOT)

    def cols_at(w, start=0, size=WSLOT):
        return pl.ds(pl.multiple_of(w * WSLOT + start, 128), size)

    def send_rows(w):
        return pltpu.make_async_remote_copy(
            src_ref=r.send.at[rows_at(w), :], dst_ref=r.other.at[rows_at(w), :],
            send_sem=r.sem_x.at[0, w], recv_sem=r.sem_x.at[1, w], device_id=partner, device_id_type=MESH,
        )

    def send_back(w):
        return pltpu.make_async_remote_copy(
            src_ref=r.back.at[w], dst_ref=r.received.at[w],
            send_sem=r.sem_b.at[0, w], recv_sem=r.sem_b.at[1, w], device_id=partner, device_id_type=MESH,
        )

    def store_rows(target, stage, w, sem, back=None):
        place = w if back is None else lax.rem(w, 2)
        w = w if back is None else w + back
        return pltpu.make_async_copy(stage.at[rows_at(place), :], target.at[rows_at(w), :], sem.at[w])

    def tiles(body):
        whole = WSLOT // SPAN

        def step(t, carry):
            body(pl.multiple_of(t * SPAN, SPAN), SPAN)
            return carry

        lax.fori_loop(0, whole, step, 0)
        body(whole * SPAN, WSLOT - whole * SPAN)

    def attend(w, exps, out, inverse):
        def tile(start, size):
            part = r.q_t[:, cols_at(w, start, size)]
            cols = pl.ds(start, size)
            sure = nn(r.k[:FEWEST, :], part)
            rest = nn(r.k[FEWEST:, :], part)
            row = lax.broadcasted_iota(jnp.int32, rest.shape, 0) + FEWEST
            rest = jnp.where(row < live, rest, NEGATIVE)
            top = scale * jnp.maximum(
                jnp.max(sure, axis=0, keepdims=True), jnp.max(rest, axis=0, keepdims=True)
            )
            exps[w, :FEWEST, cols] = jnp.exp2(sure * scale - top).astype(BF16)
            exps[w, FEWEST:, cols] = jnp.exp2(rest * scale - top).astype(BF16)
            both = nn(r.v_aug[...], exps[w, :, cols])
            share = 1.0 / both[width : width + 1]
            inverse[:, cols_at(w, start, size)] = share
            out[:, cols_at(w, start, size)] = (both[:width] * share).astype(BF16)

        tiles(tile)

    def attend_back(w, exps):
        def tile(start, size):
            cols = pl.ds(start, size)
            grad = nn(r.v[...], r.up[:, cols]) - r.inner[:, cols]
            diff = exps[w, :, cols] * grad.astype(BF16)
            r.diff[:, cols] = diff
            r.dqkv[:width, cols] = (nn(r.k_t[...], diff) * factor).astype(BF16)

        tiles(tile)

        def part(i, carry):
            keys = pl.ds(pl.multiple_of(i * PART, PART), PART)
            r.dqkv[width : 2 * width, keys] = (
                nt(r.q_t[:, cols_at(w)], r.diff[keys, :]) * factor
            ).astype(BF16)
            r.dqkv[2 * width :, keys] = nt(r.up[...], exps[w, keys, :]).astype(BF16)
            return carry

        lax.fori_loop(0, WSLOT // PART, part, 0)

    def forward_self(w, carry):
        x = r.x[rows_at(w), :]
        stacked = nt(r.self_qv_t[...], x).astype(BF16)
        r.q_t[:, cols_at(w)] = stacked[:width]
        r.v_aug[:width, :] = stacked[width:]
        r.k[...] = nn(x, r.sk[...]).astype(BF16)
        attend(w, r.exps, r.out_one, r.inverse_one)
        merged = nn(r.self_merge_t[...], r.out_one[:, cols_at(w)])
        x_t = nt(r.eye[...], r.x[rows_at(w), :])
        for start in range(0, WSLOT, CHUNK):
            cols = slice(start, start + CHUNK)
            hat, _ = norm_stats(merged[:, cols])
            x1 = x_t[:, cols] + hat * vector("sgain") + vector("sbias")
            r.x1[:, cols_at(w, start, CHUNK)] = x1
            r.concat[:width, cols_at(w, start, CHUNK)] = x1.astype(BF16)
            r.send[pl.ds(pl.multiple_of(w * WSLOT + start, CHUNK), CHUNK), :] = x1.T.astype(BF16)

        @pl.when(w == 0)
        def _():
            pl.semaphore_wait(barrier, peers)

        send_rows(w).start()
        return carry

    lax.fori_loop(0, windows, forward_self, 0)

    r.cross_q_t[...] = flip(r.cq[...])
    r.cross_k_t[...] = flip(r.ck[...])
    r.cross_v_t[...] = flip(r.cv[...])
    r.cross_merge_t[...] = flip(r.cm[...])
    r.cross_kv[:, :width] = r.ck[...]
    r.cross_kv[:, width:] = r.cv[...]
    r.expand_t[...] = flip(r.we[...])
    r.shrink_t[...] = flip(r.ws[...])

    def forward_cross(w, carry):
        r.q_t[:, cols_at(w)] = nn(r.cross_q_t[...], r.concat[:width, cols_at(w)]).astype(BF16)
        send_rows(w).wait()
        other = r.other[rows_at(w), :]
        r.v_aug[:width, :] = nt(r.cross_v_t[...], other).astype(BF16)
        r.k[...] = nn(other, r.ck[...]).astype(BF16)
        attend(w, r.exps_two, r.out_two, r.inverse_two)
        merged = nn(r.cross_merge_t[...], r.out_two[:, cols_at(w)])
        for start in range(0, WSLOT, CHUNK):
            hat, _ = norm_stats(merged[:, start : start + CHUNK])
            r.concat[width:, cols_at(w, start, CHUNK)] = (
                hat * vector("cgain") + vector("cbias")
            ).astype(BF16)
        return carry

    lax.fori_loop(0, windows, forward_cross, 0)

    spans = sizes.rows // SPAN
    blocks = hidden // SPAN

    def span(i):
        return pl.ds(pl.multiple_of(i * SPAN, SPAN), SPAN)

    def activate(i, carry):
        act, slope = gelu_both(nn(r.expand_t[span(i), :], r.concat[:, :SPAN]))
        r.act[span(i), :] = act
        r.slope[span(i), :] = slope
        return carry

    lax.fori_loop(0, blocks, activate, 0)

    def feed(i, carry):
        cols = span(i)
        base = pl.multiple_of(i * SPAN, SPAN)
        after = span(jnp.minimum(i + 1, spans - 1))
        branch = nn(r.shrink_t[...], r.act[...])
        up_all = nt(r.eye[...], r.cot[cols, :])
        for start in range(0, SPAN, CHUNK):
            part = slice(start, start + CHUNK)
            here = pl.ds(pl.multiple_of(base + start, CHUNK), CHUNK)
            alive = alive_at(base + start, CHUNK)
            hat, inverse = norm_stats(branch[:, part])
            result = (r.x1[:, here] + hat * vector("fgain") + vector("fbias")) * alive
            r.result_stage[here, :] = result.T.astype(BF16)
            up = up_all[:, part] * alive
            r.x1[:, here] = up
            r.g_vec[4] += up * hat
            r.g_vec[5] += up
            r.branch[:, part] = norm_back(hat, inverse, vector("fgain"), up).astype(BF16)
        r.grad_concat[...] = jnp.zeros_like(r.grad_concat)

        def block(b, carry):
            rows = span(b)
            grad_act = nn(r.ws[rows, :], r.branch[...])
            for_shrink = nt(r.act[rows, :], r.branch[...])
            pre = nn(r.expand_t[rows, :], r.concat[:, after])
            grad_hidden = r.slope[rows, :] * grad_act.astype(BF16)
            for_expand = nt(grad_hidden, r.concat[:, cols])
            for_concat = nn(r.we[:, rows], grad_hidden)
            act, slope = gelu_both(pre)
            r.act[rows, :] = act
            r.slope[rows, :] = slope
            r.g_ws[rows, :] += for_shrink
            r.g_we[rows, :] += for_expand
            r.grad_concat[...] += for_concat
            return carry

        lax.fori_loop(0, blocks, block, 0)
        r.x1[:, cols] += r.grad_concat[:width, :]
        r.grad_normed[:, cols] = r.grad_concat[width:, :]
        return carry

    lax.fori_loop(0, spans, feed, 0)

    def store_result(w, carry):
        store_rows(r.result, r.result_stage, w, r.sem_result).start()
        return carry

    lax.fori_loop(0, windows, store_result, 0)

    feed_sum = Reduction(r, sizes.plans["feed"], "feed", sizes.scale, sibling, peer, core, me)
    cross_sum = Reduction(r, sizes.plans["cross"], "cross", sizes.scale, sibling, peer, core, me)
    self_sum = Reduction(r, sizes.plans["self"], "self", sizes.scale, sibling, peer, core, me)
    feed_sum.begin([r.g_we.at[:, pl.ds(0, width)], r.g_we.at[:, pl.ds(width, width)], r.g_ws])

    def upstream(w, merged, grad_at, number, gain, out, gradient, merge, inverse):
        sums = [jnp.zeros((width, CHUNK), F32)] * 2
        for start in range(0, WSLOT, CHUNK):
            hat, root = norm_stats(merged[:, start : start + CHUNK])
            grad = grad_at(start)
            sums = [sums[0] + grad * hat, sums[1] + grad]
            r.grad_merged[:, start : start + CHUNK] = norm_back(hat, root, vector(gain), grad).astype(BF16)
        r.g_vec[number] += sums[0]
        r.g_vec[number + 1] += sums[1]
        out = out[:, cols_at(w)]
        gradient[...] += nt(out, r.grad_merged[...])
        up = (nn(merge[...], r.grad_merged[...]) * inverse[:, cols_at(w)]).astype(BF16)
        r.up[...] = up
        r.inner[...] = jnp.sum(up.astype(F32) * out.astype(F32), axis=0, keepdims=True)

    def backward_cross(w, carry):
        @pl.when(w == 1)
        def _():
            feed_sum.scatter()

        @pl.when(w == windows - 1)
        def _():
            feed_sum.gather()

        upstream(
            w, nn(r.cross_merge_t[...], r.out_two[:, cols_at(w)]),
            lambda start: r.grad_normed[:, cols_at(w, start, CHUNK)],
            2, "cgain", r.out_two, r.g_cm, r.cm, r.inverse_two,
        )
        other = r.other[rows_at(w), :]
        r.k_t[...] = nt(r.cross_k_t[...], other).astype(BF16)
        r.v[...] = nn(other, r.cv[...]).astype(BF16)
        attend_back(w, r.exps_two)
        r.back[w] = nn(r.cross_kv[...], r.dqkv[width:, :]).astype(BF16)
        send_back(w).start()
        r.g_cqkv[:width] += nt(r.dqkv[:width, :], r.concat[:width, cols_at(w)])
        r.g_cqkv[width:] += nn(r.dqkv[width:, :], r.other[rows_at(w), :])
        r.x1[:, cols_at(w)] += nn(r.cq[...], r.dqkv[:width, :])
        return carry

    lax.fori_loop(0, windows, backward_cross, 0)
    cross_sum.begin([r.g_cqkv, r.g_cm])

    def backward_self(w, carry):
        @pl.when(w == 1)
        def _():
            feed_sum.share()
            cross_sum.scatter()

        @pl.when(w == windows - 1)
        def _():
            feed_sum.finish()
            feed_sum.store(r.feed_out).start()
            cross_sum.gather()

        x = r.x[rows_at(w), :]
        r.q_t[:, cols_at(w)] = nt(r.self_qv_t[:width, :], x).astype(BF16)
        r.k_t[...] = nt(r.self_k_t[...], x).astype(BF16)
        r.v[...] = nn(x, r.sv[...]).astype(BF16)
        send_back(w).wait()

        def grad_at(start):
            here = cols_at(w, start, CHUNK)
            grad = r.x1[:, here] + r.received[w, :, start : start + CHUNK].astype(F32)
            r.x1[:, here] = grad
            return grad

        upstream(
            w, nn(r.self_merge_t[...], r.out_one[:, cols_at(w)]), grad_at,
            0, "sgain", r.out_one, r.g_sm, r.sm, r.inverse_one,
        )
        attend_back(w, r.exps)
        r.g_sqkv[...] += nn(r.dqkv[...], r.x[rows_at(w), :])

        @pl.when(w >= 2)
        def _():
            store_rows(r.grad, r.grad_stage, w, r.sem_grad, -2).wait()

        total = r.x1[:, cols_at(w)] + nn(r.self_qkv[...], r.dqkv[...])
        r.grad_stage[pl.ds(pl.multiple_of(lax.rem(w, 2) * WSLOT, WSLOT), WSLOT), :] = total.T
        store_rows(r.grad, r.grad_stage, w, r.sem_grad, 0).start()
        return carry

    lax.fori_loop(0, windows, backward_self, 0)
    self_sum.begin([r.g_sqkv, r.g_sm], r.g_vec)
    cross_sum.share()
    self_sum.scatter()
    cross_sum.finish()
    cross_sum.store(r.cross_out).start()
    self_sum.gather()
    if self_sum.full:
        r.totals[...] = self_sum.vector_total()
    self_sum.share()
    self_sum.finish()
    self_sum.store(r.self_out).start()
    if not self_sum.full:
        r.totals[...] = self_sum.total[0, 0, self_sum.shard :].astype(F32)

    def drain(w, carry):
        store_rows(r.result, r.result_stage, w, r.sem_result).wait()

        @pl.when(w >= windows - 2)
        def _():
            store_rows(r.grad, r.grad_stage, w, r.sem_grad, 0).wait()

        return carry

    lax.fori_loop(0, windows, drain, 0)
    feed_sum.store(r.feed_out).wait()
    cross_sum.store(r.cross_out).wait()
    self_sum.store(r.self_out).wait()


class Reduction:
    def __init__(self, r, plan, name, scale, sibling, peer, core, me):
        self.sibling, self.peer, self.core, self.me = sibling, peer, core, me
        self.scale = scale
        self.peers, self.owners, self.shard, self.extra, self.kept = (
            plan.peers, plan.owners, plan.shard, plan.extra, plan.kept
        )
        self.half = self.owners * self.shard
        self.full = self.owners == self.peers
        for field in ("pack", "from_sibling", "inbox", "total", "sems"):
            setattr(self, field, getattr(r, name + "_" + field))

    def copy(self, source, target, number, device):
        return pltpu.make_async_remote_copy(
            src_ref=source, dst_ref=target, send_sem=self.sems.at[0, number],
            recv_sem=self.sems.at[1, number], device_id=device, device_id_type=MESH,
        )

    def owning(self, then, otherwise=None):
        if self.full:
            then()
        else:
            pl.when(self.me < self.owners)(then)
            if otherwise is not None:
                pl.when(self.me >= self.owners)(otherwise)

    def halves(self):
        return self.copy(self.pack.at[1 - self.core], self.from_sibling, 0, self.sibling)

    def begin(self, pieces, vec=None):
        at = 0
        width = self.pack.shape[3]
        for piece in pieces:
            taken = 0
            while taken < piece.shape[0]:
                which, inside = divmod(at, self.half)
                index, offset = divmod(inside, self.shard)
                left = piece.shape[0] - taken
                if offset or left < self.shard:
                    count = min(left, self.shard - offset)
                    self.pack[which, index, offset : offset + count] = piece[
                        taken : taken + count, :
                    ].astype(BF16)
                else:
                    blocks = min(left // self.shard, self.owners - index)
                    count = blocks * self.shard
                    self.pack[which, index : index + blocks, : self.shard] = (
                        piece[taken : taken + count, :].astype(BF16).reshape(blocks, self.shard, width)
                    )
                at += count
                taken += count
        while at < 2 * self.half:
            which, inside = divmod(at, self.half)
            index, offset = divmod(inside, self.shard)
            count = self.shard - offset
            self.pack[which, index, offset : self.shard] = jnp.zeros((count, width), BF16)
            at += count
        if self.extra:
            sums = jnp.concatenate([jnp.sum(vec[i].T, axis=0, keepdims=True) for i in range(vec.shape[0])])
            rows = jnp.concatenate([sums, jnp.zeros((self.extra - vec.shape[0], width), F32)]).astype(BF16)
            for which in range(2):
                self.pack[which, :, self.shard :] = jnp.broadcast_to(
                    rows[None], (self.owners, self.extra, width)
                )
        self.halves().start()

    def wait(self, number, sent, received):
        if sent is not None:
            self.copy(sent, sent, number, self.sibling).wait_send()
        if received is not None:
            self.copy(received, received, number, self.sibling).wait_recv()

    def scatter(self):
        self.halves().wait()
        mine = self.pack[self.core].astype(F32) + self.from_sibling[...].astype(F32)
        self.pack[self.core] = mine.astype(BF16)

        def send(step, carry):
            index, device = self.peer(step)

            def go():
                place = self.pack.at[self.core, index]
                self.copy(place, self.inbox.at[self.me], 1, device).start()

            go() if self.full else pl.when(index < self.owners)(go)
            return carry

        lax.fori_loop(1, self.peers, send, 0)

        def own():
            self.inbox[self.me] = self.pack[self.core, self.me]

        self.owning(own)

    def gather(self):
        def own():
            self.wait(
                1, self.pack.at[0, pl.ds(0, self.owners - 1)], self.inbox.at[pl.ds(0, self.peers - 1)]
            )
            total = jnp.sum(self.inbox[:, : self.kept].astype(F32), axis=0) * self.scale
            self.total[self.core, self.me] = total.astype(BF16)

            def send(step, carry):
                place = self.total.at[self.core, self.me]
                self.copy(place, place, 2, self.peer(step)[1]).start()
                return carry

            lax.fori_loop(1, self.peers, send, 0)

        self.owning(own, lambda: self.wait(1, self.pack.at[0], None))

    def vector_total(self):
        return jnp.sum(self.inbox[:, self.shard :].astype(F32), axis=0) * self.scale

    def share(self):
        def own():
            for count in (self.owners - 1,) * ((self.peers - 1) // (self.owners - 1)) + (
                (self.peers - 1) % (self.owners - 1),
            ):
                if count:
                    self.wait(2, self.total.at[0, pl.ds(0, count)], None)
            self.wait(2, None, self.total.at[0, pl.ds(0, self.owners - 1)])

        self.owning(own, lambda: self.wait(2, None, self.total.at[0]))
        self.copy(self.total.at[self.core], self.total.at[self.core], 3, self.sibling).start()

    def finish(self):
        self.copy(self.total.at[self.core], self.total.at[self.core], 3, self.sibling).wait()

    def store(self, target):
        return pltpu.make_async_copy(self.total, target, self.sems.at[0, 4])


def scratch_shapes(sizes):
    width, hidden, windows, rows, peers = sizes.width, sizes.hidden, sizes.windows, sizes.rows, sizes.peers
    vmem = pltpu.VMEM
    dma = pltpu.SemaphoreType.DMA
    square = vmem((width, width), F32)
    shapes = {
        "eye": vmem((width, width), BF16),
        "self_qv_t": vmem((2 * width, width), BF16),
        "self_k_t": vmem((width, width), BF16),
        "self_merge_t": vmem((width, width), BF16),
        "self_qkv": vmem((width, 3 * width), BF16),
        "vectors": vmem((len(VECTORS), width, CHUNK), F32),
        "cross_q_t": vmem((width, width), BF16),
        "cross_k_t": vmem((width, width), BF16),
        "cross_v_t": vmem((width, width), BF16),
        "cross_merge_t": vmem((width, width), BF16),
        "cross_kv": vmem((width, 2 * width), BF16),
        "expand_t": vmem((hidden, 2 * width), BF16),
        "shrink_t": vmem((width, hidden), BF16),
        "g_sqkv": vmem((3 * width, width), F32),
        "g_cqkv": vmem((3 * width, width), F32),
        "g_sm": square,
        "g_cm": square,
        "g_we": vmem((hidden, 2 * width), F32),
        "g_ws": vmem((hidden, width), F32),
        "g_vec": vmem((len(VECTORS), width, CHUNK), F32),
        "q_t": vmem((width, rows), BF16),
        "k": vmem((WSLOT, width), BF16),
        "v_aug": vmem((width + ONES, WSLOT), BF16),
        "out_one": vmem((width, rows), BF16),
        "out_two": vmem((width, rows), BF16),
        "inverse_one": vmem((1, rows), F32),
        "inverse_two": vmem((1, rows), F32),
        "x1": vmem((width, rows), F32),
        "concat": vmem((2 * width, rows), BF16),
        "send": vmem((rows, width), BF16),
        "other": vmem((rows, width), BF16),
        "back": vmem((windows, width, WSLOT), BF16),
        "received": vmem((windows, width, WSLOT), BF16),
        "grad_normed": vmem((width, rows), F32),
        "exps": vmem((windows, WSLOT, WSLOT), BF16),
        "exps_two": vmem((windows, WSLOT, WSLOT), BF16),
        "diff": vmem((WSLOT, WSLOT), BF16),
        "act": vmem((hidden, SPAN), BF16),
        "slope": vmem((hidden, SPAN), BF16),
        "branch": vmem((width, SPAN), BF16),
        "grad_concat": vmem((2 * width, SPAN), F32),
        "grad_merged": vmem((width, WSLOT), BF16),
        "k_t": vmem((width, WSLOT), BF16),
        "v": vmem((WSLOT, width), BF16),
        "up": vmem((width, WSLOT), BF16),
        "inner": vmem((1, WSLOT), F32),
        "dqkv": vmem((3 * width, WSLOT), BF16),
        "result_stage": vmem((rows, width), BF16),
        "grad_stage": vmem((2 * WSLOT, width), F32),
        "sem_x": dma((2, windows)),
        "sem_b": dma((2, windows)),
        "sem_result": dma((windows,)),
        "sem_grad": dma((windows,)),
    }
    for name, plan in sizes.plans.items():
        part = plan.shard + plan.extra
        shapes[name + "_pack"] = vmem((2, plan.owners, part, width), BF16)
        shapes[name + "_from_sibling"] = vmem((plan.owners, part, width), BF16)
        shapes[name + "_inbox"] = vmem((peers, part, width), BF16)
        shapes[name + "_total"] = vmem((2, plan.owners, plan.kept, width), BF16)
        shapes[name + "_sems"] = dma((2, 5))
    return shapes


def total_rows(total, shard, start, count):
    _, peers, _, width = total.shape
    at = start
    found = []
    while at < start + count:
        which, inside = divmod(at, peers * shard)
        index, offset = divmod(inside, shard)
        left = start + count - at
        if offset or left < shard:
            take = min(shard - offset, left)
            found.append(total[which, index, offset : offset + take])
        else:
            blocks = min(left // shard, peers - index)
            take = blocks * shard
            found.append(total[which, index : index + blocks, :shard].reshape(take, width))
        at += take
    return found[0] if len(found) == 1 else jnp.concatenate(found, axis=0)


def hand_out(sizes, *refs):
    result_in, grad_in, feed, cross, own, totals, result, grad = refs[:8]
    (o_sq, o_sk, o_sv, o_sm, o_sgain, o_sbias, o_cq, o_ck, o_cv, o_cm, o_cgain, o_cbias,
     o_we, o_ws, o_fgain, o_fbias) = refs[8:24]
    width, hidden = sizes.width, sizes.hidden
    shards = [plan.shard for plan in sizes.plans.values()]
    result[...] = result_in[...]
    grad[...] = grad_in[...]

    @pl.when(pl.program_id(0) == 0)
    def _():
        o_we[:width, :] = total_rows(feed, shards[0], 0, hidden).astype(F32).T
        o_we[width:, :] = total_rows(feed, shards[0], hidden, hidden).astype(F32).T
        o_ws[...] = total_rows(feed, shards[0], 2 * hidden, hidden).astype(F32)
        for source, shard, group in (
            (cross, shards[1], (o_cq, o_ck, o_cv, o_cm)), (own, shards[2], (o_sq, o_sk, o_sv, o_sm))
        ):
            for i, ref in enumerate(group):
                total = total_rows(source, shard, i * width, width).astype(F32)
                ref[...] = total if i == 3 else total.T
        for i, ref in enumerate((o_sgain, o_sbias, o_cgain, o_cbias, o_fgain, o_fbias)):
            ref[...] = totals[i : i + 1, :]


def local(features, cotangent, slot_pair, crop_size, *weights):
    rows, width = features.shape[1:]
    hidden = weights[12].shape[1]
    peers = lax.axis_size("pix")

    def plan(count, extra=0):
        shard = -(-count // (2 * peers * 16)) * 16
        owners = min(peers, -(-count // (2 * shard)))
        kept = shard + (extra if owners < peers else 0)
        return types.SimpleNamespace(peers=peers, owners=owners, shard=shard, extra=extra, kept=kept)

    sizes = types.SimpleNamespace(
        rows=rows, width=width, hidden=hidden, windows=rows // WSLOT, peers=peers,
        scale=1.0 / math.sqrt(2.0 * rows * peers),
        plans={"feed": plan(3 * hidden), "cross": plan(4 * width), "self": plan(4 * width, 16)},
    )
    flat = lambda value: value.reshape(1, -1) if value.ndim == 1 else value
    shape = jax.ShapeDtypeStruct
    small = pl.BlockSpec(memory_space=pltpu.VMEM)
    large = pl.BlockSpec(memory_space=pl.ANY)
    scalar = pl.BlockSpec(memory_space=pltpu.SMEM)
    square = shape((width, width), F32)
    row = shape((1, width), F32)
    big = [shape((rows, width), BF16), shape((rows, width), F32)]
    middle = pl.pallas_call(
        functools.partial(layer_kernel, sizes),
        in_specs=[small, small, scalar, scalar] + [small] * 16,
        out_specs=[large] * 5 + [small],
        out_shape=big + [
            shape((2, plan.owners, plan.kept, width), BF16) for plan in sizes.plans.values()
        ] + [shape((16, width), F32)],
        scratch_shapes=list(scratch_shapes(sizes).values()),
        compiler_params=pltpu.CompilerParams(
            collective_id=0, has_side_effects=True, vmem_limit_bytes=63 * 2**20
        ),
        name="layer",
    )(features[0], cotangent[0], slot_pair, crop_size.T, *[flat(weight) for weight in weights])
    moved = [pl.BlockSpec((WSLOT, width), lambda w: (w, 0))] * 2
    whole = lambda shape: pl.BlockSpec(shape, lambda w: (0,) * len(shape))
    smalls = [
        square, square, square, square, row, row, square, square, square, square, row, row,
        shape((2 * width, hidden), F32), shape((hidden, width), F32), row, row,
    ]
    outs = pl.pallas_call(
        functools.partial(hand_out, sizes),
        grid=(sizes.windows,),
        in_specs=moved + [whole(value.shape) for value in middle[2:]],
        out_specs=moved + [whole(value.shape) for value in smalls],
        out_shape=big + smalls,
        compiler_params=pltpu.CompilerParams(vmem_limit_bytes=60 * 2**20),
        name="hand_out",
    )(*middle)
    result, grad = outs[:2]
    return (result[None], grad[None]) + tuple(
        out.reshape(-1) if out.shape[0] == 1 else out for out in outs[2:]
    )


def solution(mesh):
    split = P("frame", "pix", None)
    return jax.shard_map(
        local,
        mesh=mesh,
        in_specs=(split, split, P("pix")) + (P(),) * 17,
        out_specs=(split, split) + (P(),) * 16,
        check_vma=False,
    )
```

```python
import functools
import math
import types

import jax
import jax.numpy as jnp
from jax import lax
from jax.experimental import pallas as pl
from jax.experimental.pallas import tpu as pltpu
from jax.sharding import PartitionSpec as P

WSLOT = 1152
FEWEST = 704
NEGATIVE = -1e30
EPSILON = 1e-05
LOG2E = 1.4426950408889634
F32 = jnp.float32
BF16 = jnp.bfloat16
MESH = pl.DeviceIdType.MESH
TAIL_SHIFT = 2.7777777777777777
TAIL_POLY = (0.39765776262463953, 1.1594294101832299, 1.9333185594349698, 10.032517622923805, -5.2492700447308085, -9.371923274701059)
SPAN = 256
CHUNK = 128
TILES = ((0, 256), (256, 256), (512, 256), (768, 256), (1024, 128))
ONES = 16


def nn(left, right):
    return jnp.dot(left, right, preferred_element_type=F32)


def nt(left, right):
    return lax.dot_general(left, right, (((1,), (1,)), ((), ())), preferred_element_type=F32)


def norm_stats(values):
    centre = jnp.mean(values, axis=0, keepdims=True)
    shifted = values - centre
    spread = jnp.mean(shifted * shifted, axis=0, keepdims=True)
    inverse = lax.rsqrt(spread + EPSILON)
    return shifted * inverse, inverse


def norm_back(hat, inverse, gain, upstream):
    scaled = upstream * gain
    first = jnp.mean(scaled, axis=0, keepdims=True)
    second = jnp.mean(scaled * hat, axis=0, keepdims=True)
    return inverse * (scaled - first - hat * second)


def gelu_both(values):
    bell = jnp.exp2(values * (values * (-0.5 * LOG2E))).astype(BF16)
    t = (1.0 / (jnp.abs(values) + TAIL_SHIFT)).astype(BF16)
    low = values.astype(BF16)
    poly = t * BF16(TAIL_POLY[-1]) + BF16(TAIL_POLY[-2])
    for coefficient in TAIL_POLY[-3::-1]:
        poly = poly * t + BF16(coefficient)
    tail = poly * t * bell
    phi = jnp.where(low >= BF16(0.0), BF16(1.0) - tail, tail)
    return low * phi, phi + low * bell * BF16(1.0 / math.sqrt(2.0 * math.pi))


def flip(values):
    return values.astype(F32).T.astype(BF16)


INPUTS = (
    "x", "cot", "slot", "crop", "sq", "sk", "sv", "sm", "sgain", "sbias",
    "cq", "ck", "cv", "cm", "cgain", "cbias", "we", "ws", "fgain", "fbias",
)
OUTPUTS = ("result", "grad", "feed_out", "cross_out", "self_out", "totals")
VECTORS = ("sgain", "sbias", "cgain", "cbias", "fgain", "fbias")


def layer_kernel(sizes, *refs):
    names = INPUTS + OUTPUTS + tuple(scratch_shapes(sizes))
    r = types.SimpleNamespace(**dict(zip(names, refs, strict=True)))
    width, hidden, windows, peers = sizes.width, sizes.hidden, sizes.windows, sizes.peers
    factor = 1.0 / math.sqrt(width)
    scale = factor * LOG2E
    frame = lax.axis_index("frame")
    pix = lax.axis_index("pix")
    core = lax.rem(pix, 2)
    me = frame * (peers // 2) + lax.div(pix, 2)
    partner = (1 - frame, pix)
    sibling = (frame, pix + 1 - 2 * core)

    def peer(step):
        index = lax.rem(me + step, peers)
        return index, (lax.div(index, peers // 2), lax.rem(index, peers // 2) * 2 + core)

    barrier = pltpu.get_barrier_semaphore()
    pl.semaphore_signal(barrier, inc=1, device_id=sibling, device_id_type=MESH)

    def greet(step, carry):
        pl.semaphore_signal(barrier, inc=1, device_id=peer(step)[1], device_id_type=MESH)
        return carry

    lax.fori_loop(1, peers, greet, 0)

    slot = r.slot[0]
    live = lax.shift_right_logical(r.crop[0, slot], 1) * lax.shift_right_logical(r.crop[1, slot], 1)

    r.eye[...] = jnp.where(
        lax.broadcasted_iota(jnp.int32, (width, width), 0)
        == lax.broadcasted_iota(jnp.int32, (width, width), 1),
        1.0, 0.0,
    ).astype(BF16)
    r.self_qv_t[:width] = flip(r.sq[...])
    r.self_qv_t[width:] = flip(r.sv[...])
    r.self_k_t[...] = flip(r.sk[...])
    r.self_merge_t[...] = flip(r.sm[...])
    r.self_qkv[:, :width] = r.sq[...]
    r.self_qkv[:, width : 2 * width] = r.sk[...]
    r.self_qkv[:, 2 * width :] = r.sv[...]
    for i, name in enumerate(VECTORS):
        r.vectors[i] = jnp.broadcast_to(getattr(r, name)[...], (width, CHUNK)).T
    vector = lambda name: r.vectors[VECTORS.index(name)]
    for name in ("g_sqkv", "g_sm", "g_cqkv", "g_cm", "g_we", "g_ws", "g_vec"):
        getattr(r, name)[...] = jnp.zeros_like(getattr(r, name))
    r.v_aug[width:, :] = jnp.ones((ONES, WSLOT), BF16)

    def alive_at(start, size):
        token = lax.broadcasted_iota(jnp.int32, (1, size), 1) + lax.rem(start, WSLOT)
        return jnp.where(token < live, 1.0, 0.0)

    def rows_at(w):
        return pl.ds(pl.multiple_of(w * WSLOT, WSLOT), WSLOT)

    def cols_at(w, start=0, size=WSLOT):
        return pl.ds(pl.multiple_of(w * WSLOT + start, 128), size)

    def send_rows(w):
        return pltpu.make_async_remote_copy(
            src_ref=r.send.at[rows_at(w), :], dst_ref=r.other.at[rows_at(w), :],
            send_sem=r.sem_x.at[0, w], recv_sem=r.sem_x.at[1, w], device_id=partner, device_id_type=MESH,
        )

    def send_back(w):
        return pltpu.make_async_remote_copy(
            src_ref=r.back.at[w], dst_ref=r.received.at[w],
            send_sem=r.sem_b.at[0, w], recv_sem=r.sem_b.at[1, w], device_id=partner, device_id_type=MESH,
        )

    def store_rows(target, stage, w, sem, back=None):
        place = w if back is None else lax.rem(w, 2)
        w = w if back is None else w + back
        return pltpu.make_async_copy(stage.at[rows_at(place), :], target.at[rows_at(w), :], sem.at[w])

    def attend(w, exps, out, inverse):
        bufs = (r.buf_a, r.buf_b)
        tops = {}

        def score(t, start):
            first, size = TILES[t]
            rows = slice(start, start + CHUNK)
            got = nn(r.k[rows, :], r.q_t[:, cols_at(w, first, size)])
            if start + CHUNK > FEWEST:
                row = lax.broadcasted_iota(jnp.int32, got.shape, 0) + start
                got = jnp.where(row < live, got, NEGATIVE)
            bufs[t % 2][rows, :size] = got
            top = jnp.max(got.reshape(CHUNK // 8, 8, size), axis=0)
            tops[t] = top if t not in tops else jnp.maximum(tops[t], top)

        def output(t):
            first, size = TILES[t]
            both = nn(r.v_aug[...], exps[w, :, first : first + size])
            share = 1.0 / both[width : width + 1]
            inverse[:, cols_at(w, first, size)] = share
            out[:, cols_at(w, first, size)] = (both[:width] * share).astype(BF16)

        for start in range(0, WSLOT, CHUNK):
            score(0, start)
        for t, (first, size) in enumerate(TILES):
            top = scale * jnp.max(tops[t], axis=0, keepdims=True)
            for start in range(0, WSLOT, CHUNK):
                if t + 1 < len(TILES):
                    score(t + 1, start)
                rows = slice(start, start + CHUNK)
                exps[w, rows, first : first + size] = jnp.exp2(
                    bufs[t % 2][rows, :size] * scale - top
                ).astype(BF16)
            if t:
                output(t - 1)
        output(len(TILES) - 1)

    def attend_back(w, exps):
        def query(t):
            first, size = TILES[t]
            cols = slice(first, first + size)
            r.dqkv[:width, cols] = (nn(r.k_t[...], r.diff[:, cols]) * factor).astype(BF16)

        for t, (first, size) in enumerate(TILES):
            cols = slice(first, first + size)
            grad = nn(r.v[...], r.up[:, cols]) - r.inner[:, cols]
            r.diff[:, cols] = exps[w, :, cols] * grad.astype(BF16)
            r.dqkv[2 * width :, cols] = nt(r.up[...], exps[w, cols, :]).astype(BF16)
            if t:
                query(t - 1)
        query(len(TILES) - 1)
        r.dqkv[width : 2 * width, :] = (nt(r.q_t[:, cols_at(w)], r.diff[...]) * factor).astype(BF16)

    def forward_self(w, carry):
        x = r.x[rows_at(w), :]
        stacked = nt(r.self_qv_t[...], x).astype(BF16)
        r.q_t[:, cols_at(w)] = stacked[:width]
        r.v_aug[:width, :] = stacked[width:]
        r.k[...] = nn(x, r.sk[...]).astype(BF16)
        attend(w, r.exps, r.out_one, r.inverse_one)
        merged = nn(r.self_merge_t[...], r.out_one[:, cols_at(w)])
        x_t = nt(r.eye[...], r.x[rows_at(w), :])
        for start in range(0, WSLOT, CHUNK):
            cols = slice(start, start + CHUNK)
            hat, _ = norm_stats(merged[:, cols])
            x1 = x_t[:, cols] + hat * vector("sgain") + vector("sbias")
            r.x1[:, cols_at(w, start, CHUNK)] = x1
            r.concat[:width, cols_at(w, start, CHUNK)] = x1.astype(BF16)
            r.send[pl.ds(pl.multiple_of(w * WSLOT + start, CHUNK), CHUNK), :] = x1.T.astype(BF16)

        @pl.when(w == 0)
        def _():
            pl.semaphore_wait(barrier, peers)

        send_rows(w).start()
        return carry

    lax.fori_loop(0, windows, forward_self, 0)

    r.cross_q_t[...] = flip(r.cq[...])
    r.cross_k_t[...] = flip(r.ck[...])
    r.cross_v_t[...] = flip(r.cv[...])
    r.cross_merge_t[...] = flip(r.cm[...])
    r.cross_kv[:, :width] = r.ck[...]
    r.cross_kv[:, width:] = r.cv[...]
    r.expand_t[...] = flip(r.we[...])
    r.shrink_t[...] = flip(r.ws[...])

    def forward_cross(w, carry):
        r.q_t[:, cols_at(w)] = nn(r.cross_q_t[...], r.concat[:width, cols_at(w)]).astype(BF16)
        send_rows(w).wait()
        other = r.other[rows_at(w), :]
        r.v_aug[:width, :] = nt(r.cross_v_t[...], other).astype(BF16)
        r.k[...] = nn(other, r.ck[...]).astype(BF16)
        attend(w, r.exps_two, r.out_two, r.inverse_two)
        merged = nn(r.cross_merge_t[...], r.out_two[:, cols_at(w)])
        for start in range(0, WSLOT, CHUNK):
            hat, _ = norm_stats(merged[:, start : start + CHUNK])
            r.concat[width:, cols_at(w, start, CHUNK)] = (
                hat * vector("cgain") + vector("cbias")
            ).astype(BF16)
        return carry

    lax.fori_loop(0, windows, forward_cross, 0)

    spans = sizes.rows // SPAN

    def span(i):
        return pl.ds(pl.multiple_of(i * SPAN, SPAN), SPAN)

    def expand(i, b, rows):
        act, slope = gelu_both(nn(r.expand_t[rows, :], r.concat[:, span(i)]))
        r.act[b, rows, :] = act
        r.slope[b, rows, :] = slope

    def norm_tile(i, b, branch, up_all, start):
        part = slice(start, start + CHUNK)
        here = pl.ds(pl.multiple_of(i * SPAN + start, CHUNK), CHUNK)
        alive = alive_at(i * SPAN + start, CHUNK)
        hat, inverse = norm_stats(branch[:, part])
        result = (r.x1[:, here] + hat * vector("fgain") + vector("fbias")) * alive
        r.result_stage[here, :] = result.T.astype(BF16)
        up = up_all[:, part] * alive
        r.x1[:, here] = up
        r.g_vec[4] += up * hat
        r.g_vec[5] += up
        r.branch[b, :, part] = norm_back(hat, inverse, vector("fgain"), up).astype(BF16)

    def contract(i, b, rows, total):
        grad_act = nn(r.ws[rows, :], r.branch[b])
        for_shrink = nt(r.act[b, rows, :], r.branch[b])
        grad_hidden = r.slope[b, rows, :] * grad_act.astype(BF16)
        for_expand = nt(grad_hidden, r.concat[:, span(i)])
        for_concat = nn(r.we[:, rows], grad_hidden)
        r.g_ws[rows, :] += for_shrink
        r.g_we[rows, :] += for_expand
        return for_concat if total is None else total + for_concat

    def settle(i, total):
        r.x1[:, span(i)] += total[:width]
        r.grad_normed[:, span(i)] = total[width:]

    starts = range(0, hidden, SPAN)
    for name in ("act", "slope", "branch"):
        getattr(r, name)[2] = jnp.zeros(getattr(r, name).shape[1:], BF16)
    for start in starts:
        expand(0, 0, slice(start, start + SPAN))

    def feed(j, carry):
        for b in range(3):
            i = 3 * j + b
            before = jnp.maximum(i - 1, 0)
            after = jnp.minimum(i + 1, spans - 1)
            branch = nn(r.shrink_t[...], r.act[b])
            up_all = nt(r.eye[...], r.cot[span(i), :])
            total = None
            for number, start in enumerate(starts):
                rows = slice(start, start + SPAN)
                total = contract(before, (b + 2) % 3, rows, total)
                expand(after, (b + 1) % 3, rows)
                if number in (1, 2):
                    norm_tile(i, b, branch, up_all, (number - 1) * CHUNK)
            settle(before, total)
        return carry

    lax.fori_loop(0, spans // 3, feed, 0)
    total = None
    for start in starts:
        total = contract(spans - 1, (spans - 1) % 3, slice(start, start + SPAN), total)
    settle(spans - 1, total)

    def store_result(w, carry):
        store_rows(r.result, r.result_stage, w, r.sem_result).start()
        return carry

    lax.fori_loop(0, windows, store_result, 0)

    feed_sum = Reduction(r, sizes.plans["feed"], "feed", sizes.scale, sibling, peer, core, me)
    cross_sum = Reduction(r, sizes.plans["cross"], "cross", sizes.scale, sibling, peer, core, me)
    self_sum = Reduction(r, sizes.plans["self"], "self", sizes.scale, sibling, peer, core, me)
    feed_sum.begin([r.g_we.at[:, pl.ds(0, width)], r.g_we.at[:, pl.ds(width, width)], r.g_ws])

    def upstream(w, merged, grad_at, number, gain, out, gradient, merge, inverse):
        sums = [jnp.zeros((width, CHUNK), F32)] * 2
        for start in range(0, WSLOT, CHUNK):
            hat, root = norm_stats(merged[:, start : start + CHUNK])
            grad = grad_at(start)
            sums = [sums[0] + grad * hat, sums[1] + grad]
            r.grad_merged[:, start : start + CHUNK] = norm_back(hat, root, vector(gain), grad).astype(BF16)
        r.g_vec[number] += sums[0]
        r.g_vec[number + 1] += sums[1]
        out = out[:, cols_at(w)]
        gradient[...] += nt(out, r.grad_merged[...])
        up = (nn(merge[...], r.grad_merged[...]) * inverse[:, cols_at(w)]).astype(BF16)
        r.up[...] = up
        r.inner[...] = jnp.sum(up.astype(F32) * out.astype(F32), axis=0, keepdims=True)

    def backward_cross(w, carry):
        @pl.when(w == 1)
        def _():
            feed_sum.scatter()

        @pl.when(w == windows - 1)
        def _():
            feed_sum.gather()

        upstream(
            w, nn(r.cross_merge_t[...], r.out_two[:, cols_at(w)]),
            lambda start: r.grad_normed[:, cols_at(w, start, CHUNK)],
            2, "cgain", r.out_two, r.g_cm, r.cm, r.inverse_two,
        )
        other = r.other[rows_at(w), :]
        r.k_t[...] = nt(r.cross_k_t[...], other).astype(BF16)
        r.v[...] = nn(other, r.cv[...]).astype(BF16)
        attend_back(w, r.exps_two)
        r.back[w] = nn(r.cross_kv[...], r.dqkv[width:, :]).astype(BF16)
        send_back(w).start()
        r.g_cqkv[:width] += nt(r.dqkv[:width, :], r.concat[:width, cols_at(w)])
        r.g_cqkv[width:] += nn(r.dqkv[width:, :], r.other[rows_at(w), :])
        r.x1[:, cols_at(w)] += nn(r.cq[...], r.dqkv[:width, :])
        return carry

    lax.fori_loop(0, windows, backward_cross, 0)
    cross_sum.begin([r.g_cqkv, r.g_cm])

    def backward_self(w, carry):
        @pl.when(w == 1)
        def _():
            feed_sum.share()
            cross_sum.scatter()

        @pl.when(w == windows - 1)
        def _():
            feed_sum.finish()
            feed_sum.store(r.feed_out).start()
            cross_sum.gather()

        x = r.x[rows_at(w), :]
        r.q_t[:, cols_at(w)] = nt(r.self_qv_t[:width, :], x).astype(BF16)
        r.k_t[...] = nt(r.self_k_t[...], x).astype(BF16)
        r.v[...] = nn(x, r.sv[...]).astype(BF16)
        send_back(w).wait()

        def grad_at(start):
            here = cols_at(w, start, CHUNK)
            grad = r.x1[:, here] + r.received[w, :, start : start + CHUNK].astype(F32)
            r.x1[:, here] = grad
            return grad

        upstream(
            w, nn(r.self_merge_t[...], r.out_one[:, cols_at(w)]), grad_at,
            0, "sgain", r.out_one, r.g_sm, r.sm, r.inverse_one,
        )
        attend_back(w, r.exps)
        r.g_sqkv[...] += nn(r.dqkv[...], r.x[rows_at(w), :])

        @pl.when(w >= 2)
        def _():
            store_rows(r.grad, r.grad_stage, w, r.sem_grad, -2).wait()

        total = r.x1[:, cols_at(w)] + nn(r.self_qkv[...], r.dqkv[...])
        r.grad_stage[pl.ds(pl.multiple_of(lax.rem(w, 2) * WSLOT, WSLOT), WSLOT), :] = total.T
        store_rows(r.grad, r.grad_stage, w, r.sem_grad, 0).start()
        return carry

    lax.fori_loop(0, windows, backward_self, 0)
    self_sum.begin([r.g_sqkv, r.g_sm], r.g_vec)
    cross_sum.share()
    self_sum.scatter()
    cross_sum.finish()
    cross_sum.store(r.cross_out).start()
    self_sum.gather()
    if self_sum.full:
        r.totals[...] = self_sum.vector_total()
    self_sum.share()
    self_sum.finish()
    self_sum.store(r.self_out).start()
    if not self_sum.full:
        r.totals[...] = self_sum.total[0, 0, self_sum.shard :].astype(F32)

    def drain(w, carry):
        store_rows(r.result, r.result_stage, w, r.sem_result).wait()

        @pl.when(w >= windows - 2)
        def _():
            store_rows(r.grad, r.grad_stage, w, r.sem_grad, 0).wait()

        return carry

    lax.fori_loop(0, windows, drain, 0)
    feed_sum.store(r.feed_out).wait()
    cross_sum.store(r.cross_out).wait()
    self_sum.store(r.self_out).wait()


class Reduction:
    def __init__(self, r, plan, name, scale, sibling, peer, core, me):
        self.sibling, self.peer, self.core, self.me = sibling, peer, core, me
        self.scale = scale
        self.peers, self.owners, self.shard, self.extra, self.kept = (
            plan.peers, plan.owners, plan.shard, plan.extra, plan.kept
        )
        self.half = self.owners * self.shard
        self.full = self.owners == self.peers
        for field in ("pack", "from_sibling", "inbox", "total", "sems"):
            setattr(self, field, getattr(r, name + "_" + field))

    def copy(self, source, target, number, device):
        return pltpu.make_async_remote_copy(
            src_ref=source, dst_ref=target, send_sem=self.sems.at[0, number],
            recv_sem=self.sems.at[1, number], device_id=device, device_id_type=MESH,
        )

    def owning(self, then, otherwise=None):
        if self.full:
            then()
        else:
            pl.when(self.me < self.owners)(then)
            if otherwise is not None:
                pl.when(self.me >= self.owners)(otherwise)

    def halves(self):
        return self.copy(self.pack.at[1 - self.core], self.from_sibling, 0, self.sibling)

    def begin(self, pieces, vec=None):
        at = 0
        width = self.pack.shape[3]
        for piece in pieces:
            taken = 0
            while taken < piece.shape[0]:
                which, inside = divmod(at, self.half)
                index, offset = divmod(inside, self.shard)
                left = piece.shape[0] - taken
                if offset or left < self.shard:
                    count = min(left, self.shard - offset)
                    self.pack[which, index, offset : offset + count] = piece[
                        taken : taken + count, :
                    ].astype(BF16)
                else:
                    blocks = min(left // self.shard, self.owners - index)
                    count = blocks * self.shard
                    self.pack[which, index : index + blocks, : self.shard] = (
                        piece[taken : taken + count, :].astype(BF16).reshape(blocks, self.shard, width)
                    )
                at += count
                taken += count
        while at < 2 * self.half:
            which, inside = divmod(at, self.half)
            index, offset = divmod(inside, self.shard)
            count = self.shard - offset
            self.pack[which, index, offset : self.shard] = jnp.zeros((count, width), BF16)
            at += count
        if self.extra:
            sums = jnp.concatenate([jnp.sum(vec[i].T, axis=0, keepdims=True) for i in range(vec.shape[0])])
            rows = jnp.concatenate([sums, jnp.zeros((self.extra - vec.shape[0], width), F32)]).astype(BF16)
            for which in range(2):
                self.pack[which, :, self.shard :] = jnp.broadcast_to(
                    rows[None], (self.owners, self.extra, width)
                )
        self.halves().start()

    def wait(self, number, sent, received):
        if sent is not None:
            self.copy(sent, sent, number, self.sibling).wait_send()
        if received is not None:
            self.copy(received, received, number, self.sibling).wait_recv()

    def scatter(self):
        self.halves().wait()
        mine = self.pack[self.core].astype(F32) + self.from_sibling[...].astype(F32)
        self.pack[self.core] = mine.astype(BF16)

        def send(step, carry):
            index, device = self.peer(step)

            def go():
                place = self.pack.at[self.core, index]
                self.copy(place, self.inbox.at[self.me], 1, device).start()

            go() if self.full else pl.when(index < self.owners)(go)
            return carry

        lax.fori_loop(1, self.peers, send, 0)

        def own():
            self.inbox[self.me] = self.pack[self.core, self.me]

        self.owning(own)

    def gather(self):
        def own():
            self.wait(
                1, self.pack.at[0, pl.ds(0, self.owners - 1)], self.inbox.at[pl.ds(0, self.peers - 1)]
            )
            total = jnp.sum(self.inbox[:, : self.kept].astype(F32), axis=0) * self.scale
            self.total[self.core, self.me] = total.astype(BF16)

            def send(step, carry):
                place = self.total.at[self.core, self.me]
                self.copy(place, place, 2, self.peer(step)[1]).start()
                return carry

            lax.fori_loop(1, self.peers, send, 0)

        self.owning(own, lambda: self.wait(1, self.pack.at[0], None))

    def vector_total(self):
        return jnp.sum(self.inbox[:, self.shard :].astype(F32), axis=0) * self.scale

    def share(self):
        def own():
            for count in (self.owners - 1,) * ((self.peers - 1) // (self.owners - 1)) + (
                (self.peers - 1) % (self.owners - 1),
            ):
                if count:
                    self.wait(2, self.total.at[0, pl.ds(0, count)], None)
            self.wait(2, None, self.total.at[0, pl.ds(0, self.owners - 1)])

        self.owning(own, lambda: self.wait(2, None, self.total.at[0]))
        self.copy(self.total.at[self.core], self.total.at[self.core], 3, self.sibling).start()

    def finish(self):
        self.copy(self.total.at[self.core], self.total.at[self.core], 3, self.sibling).wait()

    def store(self, target):
        return pltpu.make_async_copy(self.total, target, self.sems.at[0, 4])


def scratch_shapes(sizes):
    width, hidden, windows, rows, peers = sizes.width, sizes.hidden, sizes.windows, sizes.rows, sizes.peers
    vmem = pltpu.VMEM
    dma = pltpu.SemaphoreType.DMA
    square = vmem((width, width), F32)
    shapes = {
        "eye": vmem((width, width), BF16),
        "self_qv_t": vmem((2 * width, width), BF16),
        "self_k_t": vmem((width, width), BF16),
        "self_merge_t": vmem((width, width), BF16),
        "self_qkv": vmem((width, 3 * width), BF16),
        "vectors": vmem((len(VECTORS), width, CHUNK), F32),
        "cross_q_t": vmem((width, width), BF16),
        "cross_k_t": vmem((width, width), BF16),
        "cross_v_t": vmem((width, width), BF16),
        "cross_merge_t": vmem((width, width), BF16),
        "cross_kv": vmem((width, 2 * width), BF16),
        "expand_t": vmem((hidden, 2 * width), BF16),
        "shrink_t": vmem((width, hidden), BF16),
        "g_sqkv": vmem((3 * width, width), F32),
        "g_cqkv": vmem((3 * width, width), F32),
        "g_sm": square,
        "g_cm": square,
        "g_we": vmem((hidden, 2 * width), F32),
        "g_ws": vmem((hidden, width), F32),
        "g_vec": vmem((len(VECTORS), width, CHUNK), F32),
        "q_t": vmem((width, rows), BF16),
        "k": vmem((WSLOT, width), BF16),
        "v_aug": vmem((width + ONES, WSLOT), BF16),
        "out_one": vmem((width, rows), BF16),
        "out_two": vmem((width, rows), BF16),
        "inverse_one": vmem((1, rows), F32),
        "inverse_two": vmem((1, rows), F32),
        "x1": vmem((width, rows), F32),
        "concat": vmem((2 * width, rows), BF16),
        "send": vmem((rows, width), BF16),
        "other": vmem((rows, width), BF16),
        "back": vmem((windows, width, WSLOT), BF16),
        "received": vmem((windows, width, WSLOT), BF16),
        "grad_normed": vmem((width, rows), F32),
        "exps": vmem((windows, WSLOT, WSLOT), BF16),
        "exps_two": vmem((windows, WSLOT, WSLOT), BF16),
        "diff": vmem((WSLOT, WSLOT), BF16),
        "act": vmem((3, hidden, SPAN), BF16),
        "slope": vmem((3, hidden, SPAN), BF16),
        "branch": vmem((3, width, SPAN), BF16),
        "buf_a": vmem((WSLOT, SPAN), F32),
        "buf_b": vmem((WSLOT, SPAN), F32),
        "grad_merged": vmem((width, WSLOT), BF16),
        "k_t": vmem((width, WSLOT), BF16),
        "v": vmem((WSLOT, width), BF16),
        "up": vmem((width, WSLOT), BF16),
        "inner": vmem((1, WSLOT), F32),
        "dqkv": vmem((3 * width, WSLOT), BF16),
        "result_stage": vmem((rows, width), BF16),
        "grad_stage": vmem((2 * WSLOT, width), F32),
        "sem_x": dma((2, windows)),
        "sem_b": dma((2, windows)),
        "sem_result": dma((windows,)),
        "sem_grad": dma((windows,)),
    }
    for name, plan in sizes.plans.items():
        part = plan.shard + plan.extra
        shapes[name + "_pack"] = vmem((2, plan.owners, part, width), BF16)
        shapes[name + "_from_sibling"] = vmem((plan.owners, part, width), BF16)
        shapes[name + "_inbox"] = vmem((peers, part, width), BF16)
        shapes[name + "_total"] = vmem((2, plan.owners, plan.kept, width), BF16)
        shapes[name + "_sems"] = dma((2, 5))
    return shapes


def total_rows(total, shard, start, count):
    _, peers, _, width = total.shape
    at = start
    found = []
    while at < start + count:
        which, inside = divmod(at, peers * shard)
        index, offset = divmod(inside, shard)
        left = start + count - at
        if offset or left < shard:
            take = min(shard - offset, left)
            found.append(total[which, index, offset : offset + take])
        else:
            blocks = min(left // shard, peers - index)
            take = blocks * shard
            found.append(total[which, index : index + blocks, :shard].reshape(take, width))
        at += take
    return found[0] if len(found) == 1 else jnp.concatenate(found, axis=0)


def hand_out(sizes, *refs):
    result_in, grad_in, feed, cross, own, totals, result, grad = refs[:8]
    (o_sq, o_sk, o_sv, o_sm, o_sgain, o_sbias, o_cq, o_ck, o_cv, o_cm, o_cgain, o_cbias,
     o_we, o_ws, o_fgain, o_fbias) = refs[8:24]
    width, hidden = sizes.width, sizes.hidden
    shards = [plan.shard for plan in sizes.plans.values()]
    result[...] = result_in[...]
    grad[...] = grad_in[...]

    @pl.when(pl.program_id(0) == 0)
    def _():
        o_we[:width, :] = total_rows(feed, shards[0], 0, hidden).astype(F32).T
        o_we[width:, :] = total_rows(feed, shards[0], hidden, hidden).astype(F32).T
        o_ws[...] = total_rows(feed, shards[0], 2 * hidden, hidden).astype(F32)
        for source, shard, group in (
            (cross, shards[1], (o_cq, o_ck, o_cv, o_cm)), (own, shards[2], (o_sq, o_sk, o_sv, o_sm))
        ):
            for i, ref in enumerate(group):
                total = total_rows(source, shard, i * width, width).astype(F32)
                ref[...] = total if i == 3 else total.T
        for i, ref in enumerate((o_sgain, o_sbias, o_cgain, o_cbias, o_fgain, o_fbias)):
            ref[...] = totals[i : i + 1, :]


def local(features, cotangent, slot_pair, crop_size, *weights):
    rows, width = features.shape[1:]
    hidden = weights[12].shape[1]
    peers = lax.axis_size("pix")

    def plan(count, extra=0):
        shard = -(-count // (2 * peers * 16)) * 16
        owners = min(peers, -(-count // (2 * shard)))
        kept = shard + (extra if owners < peers else 0)
        return types.SimpleNamespace(peers=peers, owners=owners, shard=shard, extra=extra, kept=kept)

    sizes = types.SimpleNamespace(
        rows=rows, width=width, hidden=hidden, windows=rows // WSLOT, peers=peers,
        scale=1.0 / math.sqrt(2.0 * rows * peers),
        plans={"feed": plan(3 * hidden), "cross": plan(4 * width), "self": plan(4 * width, 16)},
    )
    flat = lambda value: value.reshape(1, -1) if value.ndim == 1 else value
    shape = jax.ShapeDtypeStruct
    small = pl.BlockSpec(memory_space=pltpu.VMEM)
    large = pl.BlockSpec(memory_space=pl.ANY)
    scalar = pl.BlockSpec(memory_space=pltpu.SMEM)
    square = shape((width, width), F32)
    row = shape((1, width), F32)
    big = [shape((rows, width), BF16), shape((rows, width), F32)]
    middle = pl.pallas_call(
        functools.partial(layer_kernel, sizes),
        in_specs=[small, small, scalar, scalar] + [small] * 16,
        out_specs=[large] * 5 + [small],
        out_shape=big + [
            shape((2, plan.owners, plan.kept, width), BF16) for plan in sizes.plans.values()
        ] + [shape((16, width), F32)],
        scratch_shapes=list(scratch_shapes(sizes).values()),
        compiler_params=pltpu.CompilerParams(
            collective_id=0, has_side_effects=True, vmem_limit_bytes=63 * 2**20
        ),
        name="layer",
    )(features[0], cotangent[0], slot_pair, crop_size.T, *[flat(weight) for weight in weights])
    moved = [pl.BlockSpec((WSLOT, width), lambda w: (w, 0))] * 2
    whole = lambda shape: pl.BlockSpec(shape, lambda w: (0,) * len(shape))
    smalls = [
        square, square, square, square, row, row, square, square, square, square, row, row,
        shape((2 * width, hidden), F32), shape((hidden, width), F32), row, row,
    ]
    outs = pl.pallas_call(
        functools.partial(hand_out, sizes),
        grid=(sizes.windows,),
        in_specs=moved + [whole(value.shape) for value in middle[2:]],
        out_specs=moved + [whole(value.shape) for value in smalls],
        out_shape=big + smalls,
        compiler_params=pltpu.CompilerParams(vmem_limit_bytes=60 * 2**20),
        name="hand_out",
    )(*middle)
    result, grad = outs[:2]
    return (result[None], grad[None]) + tuple(
        out.reshape(-1) if out.shape[0] == 1 else out for out in outs[2:]
    )


def solution(mesh):
    split = P("frame", "pix", None)
    return jax.shard_map(
        local,
        mesh=mesh,
        in_specs=(split, split, P("pix")) + (P(),) * 17,
        out_specs=(split, split) + (P(),) * 16,
        check_vma=False,
    )
```

```python
import functools
import math
import types

import jax
import jax.numpy as jnp
from jax import lax
from jax.experimental import pallas as pl
from jax.experimental.pallas import tpu as pltpu
from jax.sharding import PartitionSpec as P

WSLOT = 1152
FEWEST = 704
NEGATIVE = -1e30
EPSILON = 1e-05
LOG2E = 1.4426950408889634
F32 = jnp.float32
BF16 = jnp.bfloat16
MESH = pl.DeviceIdType.MESH
TAIL_SHIFT = 2.7777777777777777
TAIL_POLY = (0.39765776262463953, 1.1594294101832299, 1.9333185594349698, 10.032517622923805, -5.2492700447308085, -9.371923274701059)
SPAN = 256
CHUNK = 128
TILES = ((0, 256), (256, 256), (512, 256), (768, 256), (1024, 128))
ONES = 16


def nn(left, right):
    return jnp.dot(left, right, preferred_element_type=F32)


def nt(left, right):
    return lax.dot_general(left, right, (((1,), (1,)), ((), ())), preferred_element_type=F32)


def norm_stats(values):
    centre = jnp.mean(values, axis=0, keepdims=True)
    shifted = values - centre
    spread = jnp.mean(shifted * shifted, axis=0, keepdims=True)
    inverse = lax.rsqrt(spread + EPSILON)
    return shifted * inverse, inverse


def norm_back(hat, inverse, gain, upstream):
    scaled = upstream * gain
    first = jnp.mean(scaled, axis=0, keepdims=True)
    second = jnp.mean(scaled * hat, axis=0, keepdims=True)
    return inverse * (scaled - first - hat * second)


def gelu_both(values):
    bell = jnp.exp2(values * (values * (-0.5 * LOG2E))).astype(BF16)
    t = (1.0 / (jnp.abs(values) + TAIL_SHIFT)).astype(BF16)
    low = values.astype(BF16)
    poly = t * BF16(TAIL_POLY[-1]) + BF16(TAIL_POLY[-2])
    for coefficient in TAIL_POLY[-3::-1]:
        poly = poly * t + BF16(coefficient)
    tail = poly * t * bell
    phi = jnp.where(low >= BF16(0.0), BF16(1.0) - tail, tail)
    return low * phi, phi + low * bell * BF16(1.0 / math.sqrt(2.0 * math.pi))


def flip(values):
    return values.astype(F32).T.astype(BF16)


INPUTS = (
    "x", "cot", "slot", "crop", "sq", "sk", "sv", "sm", "sgain", "sbias",
    "cq", "ck", "cv", "cm", "cgain", "cbias", "we", "ws", "fgain", "fbias",
)
OUTPUTS = ("result", "grad", "feed_out", "cross_out", "self_out", "totals")
VECTORS = ("sgain", "sbias", "cgain", "cbias", "fgain", "fbias")


def layer_kernel(sizes, *refs):
    names = INPUTS + OUTPUTS + tuple(scratch_shapes(sizes))
    r = types.SimpleNamespace(**dict(zip(names, refs, strict=True)))
    width, hidden, windows, peers = sizes.width, sizes.hidden, sizes.windows, sizes.peers
    factor = 1.0 / math.sqrt(width)
    scale = factor * LOG2E
    frame = lax.axis_index("frame")
    pix = lax.axis_index("pix")
    core = lax.rem(pix, 2)
    me = frame * (peers // 2) + lax.div(pix, 2)
    partner = (1 - frame, pix)
    sibling = (frame, pix + 1 - 2 * core)

    def peer(step):
        index = lax.rem(me + step, peers)
        return index, (lax.div(index, peers // 2), lax.rem(index, peers // 2) * 2 + core)

    barrier = pltpu.get_barrier_semaphore()
    pl.semaphore_signal(barrier, inc=1, device_id=sibling, device_id_type=MESH)

    def greet(step, carry):
        pl.semaphore_signal(barrier, inc=1, device_id=peer(step)[1], device_id_type=MESH)
        return carry

    lax.fori_loop(1, peers, greet, 0)

    slot = r.slot[0]
    live = lax.shift_right_logical(r.crop[0, slot], 1) * lax.shift_right_logical(r.crop[1, slot], 1)

    r.eye[...] = jnp.where(
        lax.broadcasted_iota(jnp.int32, (width, width), 0)
        == lax.broadcasted_iota(jnp.int32, (width, width), 1),
        1.0, 0.0,
    ).astype(BF16)
    r.self_qv_t[:width] = flip(r.sq[...])
    r.self_qv_t[width:] = flip(r.sv[...])
    r.self_k_t[...] = flip(r.sk[...])
    r.self_merge_t[...] = flip(r.sm[...])
    r.self_qkv[:, :width] = r.sq[...]
    r.self_qkv[:, width : 2 * width] = r.sk[...]
    r.self_qkv[:, 2 * width :] = r.sv[...]
    for i, name in enumerate(VECTORS):
        r.vectors[i] = jnp.broadcast_to(getattr(r, name)[...], (width, CHUNK)).T
    vector = lambda name: r.vectors[VECTORS.index(name)]
    for name in ("g_sqkv", "g_sm", "g_cqkv", "g_cm", "g_we", "g_ws", "g_vec"):
        getattr(r, name)[...] = jnp.zeros_like(getattr(r, name))
    r.v_aug[width:, :] = jnp.ones((ONES, WSLOT), BF16)

    def alive_at(start, size):
        token = lax.broadcasted_iota(jnp.int32, (1, size), 1) + lax.rem(start, WSLOT)
        return jnp.where(token < live, 1.0, 0.0)

    def rows_at(w):
        return pl.ds(pl.multiple_of(w * WSLOT, WSLOT), WSLOT)

    def cols_at(w, start=0, size=WSLOT):
        return pl.ds(pl.multiple_of(w * WSLOT + start, 128), size)

    def send_rows(w):
        return pltpu.make_async_remote_copy(
            src_ref=r.send.at[rows_at(w), :], dst_ref=r.other.at[rows_at(w), :],
            send_sem=r.sem_x.at[0, w], recv_sem=r.sem_x.at[1, w], device_id=partner, device_id_type=MESH,
        )

    def send_back(w):
        return pltpu.make_async_remote_copy(
            src_ref=r.back.at[w], dst_ref=r.received.at[w],
            send_sem=r.sem_b.at[0, w], recv_sem=r.sem_b.at[1, w], device_id=partner, device_id_type=MESH,
        )

    def store_rows(target, stage, w, sem, back=None):
        place = w if back is None else lax.rem(w, 2)
        w = w if back is None else w + back
        return pltpu.make_async_copy(stage.at[rows_at(place), :], target.at[rows_at(w), :], sem.at[w])

    def attend(w, exps, out, inverse):
        bufs = (r.buf_a, r.buf_b)

        def score(t):
            first, size = TILES[t]
            got = nn(r.k[...], r.q_t[:, cols_at(w, first, size)])
            rest = got[FEWEST:]
            row = lax.broadcasted_iota(jnp.int32, rest.shape, 0) + FEWEST
            rest = jnp.where(row < live, rest, NEGATIVE)
            bufs[t % 2][:FEWEST, :size] = got[:FEWEST]
            bufs[t % 2][FEWEST:, :size] = rest
            return scale * jnp.maximum(
                jnp.max(got[:FEWEST], axis=0, keepdims=True), jnp.max(rest, axis=0, keepdims=True)
            )

        def output_part(t, rows, total):
            first, size = TILES[t]
            part = nn(r.v_aug[:, rows], exps[w, rows, first : first + size])
            return part if total is None else total + part

        def output(t, both):
            first, size = TILES[t]
            share = 1.0 / both[width : width + 1]
            inverse[:, cols_at(w, first, size)] = share
            out[:, cols_at(w, first, size)] = (both[:width] * share).astype(BF16)

        top = score(0)
        for t, (first, size) in enumerate(TILES):
            after = score(t + 1) if t + 1 < len(TILES) else None
            total = None
            for start, count in TILES:
                rows = slice(start, start + count)
                if t:
                    total = output_part(t - 1, rows, total)
                exps[w, rows, first : first + size] = jnp.exp2(
                    bufs[t % 2][rows, :size] * scale - top
                ).astype(BF16)
            if t:
                output(t - 1, total)
            top = after
        last = len(TILES) - 1
        output(last, output_part(last, slice(0, WSLOT), None))

    def attend_back(w, exps):
        def query(t):
            first, size = TILES[t]
            cols = slice(first, first + size)
            r.dqkv[:width, cols] = (nn(r.k_t[...], r.diff[:, cols]) * factor).astype(BF16)

        for t, (first, size) in enumerate(TILES):
            cols = slice(first, first + size)
            grad = nn(r.v[...], r.up[:, cols]) - r.inner[:, cols]
            r.diff[:, cols] = exps[w, :, cols] * grad.astype(BF16)
            if t:
                query(t - 1)
        grad_value = nt(exps[w], r.up[...])
        query(len(TILES) - 1)
        grad_key = nt(r.diff[...], r.q_t[:, cols_at(w)]) * factor
        r.dqkv[2 * width :, :] = grad_value.T.astype(BF16)
        r.dqkv[width : 2 * width, :] = grad_key.T.astype(BF16)

    def forward_self(w, carry):
        x = r.x[rows_at(w), :]
        stacked = nt(r.self_qv_t[...], x).astype(BF16)
        r.q_t[:, cols_at(w)] = stacked[:width]
        r.v_aug[:width, :] = stacked[width:]
        r.k[...] = nn(x, r.sk[...]).astype(BF16)
        attend(w, r.exps, r.out_one, r.inverse_one)
        merged = nn(r.self_merge_t[...], r.out_one[:, cols_at(w)])
        x_t = nt(r.eye[...], r.x[rows_at(w), :])
        for start in range(0, WSLOT, CHUNK):
            cols = slice(start, start + CHUNK)
            hat, _ = norm_stats(merged[:, cols])
            x1 = x_t[:, cols] + hat * vector("sgain") + vector("sbias")
            r.x1[:, cols_at(w, start, CHUNK)] = x1
            r.concat[:width, cols_at(w, start, CHUNK)] = x1.astype(BF16)
            r.send[pl.ds(pl.multiple_of(w * WSLOT + start, CHUNK), CHUNK), :] = x1.T.astype(BF16)

        @pl.when(w == 0)
        def _():
            pl.semaphore_wait(barrier, peers)

        send_rows(w).start()
        return carry

    lax.fori_loop(0, windows, forward_self, 0)

    r.cross_q_t[...] = flip(r.cq[...])
    r.cross_k_t[...] = flip(r.ck[...])
    r.cross_v_t[...] = flip(r.cv[...])
    r.cross_merge_t[...] = flip(r.cm[...])
    r.cross_kv[:, :width] = r.ck[...]
    r.cross_kv[:, width:] = r.cv[...]
    r.expand_t[...] = flip(r.we[...])
    r.shrink_t[...] = flip(r.ws[...])

    def forward_cross(w, carry):
        r.q_t[:, cols_at(w)] = nn(r.cross_q_t[...], r.concat[:width, cols_at(w)]).astype(BF16)
        send_rows(w).wait()
        other = r.other[rows_at(w), :]
        r.v_aug[:width, :] = nt(r.cross_v_t[...], other).astype(BF16)
        r.k[...] = nn(other, r.ck[...]).astype(BF16)
        attend(w, r.exps_two, r.out_two, r.inverse_two)
        merged = nn(r.cross_merge_t[...], r.out_two[:, cols_at(w)])
        for start in range(0, WSLOT, CHUNK):
            hat, _ = norm_stats(merged[:, start : start + CHUNK])
            r.concat[width:, cols_at(w, start, CHUNK)] = (
                hat * vector("cgain") + vector("cbias")
            ).astype(BF16)
        return carry

    lax.fori_loop(0, windows, forward_cross, 0)

    spans = sizes.rows // SPAN

    def span(i):
        return pl.ds(pl.multiple_of(i * SPAN, SPAN), SPAN)

    def norm_tile(i, b, branch, up_all, start):
        part = slice(start, start + CHUNK)
        here = pl.ds(pl.multiple_of(i * SPAN + start, CHUNK), CHUNK)
        alive = alive_at(i * SPAN + start, CHUNK)
        hat, inverse = norm_stats(branch[:, part])
        result = (r.x1[:, here] + hat * vector("fgain") + vector("fbias")) * alive
        r.result_stage[here, :] = result.T.astype(BF16)
        up = up_all[:, part] * alive
        r.x1[:, here] = up
        r.g_vec[4] += up * hat
        r.g_vec[5] += up
        r.branch[b, :, part] = norm_back(hat, inverse, vector("fgain"), up).astype(BF16)

    def settle(i, total):
        r.x1[:, span(i)] += total[:width]
        r.grad_normed[:, span(i)] = total[width:]

    parts = [slice(start, start + SPAN) for start in range(0, hidden, SPAN)]

    def expand(i):
        r.buf_a[:hidden, :] = nn(r.expand_t[...], r.concat[:, span(i)])

    def activate(b, rows):
        act, slope = gelu_both(r.buf_a[rows, :])
        r.act[b, rows, :] = act
        r.slope[b, rows, :] = slope

    def hide(b):
        r.hid[...] = r.slope[b] * nn(r.ws[...], r.branch[b]).astype(BF16)

    def add(total, part):
        return part if total is None else total + part

    for name in ("act", "slope", "branch"):
        getattr(r, name)[2] = jnp.zeros(getattr(r, name).shape[1:], BF16)
    expand(0)
    for rows in parts:
        activate(0, rows)

    def feed(j, carry):
        for b in range(3):
            i = 3 * j + b
            old = (b + 2) % 3
            before = jnp.maximum(i - 1, 0)
            expand(jnp.minimum(i + 1, spans - 1))
            hide(old)
            branch, total = None, None
            for rows in parts:
                branch = add(branch, nn(r.shrink_t[:, rows], r.act[b, rows, :]))
                total = add(total, nn(r.we[:, rows], r.hid[rows, :]))
                activate((b + 1) % 3, rows)
            settle(before, total)
            up_all = nt(r.eye[...], r.cot[span(i), :])
            for_shrink = nt(r.act[old], r.branch[old])
            norm_tile(i, b, branch, up_all, 0)
            for_expand = nt(r.hid[...], r.concat[:, span(before)])
            norm_tile(i, b, branch, up_all, CHUNK)
            r.g_ws[...] += for_shrink
            r.g_we[...] += for_expand
        return carry

    lax.fori_loop(0, spans // 3, feed, 0)
    last = (spans - 1) % 3
    hide(last)
    settle(spans - 1, nn(r.we[...], r.hid[...]))
    r.g_ws[...] += nt(r.act[last], r.branch[last])
    r.g_we[...] += nt(r.hid[...], r.concat[:, span(spans - 1)])

    def store_result(w, carry):
        store_rows(r.result, r.result_stage, w, r.sem_result).start()
        return carry

    lax.fori_loop(0, windows, store_result, 0)

    feed_sum = Reduction(r, sizes.plans["feed"], "feed", sizes.scale, sibling, peer, core, me)
    cross_sum = Reduction(r, sizes.plans["cross"], "cross", sizes.scale, sibling, peer, core, me)
    self_sum = Reduction(r, sizes.plans["self"], "self", sizes.scale, sibling, peer, core, me)
    feed_sum.begin([r.g_we.at[:, pl.ds(0, width)], r.g_we.at[:, pl.ds(width, width)], r.g_ws])

    def upstream(w, merged, grad_at, number, gain, out, gradient, merge, inverse):
        sums = [jnp.zeros((width, CHUNK), F32)] * 2
        for start in range(0, WSLOT, CHUNK):
            hat, root = norm_stats(merged[:, start : start + CHUNK])
            grad = grad_at(start)
            sums = [sums[0] + grad * hat, sums[1] + grad]
            r.grad_merged[:, start : start + CHUNK] = norm_back(hat, root, vector(gain), grad).astype(BF16)
        r.g_vec[number] += sums[0]
        r.g_vec[number + 1] += sums[1]
        out = out[:, cols_at(w)]
        gradient[...] += nt(out, r.grad_merged[...])
        up = (nn(merge[...], r.grad_merged[...]) * inverse[:, cols_at(w)]).astype(BF16)
        r.up[...] = up
        r.inner[...] = jnp.sum(up.astype(F32) * out.astype(F32), axis=0, keepdims=True)

    def backward_cross(w, carry):
        @pl.when(w == 1)
        def _():
            feed_sum.scatter()

        @pl.when(w == windows - 1)
        def _():
            feed_sum.gather()

        upstream(
            w, nn(r.cross_merge_t[...], r.out_two[:, cols_at(w)]),
            lambda start: r.grad_normed[:, cols_at(w, start, CHUNK)],
            2, "cgain", r.out_two, r.g_cm, r.cm, r.inverse_two,
        )
        other = r.other[rows_at(w), :]
        r.k_t[...] = nt(r.cross_k_t[...], other).astype(BF16)
        r.v[...] = nn(other, r.cv[...]).astype(BF16)
        attend_back(w, r.exps_two)
        r.back[w] = nn(r.cross_kv[...], r.dqkv[width:, :]).astype(BF16)
        send_back(w).start()
        r.g_cqkv[:width] += nt(r.dqkv[:width, :], r.concat[:width, cols_at(w)])
        r.g_cqkv[width:] += nn(r.dqkv[width:, :], r.other[rows_at(w), :])
        r.x1[:, cols_at(w)] += nn(r.cq[...], r.dqkv[:width, :])
        return carry

    lax.fori_loop(0, windows, backward_cross, 0)
    cross_sum.begin([r.g_cqkv, r.g_cm])

    def backward_self(w, carry):
        @pl.when(w == 1)
        def _():
            feed_sum.share()
            cross_sum.scatter()

        @pl.when(w == windows - 1)
        def _():
            feed_sum.finish()
            feed_sum.store(r.feed_out).start()
            cross_sum.gather()

        x = r.x[rows_at(w), :]
        r.q_t[:, cols_at(w)] = nt(r.self_qv_t[:width, :], x).astype(BF16)
        r.k_t[...] = nt(r.self_k_t[...], x).astype(BF16)
        r.v[...] = nn(x, r.sv[...]).astype(BF16)
        send_back(w).wait()

        def grad_at(start):
            here = cols_at(w, start, CHUNK)
            grad = r.x1[:, here] + r.received[w, :, start : start + CHUNK].astype(F32)
            r.x1[:, here] = grad
            return grad

        upstream(
            w, nn(r.self_merge_t[...], r.out_one[:, cols_at(w)]), grad_at,
            0, "sgain", r.out_one, r.g_sm, r.sm, r.inverse_one,
        )
        attend_back(w, r.exps)
        r.g_sqkv[...] += nn(r.dqkv[...], r.x[rows_at(w), :])

        @pl.when(w >= 2)
        def _():
            store_rows(r.grad, r.grad_stage, w, r.sem_grad, -2).wait()

        total = r.x1[:, cols_at(w)] + nn(r.self_qkv[...], r.dqkv[...])
        r.grad_stage[pl.ds(pl.multiple_of(lax.rem(w, 2) * WSLOT, WSLOT), WSLOT), :] = total.T
        store_rows(r.grad, r.grad_stage, w, r.sem_grad, 0).start()
        return carry

    lax.fori_loop(0, windows, backward_self, 0)
    self_sum.begin([r.g_sqkv, r.g_sm], r.g_vec)
    cross_sum.share()
    self_sum.scatter()
    cross_sum.finish()
    cross_sum.store(r.cross_out).start()
    self_sum.gather()
    if self_sum.full:
        r.totals[...] = self_sum.vector_total()
    self_sum.share()
    self_sum.finish()
    self_sum.store(r.self_out).start()
    if not self_sum.full:
        r.totals[...] = self_sum.total[0, 0, self_sum.shard :].astype(F32)

    def drain(w, carry):
        store_rows(r.result, r.result_stage, w, r.sem_result).wait()

        @pl.when(w >= windows - 2)
        def _():
            store_rows(r.grad, r.grad_stage, w, r.sem_grad, 0).wait()

        return carry

    lax.fori_loop(0, windows, drain, 0)
    feed_sum.store(r.feed_out).wait()
    cross_sum.store(r.cross_out).wait()
    self_sum.store(r.self_out).wait()


class Reduction:
    def __init__(self, r, plan, name, scale, sibling, peer, core, me):
        self.sibling, self.peer, self.core, self.me = sibling, peer, core, me
        self.scale = scale
        self.peers, self.owners, self.shard, self.extra, self.kept = (
            plan.peers, plan.owners, plan.shard, plan.extra, plan.kept
        )
        self.half = self.owners * self.shard
        self.full = self.owners == self.peers
        for field in ("pack", "from_sibling", "inbox", "total", "sems"):
            setattr(self, field, getattr(r, name + "_" + field))

    def copy(self, source, target, number, device):
        return pltpu.make_async_remote_copy(
            src_ref=source, dst_ref=target, send_sem=self.sems.at[0, number],
            recv_sem=self.sems.at[1, number], device_id=device, device_id_type=MESH,
        )

    def owning(self, then, otherwise=None):
        if self.full:
            then()
        else:
            pl.when(self.me < self.owners)(then)
            if otherwise is not None:
                pl.when(self.me >= self.owners)(otherwise)

    def halves(self):
        return self.copy(self.pack.at[1 - self.core], self.from_sibling, 0, self.sibling)

    def begin(self, pieces, vec=None):
        at = 0
        width = self.pack.shape[3]
        for piece in pieces:
            taken = 0
            while taken < piece.shape[0]:
                which, inside = divmod(at, self.half)
                index, offset = divmod(inside, self.shard)
                left = piece.shape[0] - taken
                if offset or left < self.shard:
                    count = min(left, self.shard - offset)
                    self.pack[which, index, offset : offset + count] = piece[
                        taken : taken + count, :
                    ].astype(BF16)
                else:
                    blocks = min(left // self.shard, self.owners - index)
                    count = blocks * self.shard
                    self.pack[which, index : index + blocks, : self.shard] = (
                        piece[taken : taken + count, :].astype(BF16).reshape(blocks, self.shard, width)
                    )
                at += count
                taken += count
        while at < 2 * self.half:
            which, inside = divmod(at, self.half)
            index, offset = divmod(inside, self.shard)
            count = self.shard - offset
            self.pack[which, index, offset : self.shard] = jnp.zeros((count, width), BF16)
            at += count
        if self.extra:
            sums = jnp.concatenate([jnp.sum(vec[i].T, axis=0, keepdims=True) for i in range(vec.shape[0])])
            rows = jnp.concatenate([sums, jnp.zeros((self.extra - vec.shape[0], width), F32)]).astype(BF16)
            for which in range(2):
                self.pack[which, :, self.shard :] = jnp.broadcast_to(
                    rows[None], (self.owners, self.extra, width)
                )
        self.halves().start()

    def wait(self, number, sent, received):
        if sent is not None:
            self.copy(sent, sent, number, self.sibling).wait_send()
        if received is not None:
            self.copy(received, received, number, self.sibling).wait_recv()

    def scatter(self):
        self.halves().wait()
        mine = self.pack[self.core].astype(F32) + self.from_sibling[...].astype(F32)
        self.pack[self.core] = mine.astype(BF16)

        def send(step, carry):
            index, device = self.peer(step)

            def go():
                place = self.pack.at[self.core, index]
                self.copy(place, self.inbox.at[self.me], 1, device).start()

            go() if self.full else pl.when(index < self.owners)(go)
            return carry

        lax.fori_loop(1, self.peers, send, 0)

        def own():
            self.inbox[self.me] = self.pack[self.core, self.me]

        self.owning(own)

    def gather(self):
        def own():
            self.wait(
                1, self.pack.at[0, pl.ds(0, self.owners - 1)], self.inbox.at[pl.ds(0, self.peers - 1)]
            )
            total = jnp.sum(self.inbox[:, : self.kept].astype(F32), axis=0) * self.scale
            self.total[self.core, self.me] = total.astype(BF16)

            def send(step, carry):
                place = self.total.at[self.core, self.me]
                self.copy(place, place, 2, self.peer(step)[1]).start()
                return carry

            lax.fori_loop(1, self.peers, send, 0)

        self.owning(own, lambda: self.wait(1, self.pack.at[0], None))

    def vector_total(self):
        return jnp.sum(self.inbox[:, self.shard :].astype(F32), axis=0) * self.scale

    def share(self):
        def own():
            for count in (self.owners - 1,) * ((self.peers - 1) // (self.owners - 1)) + (
                (self.peers - 1) % (self.owners - 1),
            ):
                if count:
                    self.wait(2, self.total.at[0, pl.ds(0, count)], None)
            self.wait(2, None, self.total.at[0, pl.ds(0, self.owners - 1)])

        self.owning(own, lambda: self.wait(2, None, self.total.at[0]))
        self.copy(self.total.at[self.core], self.total.at[self.core], 3, self.sibling).start()

    def finish(self):
        self.copy(self.total.at[self.core], self.total.at[self.core], 3, self.sibling).wait()

    def store(self, target):
        return pltpu.make_async_copy(self.total, target, self.sems.at[0, 4])


def scratch_shapes(sizes):
    width, hidden, windows, rows, peers = sizes.width, sizes.hidden, sizes.windows, sizes.rows, sizes.peers
    vmem = pltpu.VMEM
    dma = pltpu.SemaphoreType.DMA
    square = vmem((width, width), F32)
    shapes = {
        "eye": vmem((width, width), BF16),
        "self_qv_t": vmem((2 * width, width), BF16),
        "self_k_t": vmem((width, width), BF16),
        "self_merge_t": vmem((width, width), BF16),
        "self_qkv": vmem((width, 3 * width), BF16),
        "vectors": vmem((len(VECTORS), width, CHUNK), F32),
        "cross_q_t": vmem((width, width), BF16),
        "cross_k_t": vmem((width, width), BF16),
        "cross_v_t": vmem((width, width), BF16),
        "cross_merge_t": vmem((width, width), BF16),
        "cross_kv": vmem((width, 2 * width), BF16),
        "expand_t": vmem((hidden, 2 * width), BF16),
        "shrink_t": vmem((width, hidden), BF16),
        "g_sqkv": vmem((3 * width, width), F32),
        "g_cqkv": vmem((3 * width, width), F32),
        "g_sm": square,
        "g_cm": square,
        "g_we": vmem((hidden, 2 * width), F32),
        "g_ws": vmem((hidden, width), F32),
        "g_vec": vmem((len(VECTORS), width, CHUNK), F32),
        "q_t": vmem((width, rows), BF16),
        "k": vmem((WSLOT, width), BF16),
        "v_aug": vmem((width + ONES, WSLOT), BF16),
        "out_one": vmem((width, rows), BF16),
        "out_two": vmem((width, rows), BF16),
        "inverse_one": vmem((1, rows), F32),
        "inverse_two": vmem((1, rows), F32),
        "x1": vmem((width, rows), F32),
        "concat": vmem((2 * width, rows), BF16),
        "send": vmem((rows, width), BF16),
        "other": vmem((rows, width), BF16),
        "back": vmem((windows, width, WSLOT), BF16),
        "received": vmem((windows, width, WSLOT), BF16),
        "grad_normed": vmem((width, rows), F32),
        "exps": vmem((windows, WSLOT, WSLOT), BF16),
        "exps_two": vmem((windows, WSLOT, WSLOT), BF16),
        "diff": vmem((WSLOT, WSLOT), BF16),
        "act": vmem((3, hidden, SPAN), BF16),
        "slope": vmem((3, hidden, SPAN), BF16),
        "branch": vmem((3, width, SPAN), BF16),
        "hid": vmem((hidden, SPAN), BF16),
        "buf_a": vmem((max(WSLOT, hidden), SPAN), F32),
        "buf_b": vmem((WSLOT, SPAN), F32),
        "grad_merged": vmem((width, WSLOT), BF16),
        "k_t": vmem((width, WSLOT), BF16),
        "v": vmem((WSLOT, width), BF16),
        "up": vmem((width, WSLOT), BF16),
        "inner": vmem((1, WSLOT), F32),
        "dqkv": vmem((3 * width, WSLOT), BF16),
        "result_stage": vmem((rows, width), BF16),
        "grad_stage": vmem((2 * WSLOT, width), F32),
        "sem_x": dma((2, windows)),
        "sem_b": dma((2, windows)),
        "sem_result": dma((windows,)),
        "sem_grad": dma((windows,)),
    }
    for name, plan in sizes.plans.items():
        part = plan.shard + plan.extra
        shapes[name + "_pack"] = vmem((2, plan.owners, part, width), BF16)
        shapes[name + "_from_sibling"] = vmem((plan.owners, part, width), BF16)
        shapes[name + "_inbox"] = vmem((peers, part, width), BF16)
        shapes[name + "_total"] = vmem((2, plan.owners, plan.kept, width), BF16)
        shapes[name + "_sems"] = dma((2, 5))
    return shapes


def total_rows(total, shard, start, count):
    _, peers, _, width = total.shape
    at = start
    found = []
    while at < start + count:
        which, inside = divmod(at, peers * shard)
        index, offset = divmod(inside, shard)
        left = start + count - at
        if offset or left < shard:
            take = min(shard - offset, left)
            found.append(total[which, index, offset : offset + take])
        else:
            blocks = min(left // shard, peers - index)
            take = blocks * shard
            found.append(total[which, index : index + blocks, :shard].reshape(take, width))
        at += take
    return found[0] if len(found) == 1 else jnp.concatenate(found, axis=0)


def hand_out(sizes, *refs):
    result_in, grad_in, feed, cross, own, totals, result, grad = refs[:8]
    (o_sq, o_sk, o_sv, o_sm, o_sgain, o_sbias, o_cq, o_ck, o_cv, o_cm, o_cgain, o_cbias,
     o_we, o_ws, o_fgain, o_fbias) = refs[8:24]
    width, hidden = sizes.width, sizes.hidden
    shards = [plan.shard for plan in sizes.plans.values()]
    result[...] = result_in[...]
    grad[...] = grad_in[...]

    @pl.when(pl.program_id(0) == 0)
    def _():
        o_we[:width, :] = total_rows(feed, shards[0], 0, hidden).astype(F32).T
        o_we[width:, :] = total_rows(feed, shards[0], hidden, hidden).astype(F32).T
        o_ws[...] = total_rows(feed, shards[0], 2 * hidden, hidden).astype(F32)
        for source, shard, group in (
            (cross, shards[1], (o_cq, o_ck, o_cv, o_cm)), (own, shards[2], (o_sq, o_sk, o_sv, o_sm))
        ):
            for i, ref in enumerate(group):
                total = total_rows(source, shard, i * width, width).astype(F32)
                ref[...] = total if i == 3 else total.T
        for i, ref in enumerate((o_sgain, o_sbias, o_cgain, o_cbias, o_fgain, o_fbias)):
            ref[...] = totals[i : i + 1, :]


def local(features, cotangent, slot_pair, crop_size, *weights):
    rows, width = features.shape[1:]
    hidden = weights[12].shape[1]
    peers = lax.axis_size("pix")

    def plan(count, extra=0):
        shard = -(-count // (2 * peers * 16)) * 16
        owners = min(peers, -(-count // (2 * shard)))
        kept = shard + (extra if owners < peers else 0)
        return types.SimpleNamespace(peers=peers, owners=owners, shard=shard, extra=extra, kept=kept)

    sizes = types.SimpleNamespace(
        rows=rows, width=width, hidden=hidden, windows=rows // WSLOT, peers=peers,
        scale=1.0 / math.sqrt(2.0 * rows * peers),
        plans={"feed": plan(3 * hidden), "cross": plan(4 * width), "self": plan(4 * width, 16)},
    )
    flat = lambda value: value.reshape(1, -1) if value.ndim == 1 else value
    shape = jax.ShapeDtypeStruct
    small = pl.BlockSpec(memory_space=pltpu.VMEM)
    large = pl.BlockSpec(memory_space=pl.ANY)
    scalar = pl.BlockSpec(memory_space=pltpu.SMEM)
    square = shape((width, width), F32)
    row = shape((1, width), F32)
    big = [shape((rows, width), BF16), shape((rows, width), F32)]
    middle = pl.pallas_call(
        functools.partial(layer_kernel, sizes),
        in_specs=[small, small, scalar, scalar] + [small] * 16,
        out_specs=[large] * 5 + [small],
        out_shape=big + [
            shape((2, plan.owners, plan.kept, width), BF16) for plan in sizes.plans.values()
        ] + [shape((16, width), F32)],
        scratch_shapes=list(scratch_shapes(sizes).values()),
        compiler_params=pltpu.CompilerParams(
            collective_id=0, has_side_effects=True, vmem_limit_bytes=63 * 2**20
        ),
        name="layer",
    )(features[0], cotangent[0], slot_pair, crop_size.T, *[flat(weight) for weight in weights])
    moved = [pl.BlockSpec((WSLOT, width), lambda w: (w, 0))] * 2
    whole = lambda shape: pl.BlockSpec(shape, lambda w: (0,) * len(shape))
    smalls = [
        square, square, square, square, row, row, square, square, square, square, row, row,
        shape((2 * width, hidden), F32), shape((hidden, width), F32), row, row,
    ]
    outs = pl.pallas_call(
        functools.partial(hand_out, sizes),
        grid=(sizes.windows,),
        in_specs=moved + [whole(value.shape) for value in middle[2:]],
        out_specs=moved + [whole(value.shape) for value in smalls],
        out_shape=big + smalls,
        compiler_params=pltpu.CompilerParams(vmem_limit_bytes=60 * 2**20),
        name="hand_out",
    )(*middle)
    result, grad = outs[:2]
    return (result[None], grad[None]) + tuple(
        out.reshape(-1) if out.shape[0] == 1 else out for out in outs[2:]
    )


def solution(mesh):
    split = P("frame", "pix", None)
    return jax.shard_map(
        local,
        mesh=mesh,
        in_specs=(split, split, P("pix")) + (P(),) * 17,
        out_specs=(split, split) + (P(),) * 16,
        check_vma=False,
    )
```

```python
import functools
import math
import types

import jax
import jax.numpy as jnp
from jax import lax
from jax.experimental import pallas as pl
from jax.experimental.pallas import tpu as pltpu
from jax.sharding import PartitionSpec as P

WSLOT = 1152
FEWEST = 704
NEGATIVE = -1e30
EPSILON = 1e-05
LOG2E = 1.4426950408889634
F32 = jnp.float32
BF16 = jnp.bfloat16
MESH = pl.DeviceIdType.MESH
TAIL_SHIFT = 2.7777777777777777
TAIL_POLY = (0.39765776262463953, 1.1594294101832299, 1.9333185594349698, 10.032517622923805, -5.2492700447308085, -9.371923274701059)
SPAN = 256
CHUNK = 128
TILES = ((0, 256), (256, 256), (512, 256), (768, 256), (1024, 128))
ONES = 16


def nn(left, right):
    return jnp.dot(left, right, preferred_element_type=F32)


def nt(left, right):
    return lax.dot_general(left, right, (((1,), (1,)), ((), ())), preferred_element_type=F32)


def norm_stats(values):
    centre = jnp.mean(values, axis=0, keepdims=True)
    shifted = values - centre
    spread = jnp.mean(shifted * shifted, axis=0, keepdims=True)
    inverse = lax.rsqrt(spread + EPSILON)
    return shifted * inverse, inverse


def norm_back(hat, inverse, gain, upstream):
    scaled = upstream * gain
    first = jnp.mean(scaled, axis=0, keepdims=True)
    second = jnp.mean(scaled * hat, axis=0, keepdims=True)
    return inverse * (scaled - first - hat * second)


def gelu_both(values):
    bell = jnp.exp2(values * (values * (-0.5 * LOG2E))).astype(BF16)
    t = (1.0 / (jnp.abs(values) + TAIL_SHIFT)).astype(BF16)
    low = values.astype(BF16)
    poly = t * BF16(TAIL_POLY[-1]) + BF16(TAIL_POLY[-2])
    for coefficient in TAIL_POLY[-3::-1]:
        poly = poly * t + BF16(coefficient)
    tail = poly * t * bell
    phi = jnp.where(low >= BF16(0.0), BF16(1.0) - tail, tail)
    return low * phi, phi + low * bell * BF16(1.0 / math.sqrt(2.0 * math.pi))


def flip(values):
    return values.astype(F32).T.astype(BF16)


INPUTS = (
    "x", "cot", "slot", "crop", "sq", "sk", "sv", "sm", "sgain", "sbias",
    "cq", "ck", "cv", "cm", "cgain", "cbias", "we", "ws", "fgain", "fbias",
)
OUTPUTS = ("result", "grad", "early_out", "late_out", "totals")
VECTORS = ("sgain", "sbias", "cgain", "cbias", "fgain", "fbias")


def layer_kernel(sizes, *refs):
    names = INPUTS + OUTPUTS + tuple(scratch_shapes(sizes))
    r = types.SimpleNamespace(**dict(zip(names, refs, strict=True)))
    width, hidden, windows, peers = sizes.width, sizes.hidden, sizes.windows, sizes.peers
    factor = 1.0 / math.sqrt(width)
    scale = factor * LOG2E
    frame = lax.axis_index("frame")
    pix = lax.axis_index("pix")
    core = lax.rem(pix, 2)
    me = frame * (peers // 2) + lax.div(pix, 2)
    partner = (1 - frame, pix)
    sibling = (frame, pix + 1 - 2 * core)

    def peer(step):
        index = lax.rem(me + step, peers)
        return index, (lax.div(index, peers // 2), lax.rem(index, peers // 2) * 2 + core)

    barrier = pltpu.get_barrier_semaphore()
    pl.semaphore_signal(barrier, inc=1, device_id=sibling, device_id_type=MESH)

    def greet(step, carry):
        pl.semaphore_signal(barrier, inc=1, device_id=peer(step)[1], device_id_type=MESH)
        return carry

    lax.fori_loop(1, peers, greet, 0)

    slot = r.slot[0]
    live = lax.shift_right_logical(r.crop[0, slot], 1) * lax.shift_right_logical(r.crop[1, slot], 1)

    r.eye[...] = jnp.where(
        lax.broadcasted_iota(jnp.int32, (width, width), 0)
        == lax.broadcasted_iota(jnp.int32, (width, width), 1),
        1.0, 0.0,
    ).astype(BF16)
    r.self_qv_t[:width] = flip(r.sq[...])
    r.self_qv_t[width:] = flip(r.sv[...])
    r.self_k_t[...] = flip(r.sk[...])
    r.self_merge_t[...] = flip(r.sm[...])
    r.self_qkv[:, :width] = r.sq[...]
    r.self_qkv[:, width : 2 * width] = r.sk[...]
    r.self_qkv[:, 2 * width :] = r.sv[...]
    for i, name in enumerate(VECTORS):
        r.vectors[i] = jnp.broadcast_to(getattr(r, name)[...], (width, CHUNK)).T
    vector = lambda name: r.vectors[VECTORS.index(name)]
    for name in ("g_sqkv", "g_sm", "g_cqkv", "g_cm", "g_we", "g_ws", "g_vec"):
        getattr(r, name)[...] = jnp.zeros_like(getattr(r, name))
    r.v_aug[width:, :] = jnp.ones((ONES, WSLOT), BF16)

    def alive_at(start, size):
        token = lax.broadcasted_iota(jnp.int32, (1, size), 1) + lax.rem(start, WSLOT)
        return jnp.where(token < live, 1.0, 0.0)

    def rows_at(w):
        return pl.ds(pl.multiple_of(w * WSLOT, WSLOT), WSLOT)

    def cols_at(w, start=0, size=WSLOT):
        return pl.ds(pl.multiple_of(w * WSLOT + start, 128), size)

    def send_rows(w):
        return pltpu.make_async_remote_copy(
            src_ref=r.send.at[rows_at(w), :], dst_ref=r.other.at[rows_at(w), :],
            send_sem=r.sem_x.at[0, w], recv_sem=r.sem_x.at[1, w], device_id=partner, device_id_type=MESH,
        )

    def send_back(w):
        return pltpu.make_async_remote_copy(
            src_ref=r.back.at[w], dst_ref=r.received.at[w],
            send_sem=r.sem_b.at[0, w], recv_sem=r.sem_b.at[1, w], device_id=partner, device_id_type=MESH,
        )

    def store_rows(target, stage, w, sem):
        return pltpu.make_async_copy(stage.at[rows_at(w), :], target.at[rows_at(w), :], sem.at[w])

    def attend(w, exps, out, inverse):
        bufs = (r.buf_a, r.buf_b)

        def score(t):
            first, size = TILES[t]
            got = nn(r.k[...], r.q_t[:, cols_at(w, first, size)])
            rest = got[FEWEST:]
            row = lax.broadcasted_iota(jnp.int32, rest.shape, 0) + FEWEST
            rest = jnp.where(row < live, rest, NEGATIVE)
            bufs[t % 2][:FEWEST, :size] = got[:FEWEST]
            bufs[t % 2][FEWEST:, :size] = rest
            return scale * jnp.maximum(
                jnp.max(got[:FEWEST], axis=0, keepdims=True), jnp.max(rest, axis=0, keepdims=True)
            )

        def output_part(t, rows, total):
            first, size = TILES[t]
            part = nn(r.v_aug[:, rows], exps[rows, first : first + size])
            return part if total is None else total + part

        def output(t, both):
            first, size = TILES[t]
            share = 1.0 / both[width : width + 1]
            inverse[:, cols_at(w, first, size)] = share
            out[:, cols_at(w, first, size)] = (both[:width] * share).astype(BF16)

        top = score(0)
        for t, (first, size) in enumerate(TILES):
            after = score(t + 1) if t + 1 < len(TILES) else None
            total = None
            for start, count in TILES:
                rows = slice(start, start + count)
                if t:
                    total = output_part(t - 1, rows, total)
                exps[rows, first : first + size] = jnp.exp2(
                    bufs[t % 2][rows, :size] * scale - top
                ).astype(BF16)
            if t:
                output(t - 1, total)
            top = after
        last = len(TILES) - 1
        output(last, output_part(last, slice(0, WSLOT), None))

    def attend_back(w, exps, dqkv):
        def query(t):
            first, size = TILES[t]
            cols = slice(first, first + size)
            dqkv[:width, cols] = (nn(r.k_t[...], r.diff[:, cols]) * factor).astype(BF16)

        for t, (first, size) in enumerate(TILES):
            cols = slice(first, first + size)
            grad = nn(r.v[...], r.up[:, cols]) - r.inner[:, cols]
            r.diff[:, cols] = exps[:, cols] * grad.astype(BF16)
            if t:
                query(t - 1)
        grad_value = nt(exps[...], r.up[...])
        query(len(TILES) - 1)
        grad_key = nt(r.diff[...], r.q_t[:, cols_at(w)]) * factor
        dqkv[2 * width :, :] = grad_value.T.astype(BF16)
        dqkv[width : 2 * width, :] = grad_key.T.astype(BF16)

    def forward_self(w, carry):
        x = r.x[rows_at(w), :]
        stacked = nt(r.self_qv_t[...], x).astype(BF16)
        r.q_t[:, cols_at(w)] = stacked[:width]
        r.v_aug[:width, :] = stacked[width:]
        r.k[...] = nn(x, r.sk[...]).astype(BF16)
        attend(w, r.exps.at[w], r.out_one, r.inverse_one)
        merged = nn(r.self_merge_t[...], r.out_one[:, cols_at(w)])
        x_t = nt(r.eye[...], r.x[rows_at(w), :])
        for start in range(0, WSLOT, CHUNK):
            cols = slice(start, start + CHUNK)
            hat, _ = norm_stats(merged[:, cols])
            x1 = x_t[:, cols] + hat * vector("sgain") + vector("sbias")
            r.x1[:, cols_at(w, start, CHUNK)] = x1
            r.concat[:width, cols_at(w, start, CHUNK)] = x1.astype(BF16)
            r.send[pl.ds(pl.multiple_of(w * WSLOT + start, CHUNK), CHUNK), :] = x1.T.astype(BF16)

        @pl.when(w == 0)
        def _():
            pl.semaphore_wait(barrier, peers)

        send_rows(w).start()
        return carry

    lax.fori_loop(0, windows, forward_self, 0)

    r.cross_q_t[...] = flip(r.cq[...])
    r.cross_k_t[...] = flip(r.ck[...])
    r.cross_v_t[...] = flip(r.cv[...])
    r.cross_merge_t[...] = flip(r.cm[...])
    r.cross_kv[:, :width] = r.ck[...]
    r.cross_kv[:, width:] = r.cv[...]
    r.expand_t[...] = flip(r.we[...])
    r.shrink_t[...] = flip(r.ws[...])

    def forward_cross(w):
        r.q_t[:, cols_at(w)] = nn(r.cross_q_t[...], r.concat[:width, cols_at(w)]).astype(BF16)
        send_rows(w).wait()
        other = r.other[rows_at(w), :]
        r.v_aug[:width, :] = nt(r.cross_v_t[...], other).astype(BF16)
        r.k[...] = nn(other, r.ck[...]).astype(BF16)
        attend(w, r.exps_two.at[lax.rem(w, 2)], r.out_two, r.inverse_two)
        merged = nn(r.cross_merge_t[...], r.out_two[:, cols_at(w)])
        for start in range(0, WSLOT, CHUNK):
            hat, _ = norm_stats(merged[:, start : start + CHUNK])
            r.concat[width:, cols_at(w, start, CHUNK)] = (
                hat * vector("cgain") + vector("cbias")
            ).astype(BF16)

    spans = sizes.rows // SPAN

    def span(i):
        return pl.ds(pl.multiple_of(i * SPAN, SPAN), SPAN)

    def norm_tile(i, b, branch, up_all, start):
        part = slice(start, start + CHUNK)
        here = pl.ds(pl.multiple_of(i * SPAN + start, CHUNK), CHUNK)
        alive = alive_at(i * SPAN + start, CHUNK)
        hat, inverse = norm_stats(branch[:, part])
        result = (r.x1[:, here] + hat * vector("fgain") + vector("fbias")) * alive
        r.result_stage[here, :] = result.T.astype(BF16)
        up = up_all[:, part] * alive
        r.x1[:, here] = up
        r.g_vec[4] += up * hat
        r.g_vec[5] += up
        r.branch[b, :, part] = norm_back(hat, inverse, vector("fgain"), up).astype(BF16)

    def settle(i, total):
        r.x1[:, span(i)] += total[:width]
        r.grad_normed[:, span(i)] = total[width:]

    parts = [slice(start, start + SPAN) for start in range(0, hidden, SPAN)]

    def expand(i):
        r.buf_a[:hidden, :] = nn(r.expand_t[...], r.concat[:, span(i)])

    def activate(b, rows):
        act, slope = gelu_both(r.buf_a[rows, :])
        r.act[b, rows, :] = act
        r.slope[b, rows, :] = slope

    def hide(b):
        r.hid[...] = r.slope[b] * nn(r.ws[...], r.branch[b]).astype(BF16)

    def add(total, part):
        return part if total is None else total + part

    per_half = 2 * WSLOT // SPAN

    def feed_forward(half):
        first = per_half * half
        for name in ("act", "slope", "branch"):
            getattr(r, name)[2] = jnp.zeros(getattr(r, name).shape[1:], BF16)
        expand(first)
        for rows in parts:
            activate(0, rows)

        def feed(j, carry):
            for b in range(3):
                i = first + 3 * j + b
                old = (b + 2) % 3
                before = jnp.maximum(i - 1, first)
                expand(jnp.minimum(i + 1, spans - 1))
                hide(old)
                branch, total = None, None
                for rows in parts:
                    branch = add(branch, nn(r.shrink_t[:, rows], r.act[b, rows, :]))
                    total = add(total, nn(r.we[:, rows], r.hid[rows, :]))
                    activate((b + 1) % 3, rows)
                settle(before, total)
                up_all = nt(r.eye[...], r.cot[span(i), :])
                for_shrink = nt(r.act[old], r.branch[old])
                norm_tile(i, b, branch, up_all, 0)
                for_expand = nt(r.hid[...], r.concat[:, span(before)])
                norm_tile(i, b, branch, up_all, CHUNK)
                r.g_ws[...] += for_shrink
                r.g_we[...] += for_expand
            return carry

        lax.fori_loop(0, per_half // 3, feed, 0)
        end = first + per_half - 1
        last = (per_half - 1) % 3
        hide(last)
        settle(end, nn(r.we[...], r.hid[...]))
        r.g_ws[...] += nt(r.act[last], r.branch[last])
        r.g_we[...] += nt(r.hid[...], r.concat[:, span(end)])

    def upstream(w, merged, grad_at, number, gain, out, gradient, merge, inverse):
        sums = [jnp.zeros((width, CHUNK), F32)] * 2
        for start in range(0, WSLOT, CHUNK):
            hat, root = norm_stats(merged[:, start : start + CHUNK])
            grad = grad_at(start)
            sums = [sums[0] + grad * hat, sums[1] + grad]
            r.grad_merged[:, start : start + CHUNK] = norm_back(hat, root, vector(gain), grad).astype(BF16)
        r.g_vec[number] += sums[0]
        r.g_vec[number + 1] += sums[1]
        out = out[:, cols_at(w)]
        gradient[...] += nt(out, r.grad_merged[...])
        up = (nn(merge[...], r.grad_merged[...]) * inverse[:, cols_at(w)]).astype(BF16)
        r.up[...] = up
        r.inner[...] = jnp.sum(up.astype(F32) * out.astype(F32), axis=0, keepdims=True)

    def backward_cross(w):
        exps = r.exps_two.at[lax.rem(w, 2)]
        dqkv = r.dqkv.at[w]
        upstream(
            w, nn(r.cross_merge_t[...], r.out_two[:, cols_at(w)]),
            lambda start: r.grad_normed[:, cols_at(w, start, CHUNK)],
            2, "cgain", r.out_two, r.g_cm, r.cm, r.inverse_two,
        )
        other = r.other[rows_at(w), :]
        r.k_t[...] = nt(r.cross_k_t[...], other).astype(BF16)
        r.v[...] = nn(other, r.cv[...]).astype(BF16)
        attend_back(w, exps, dqkv)
        r.back[w] = nn(r.cross_kv[...], dqkv[width:, :]).astype(BF16)
        send_back(w).start()
        r.g_cqkv[:width] += nt(dqkv[:width, :], r.concat[:width, cols_at(w)])
        r.g_cqkv[width:] += nn(dqkv[width:, :], r.other[rows_at(w), :])
        r.x1[:, cols_at(w)] += nn(r.cq[...], dqkv[:width, :])

    def middle(half, carry):
        def before(u, carry):
            forward_cross(2 * half + u)
            return carry

        lax.fori_loop(0, 2, before, 0)
        feed_forward(half)

        def after(u, carry):
            store_rows(r.result, r.result_stage, 2 * half + u, r.sem_result).start()
            backward_cross(2 * half + u)
            return carry

        lax.fori_loop(0, 2, after, 0)
        return carry

    lax.fori_loop(0, windows // 2, middle, 0)

    early = Reduction(r, sizes.plans["early"], "early", sizes.scale, sibling, peer, core, me)
    late = Reduction(r, sizes.plans["late"], "late", sizes.scale, sibling, peer, core, me)
    early.begin(
        [r.g_we.at[:, pl.ds(0, width)], r.g_we.at[:, pl.ds(width, width)], r.g_ws, r.g_cqkv, r.g_cm]
    )

    def backward_self(w, carry):
        @pl.when(w == 1)
        def _():
            early.scatter()

        @pl.when(w == windows - 1)
        def _():
            early.gather()

        exps = r.exps.at[w]
        dqkv = r.dqkv.at[w]
        x = r.x[rows_at(w), :]
        r.q_t[:, cols_at(w)] = nt(r.self_qv_t[:width, :], x).astype(BF16)
        r.k_t[...] = nt(r.self_k_t[...], x).astype(BF16)
        r.v[...] = nn(x, r.sv[...]).astype(BF16)
        send_back(w).wait()

        def grad_at(start):
            here = cols_at(w, start, CHUNK)
            grad = r.x1[:, here] + r.received[w, :, start : start + CHUNK].astype(F32)
            r.x1[:, here] = grad
            return grad

        upstream(
            w, nn(r.self_merge_t[...], r.out_one[:, cols_at(w)]), grad_at,
            0, "sgain", r.out_one, r.g_sm, r.sm, r.inverse_one,
        )
        attend_back(w, exps, dqkv)
        r.g_sqkv[...] += nn(dqkv[...], r.x[rows_at(w), :])
        return carry

    lax.fori_loop(0, windows, backward_self, 0)

    def finish(w):
        place = w % 2
        stage = r.grad_stage.at[pl.ds(place * WSLOT, WSLOT), :]
        if w >= 2:
            store_grad(w - 2).wait()
        stage[...] = (r.x1[:, cols_at(w)] + nn(r.self_qkv[...], r.dqkv[w])).T
        store_grad(w).start()

    def store_grad(w):
        place = w % 2
        return pltpu.make_async_copy(
            r.grad_stage.at[pl.ds(place * WSLOT, WSLOT), :], r.grad.at[pl.ds(w * WSLOT, WSLOT), :],
            r.sem_grad.at[w],
        )

    late.begin([r.g_sqkv, r.g_sm], r.g_vec)
    early.share()
    finish(0)
    late.scatter()
    early.finish()
    early.store(r.early_out).start()
    finish(1)
    late.gather()
    if late.full:
        r.totals[...] = late.vector_total()
    finish(2)
    late.share()
    finish(3)
    late.finish()
    late.store(r.late_out).start()
    if not late.full:
        r.totals[...] = late.total[0, 0, late.shard :].astype(F32)

    def drain(w, carry):
        store_rows(r.result, r.result_stage, w, r.sem_result).wait()
        return carry

    lax.fori_loop(0, windows, drain, 0)
    store_grad(2).wait()
    store_grad(3).wait()
    early.store(r.early_out).wait()
    late.store(r.late_out).wait()


class Reduction:
    def __init__(self, r, plan, name, scale, sibling, peer, core, me):
        self.sibling, self.peer, self.core, self.me = sibling, peer, core, me
        self.scale = scale
        self.peers, self.owners, self.shard, self.extra, self.kept = (
            plan.peers, plan.owners, plan.shard, plan.extra, plan.kept
        )
        self.half = self.owners * self.shard
        self.full = self.owners == self.peers
        for field in ("pack", "from_sibling", "inbox", "total", "sems"):
            setattr(self, field, getattr(r, name + "_" + field))

    def copy(self, source, target, number, device):
        return pltpu.make_async_remote_copy(
            src_ref=source, dst_ref=target, send_sem=self.sems.at[0, number],
            recv_sem=self.sems.at[1, number], device_id=device, device_id_type=MESH,
        )

    def owning(self, then, otherwise=None):
        if self.full:
            then()
        else:
            pl.when(self.me < self.owners)(then)
            if otherwise is not None:
                pl.when(self.me >= self.owners)(otherwise)

    def halves(self):
        return self.copy(self.pack.at[1 - self.core], self.from_sibling, 0, self.sibling)

    def begin(self, pieces, vec=None):
        at = 0
        width = self.pack.shape[3]
        for piece in pieces:
            taken = 0
            while taken < piece.shape[0]:
                which, inside = divmod(at, self.half)
                index, offset = divmod(inside, self.shard)
                left = piece.shape[0] - taken
                if offset or left < self.shard:
                    count = min(left, self.shard - offset)
                    self.pack[which, index, offset : offset + count] = piece[
                        taken : taken + count, :
                    ].astype(BF16)
                else:
                    blocks = min(left // self.shard, self.owners - index)
                    count = blocks * self.shard
                    self.pack[which, index : index + blocks, : self.shard] = (
                        piece[taken : taken + count, :].astype(BF16).reshape(blocks, self.shard, width)
                    )
                at += count
                taken += count
        while at < 2 * self.half:
            which, inside = divmod(at, self.half)
            index, offset = divmod(inside, self.shard)
            count = self.shard - offset
            self.pack[which, index, offset : self.shard] = jnp.zeros((count, width), BF16)
            at += count
        if self.extra:
            sums = jnp.concatenate([jnp.sum(vec[i].T, axis=0, keepdims=True) for i in range(vec.shape[0])])
            rows = jnp.concatenate([sums, jnp.zeros((self.extra - vec.shape[0], width), F32)]).astype(BF16)
            for which in range(2):
                self.pack[which, :, self.shard :] = jnp.broadcast_to(
                    rows[None], (self.owners, self.extra, width)
                )
        self.halves().start()

    def wait(self, number, sent, received):
        if sent is not None:
            self.copy(sent, sent, number, self.sibling).wait_send()
        if received is not None:
            self.copy(received, received, number, self.sibling).wait_recv()

    def scatter(self):
        self.halves().wait()
        mine = self.pack[self.core].astype(F32) + self.from_sibling[...].astype(F32)
        self.pack[self.core] = mine.astype(BF16)

        def send(step, carry):
            index, device = self.peer(step)

            def go():
                place = self.pack.at[self.core, index]
                self.copy(place, self.inbox.at[self.me], 1, device).start()

            go() if self.full else pl.when(index < self.owners)(go)
            return carry

        lax.fori_loop(1, self.peers, send, 0)

        def own():
            self.inbox[self.me] = self.pack[self.core, self.me]

        self.owning(own)

    def gather(self):
        def own():
            self.wait(
                1, self.pack.at[0, pl.ds(0, self.owners - 1)], self.inbox.at[pl.ds(0, self.peers - 1)]
            )
            total = jnp.sum(self.inbox[:, : self.kept].astype(F32), axis=0) * self.scale
            self.total[self.core, self.me] = total.astype(BF16)

            def send(step, carry):
                place = self.total.at[self.core, self.me]
                self.copy(place, place, 2, self.peer(step)[1]).start()
                return carry

            lax.fori_loop(1, self.peers, send, 0)

        self.owning(own, lambda: self.wait(1, self.pack.at[0], None))

    def vector_total(self):
        return jnp.sum(self.inbox[:, self.shard :].astype(F32), axis=0) * self.scale

    def share(self):
        def own():
            for count in (self.owners - 1,) * ((self.peers - 1) // (self.owners - 1)) + (
                (self.peers - 1) % (self.owners - 1),
            ):
                if count:
                    self.wait(2, self.total.at[0, pl.ds(0, count)], None)
            self.wait(2, None, self.total.at[0, pl.ds(0, self.owners - 1)])

        self.owning(own, lambda: self.wait(2, None, self.total.at[0]))
        self.copy(self.total.at[self.core], self.total.at[self.core], 3, self.sibling).start()

    def finish(self):
        self.copy(self.total.at[self.core], self.total.at[self.core], 3, self.sibling).wait()

    def store(self, target):
        return pltpu.make_async_copy(self.total, target, self.sems.at[0, 4])


def scratch_shapes(sizes):
    width, hidden, windows, rows, peers = sizes.width, sizes.hidden, sizes.windows, sizes.rows, sizes.peers
    vmem = pltpu.VMEM
    dma = pltpu.SemaphoreType.DMA
    square = vmem((width, width), F32)
    shapes = {
        "eye": vmem((width, width), BF16),
        "self_qv_t": vmem((2 * width, width), BF16),
        "self_k_t": vmem((width, width), BF16),
        "self_merge_t": vmem((width, width), BF16),
        "self_qkv": vmem((width, 3 * width), BF16),
        "vectors": vmem((len(VECTORS), width, CHUNK), F32),
        "cross_q_t": vmem((width, width), BF16),
        "cross_k_t": vmem((width, width), BF16),
        "cross_v_t": vmem((width, width), BF16),
        "cross_merge_t": vmem((width, width), BF16),
        "cross_kv": vmem((width, 2 * width), BF16),
        "expand_t": vmem((hidden, 2 * width), BF16),
        "shrink_t": vmem((width, hidden), BF16),
        "g_sqkv": vmem((3 * width, width), F32),
        "g_cqkv": vmem((3 * width, width), F32),
        "g_sm": square,
        "g_cm": square,
        "g_we": vmem((hidden, 2 * width), F32),
        "g_ws": vmem((hidden, width), F32),
        "g_vec": vmem((len(VECTORS), width, CHUNK), F32),
        "q_t": vmem((width, rows), BF16),
        "k": vmem((WSLOT, width), BF16),
        "v_aug": vmem((width + ONES, WSLOT), BF16),
        "out_one": vmem((width, rows), BF16),
        "out_two": vmem((width, rows), BF16),
        "inverse_one": vmem((1, rows), F32),
        "inverse_two": vmem((1, rows), F32),
        "x1": vmem((width, rows), F32),
        "concat": vmem((2 * width, rows), BF16),
        "send": vmem((rows, width), BF16),
        "other": vmem((rows, width), BF16),
        "back": vmem((windows, width, WSLOT), BF16),
        "received": vmem((windows, width, WSLOT), BF16),
        "grad_normed": vmem((width, rows), F32),
        "exps": vmem((windows, WSLOT, WSLOT), BF16),
        "exps_two": vmem((2, WSLOT, WSLOT), BF16),
        "diff": vmem((WSLOT, WSLOT), BF16),
        "act": vmem((3, hidden, SPAN), BF16),
        "slope": vmem((3, hidden, SPAN), BF16),
        "branch": vmem((3, width, SPAN), BF16),
        "hid": vmem((hidden, SPAN), BF16),
        "buf_a": vmem((max(WSLOT, hidden), SPAN), F32),
        "buf_b": vmem((WSLOT, SPAN), F32),
        "grad_merged": vmem((width, WSLOT), BF16),
        "k_t": vmem((width, WSLOT), BF16),
        "v": vmem((WSLOT, width), BF16),
        "up": vmem((width, WSLOT), BF16),
        "inner": vmem((1, WSLOT), F32),
        "dqkv": vmem((windows, 3 * width, WSLOT), BF16),
        "result_stage": vmem((rows, width), BF16),
        "grad_stage": vmem((2 * WSLOT, width), F32),
        "sem_x": dma((2, windows)),
        "sem_b": dma((2, windows)),
        "sem_result": dma((windows,)),
        "sem_grad": dma((windows,)),
    }
    for name, plan in sizes.plans.items():
        part = plan.shard + plan.extra
        shapes[name + "_pack"] = vmem((2, plan.owners, part, width), BF16)
        shapes[name + "_from_sibling"] = vmem((plan.owners, part, width), BF16)
        shapes[name + "_inbox"] = vmem((peers, part, width), BF16)
        shapes[name + "_total"] = vmem((2, plan.owners, plan.kept, width), BF16)
        shapes[name + "_sems"] = dma((2, 5))
    return shapes


def total_rows(total, shard, start, count):
    _, peers, _, width = total.shape
    at = start
    found = []
    while at < start + count:
        which, inside = divmod(at, peers * shard)
        index, offset = divmod(inside, shard)
        left = start + count - at
        if offset or left < shard:
            take = min(shard - offset, left)
            found.append(total[which, index, offset : offset + take])
        else:
            blocks = min(left // shard, peers - index)
            take = blocks * shard
            found.append(total[which, index : index + blocks, :shard].reshape(take, width))
        at += take
    return found[0] if len(found) == 1 else jnp.concatenate(found, axis=0)


def hand_out(sizes, *refs):
    result_in, grad_in, early, late, totals, result, grad = refs[:7]
    (o_sq, o_sk, o_sv, o_sm, o_sgain, o_sbias, o_cq, o_ck, o_cv, o_cm, o_cgain, o_cbias,
     o_we, o_ws, o_fgain, o_fbias) = refs[7:23]
    width, hidden = sizes.width, sizes.hidden
    shards = [plan.shard for plan in sizes.plans.values()]
    result[...] = result_in[...]
    grad[...] = grad_in[...]

    @pl.when(pl.program_id(0) == 0)
    def _():
        o_we[:width, :] = total_rows(early, shards[0], 0, hidden).astype(F32).T
        o_we[width:, :] = total_rows(early, shards[0], hidden, hidden).astype(F32).T
        o_ws[...] = total_rows(early, shards[0], 2 * hidden, hidden).astype(F32)
        for source, shard, base, group in (
            (early, shards[0], 3 * hidden, (o_cq, o_ck, o_cv, o_cm)), (late, shards[1], 0, (o_sq, o_sk, o_sv, o_sm))
        ):
            for i, ref in enumerate(group):
                total = total_rows(source, shard, base + i * width, width).astype(F32)
                ref[...] = total if i == 3 else total.T
        for i, ref in enumerate((o_sgain, o_sbias, o_cgain, o_cbias, o_fgain, o_fbias)):
            ref[...] = totals[i : i + 1, :]


def local(features, cotangent, slot_pair, crop_size, *weights):
    rows, width = features.shape[1:]
    hidden = weights[12].shape[1]
    peers = lax.axis_size("pix")

    def plan(count, extra=0):
        shard = -(-count // (2 * peers * 16)) * 16
        owners = min(peers, -(-count // (2 * shard)))
        kept = shard + (extra if owners < peers else 0)
        return types.SimpleNamespace(peers=peers, owners=owners, shard=shard, extra=extra, kept=kept)

    sizes = types.SimpleNamespace(
        rows=rows, width=width, hidden=hidden, windows=rows // WSLOT, peers=peers,
        scale=1.0 / math.sqrt(2.0 * rows * peers),
        plans={"early": plan(3 * hidden + 4 * width), "late": plan(4 * width, 16)},
    )
    flat = lambda value: value.reshape(1, -1) if value.ndim == 1 else value
    shape = jax.ShapeDtypeStruct
    small = pl.BlockSpec(memory_space=pltpu.VMEM)
    large = pl.BlockSpec(memory_space=pl.ANY)
    scalar = pl.BlockSpec(memory_space=pltpu.SMEM)
    square = shape((width, width), F32)
    row = shape((1, width), F32)
    big = [shape((rows, width), BF16), shape((rows, width), F32)]
    middle = pl.pallas_call(
        functools.partial(layer_kernel, sizes),
        in_specs=[small, small, scalar, scalar] + [small] * 16,
        out_specs=[large] * 4 + [small],
        out_shape=big + [
            shape((2, plan.owners, plan.kept, width), BF16) for plan in sizes.plans.values()
        ] + [shape((16, width), F32)],
        scratch_shapes=list(scratch_shapes(sizes).values()),
        compiler_params=pltpu.CompilerParams(
            collective_id=0, has_side_effects=True, vmem_limit_bytes=63 * 2**20
        ),
        name="layer",
    )(features[0], cotangent[0], slot_pair, crop_size.T, *[flat(weight) for weight in weights])
    moved = [pl.BlockSpec((WSLOT, width), lambda w: (w, 0))] * 2
    whole = lambda shape: pl.BlockSpec(shape, lambda w: (0,) * len(shape))
    smalls = [
        square, square, square, square, row, row, square, square, square, square, row, row,
        shape((2 * width, hidden), F32), shape((hidden, width), F32), row, row,
    ]
    outs = pl.pallas_call(
        functools.partial(hand_out, sizes),
        grid=(sizes.windows,),
        in_specs=moved + [whole(value.shape) for value in middle[2:]],
        out_specs=moved + [whole(value.shape) for value in smalls],
        out_shape=big + smalls,
        compiler_params=pltpu.CompilerParams(vmem_limit_bytes=60 * 2**20),
        name="hand_out",
    )(*middle)
    result, grad = outs[:2]
    return (result[None], grad[None]) + tuple(
        out.reshape(-1) if out.shape[0] == 1 else out for out in outs[2:]
    )


def solution(mesh):
    split = P("frame", "pix", None)
    return jax.shard_map(
        local,
        mesh=mesh,
        in_specs=(split, split, P("pix")) + (P(),) * 17,
        out_specs=(split, split) + (P(),) * 16,
        check_vma=False,
    )
```

```python
import functools
import math
import types

import jax
import jax.numpy as jnp
from jax import lax
from jax.experimental import pallas as pl
from jax.experimental.pallas import tpu as pltpu
from jax.sharding import PartitionSpec as P

WSLOT = 1152
FEWEST = 704
NEGATIVE = -1e30
EPSILON = 1e-05
LOG2E = 1.4426950408889634
F32 = jnp.float32
BF16 = jnp.bfloat16
MESH = pl.DeviceIdType.MESH
TAIL_SHIFT = 2.7777777777777777
TAIL_POLY = (0.39765776262463953, 1.1594294101832299, 1.9333185594349698, 10.032517622923805, -5.2492700447308085, -9.371923274701059)
SPAN = 256
CHUNK = 128
TILES = ((0, 256), (256, 256), (512, 256), (768, 256), (1024, 128))
ONES = 16


def nn(left, right):
    return jnp.dot(left, right, preferred_element_type=F32)


def nt(left, right):
    return lax.dot_general(left, right, (((1,), (1,)), ((), ())), preferred_element_type=F32)


def norm_stats(values):
    centre = jnp.mean(values, axis=0, keepdims=True)
    shifted = values - centre
    spread = jnp.mean(shifted * shifted, axis=0, keepdims=True)
    inverse = lax.rsqrt(spread + EPSILON)
    return shifted * inverse, inverse


def norm_back(hat, inverse, gain, upstream):
    scaled = upstream * gain
    first = jnp.mean(scaled, axis=0, keepdims=True)
    second = jnp.mean(scaled * hat, axis=0, keepdims=True)
    return inverse * (scaled - first - hat * second)


def gelu_both(values):
    bell = jnp.exp2(values * (values * (-0.5 * LOG2E))).astype(BF16)
    t = (1.0 / (jnp.abs(values) + TAIL_SHIFT)).astype(BF16)
    low = values.astype(BF16)
    poly = t * BF16(TAIL_POLY[-1]) + BF16(TAIL_POLY[-2])
    for coefficient in TAIL_POLY[-3::-1]:
        poly = poly * t + BF16(coefficient)
    tail = poly * t * bell
    phi = jnp.where(low >= BF16(0.0), BF16(1.0) - tail, tail)
    return low * phi, phi + low * bell * BF16(1.0 / math.sqrt(2.0 * math.pi))


def weave(main, *others):
    order = [((i + 0.5) / len(main), step) for i, step in enumerate(main)]
    for first, last, steps in others:
        order += [(first + (last - first) * (i + 0.5) / len(steps), step) for i, step in enumerate(steps)]
    for _, step in sorted(order, key=lambda entry: entry[0]):
        step()


def flip(values):
    return values.astype(F32).T.astype(BF16)


INPUTS = (
    "x", "cot", "slot", "crop", "sq", "sk", "sv", "sm", "sgain", "sbias",
    "cq", "ck", "cv", "cm", "cgain", "cbias", "we", "ws", "fgain", "fbias",
)
OUTPUTS = ("result", "grad", "early_out", "late_out", "totals")
VECTORS = ("sgain", "sbias", "cgain", "cbias", "fgain", "fbias")


def layer_kernel(sizes, *refs):
    names = INPUTS + OUTPUTS + tuple(scratch_shapes(sizes))
    r = types.SimpleNamespace(**dict(zip(names, refs, strict=True)))
    width, hidden, windows, peers = sizes.width, sizes.hidden, sizes.windows, sizes.peers
    factor = 1.0 / math.sqrt(width)
    scale = factor * LOG2E
    frame = lax.axis_index("frame")
    pix = lax.axis_index("pix")
    core = lax.rem(pix, 2)
    me = frame * (peers // 2) + lax.div(pix, 2)
    partner = (1 - frame, pix)
    sibling = (frame, pix + 1 - 2 * core)

    def peer(step):
        index = lax.rem(me + step, peers)
        return index, (lax.div(index, peers // 2), lax.rem(index, peers // 2) * 2 + core)

    barrier = pltpu.get_barrier_semaphore()
    pl.semaphore_signal(barrier, inc=1, device_id=sibling, device_id_type=MESH)

    def greet(step, carry):
        pl.semaphore_signal(barrier, inc=1, device_id=peer(step)[1], device_id_type=MESH)
        return carry

    lax.fori_loop(1, peers, greet, 0)

    slot = r.slot[0]
    live = lax.shift_right_logical(r.crop[0, slot], 1) * lax.shift_right_logical(r.crop[1, slot], 1)

    r.eye[...] = jnp.where(
        lax.broadcasted_iota(jnp.int32, (width, width), 0)
        == lax.broadcasted_iota(jnp.int32, (width, width), 1),
        1.0, 0.0,
    ).astype(BF16)
    r.self_qv_t[:width] = flip(r.sq[...])
    r.self_qv_t[width:] = flip(r.sv[...])
    r.self_k_t[...] = flip(r.sk[...])
    r.self_merge_t[...] = flip(r.sm[...])
    r.self_qkv[:, :width] = r.sq[...]
    r.self_qkv[:, width : 2 * width] = r.sk[...]
    r.self_qkv[:, 2 * width :] = r.sv[...]
    for i, name in enumerate(VECTORS):
        r.vectors[i] = jnp.broadcast_to(getattr(r, name)[...], (width, CHUNK)).T
    vector = lambda name: r.vectors[VECTORS.index(name)]
    for name in ("g_sqkv", "g_sm", "g_cqkv", "g_cm", "g_we", "g_ws", "g_vec"):
        getattr(r, name)[...] = jnp.zeros_like(getattr(r, name))
    r.v_aug[:, width:, :] = jnp.ones((2, ONES, WSLOT), BF16)

    def alive_at(start, size):
        token = lax.broadcasted_iota(jnp.int32, (1, size), 1) + lax.rem(start, WSLOT)
        return jnp.where(token < live, 1.0, 0.0)

    def rows_at(w):
        return pl.ds(pl.multiple_of(w * WSLOT, WSLOT), WSLOT)

    def cols_at(w, start=0, size=WSLOT):
        return pl.ds(pl.multiple_of(w * WSLOT + start, 128), size)

    def send_rows(w):
        return pltpu.make_async_remote_copy(
            src_ref=r.send.at[rows_at(w), :], dst_ref=r.other.at[rows_at(w), :],
            send_sem=r.sem_x.at[0, w], recv_sem=r.sem_x.at[1, w], device_id=partner, device_id_type=MESH,
        )

    def send_back(w):
        return pltpu.make_async_remote_copy(
            src_ref=r.back.at[w], dst_ref=r.received.at[w],
            send_sem=r.sem_b.at[0, w], recv_sem=r.sem_b.at[1, w], device_id=partner, device_id_type=MESH,
        )

    def store_rows(target, stage, w, sem):
        return pltpu.make_async_copy(stage.at[rows_at(w), :], target.at[rows_at(w), :], sem.at[w])

    def attend(w, u, exps, out, inverse):
        bufs = (r.buf_a, r.buf_b)
        tops, sums = {}, {}

        def score(t):
            first, size = TILES[t]
            got = nn(r.k[u], r.q_t[:, cols_at(w, first, size)])
            rest = got[FEWEST:]
            row = lax.broadcasted_iota(jnp.int32, rest.shape, 0) + FEWEST
            rest = jnp.where(row < live, rest, NEGATIVE)
            bufs[t % 2][:FEWEST, :size] = got[:FEWEST]
            bufs[t % 2][FEWEST:, :size] = rest
            tops[t] = scale * jnp.maximum(
                jnp.max(got[:FEWEST], axis=0, keepdims=True), jnp.max(rest, axis=0, keepdims=True)
            )

        def output_part(t, rows):
            first, size = TILES[t]
            part = nn(r.v_aug[u, :, rows], exps[rows, first : first + size])
            sums[t] = part if t not in sums else sums[t] + part

        def output(t):
            first, size = TILES[t]
            both = sums[t]
            share = 1.0 / both[width : width + 1]
            inverse[:, cols_at(w, first, size)] = share
            out[:, cols_at(w, first, size)] = (both[:width] * share).astype(BF16)

        def soften(t, start, count):
            first, size = TILES[t]
            rows = slice(start, start + count)
            if t:
                output_part(t - 1, rows)
            exps[rows, first : first + size] = jnp.exp2(
                bufs[t % 2][rows, :size] * scale - tops[t]
            ).astype(BF16)

        last = len(TILES) - 1
        steps = [functools.partial(score, 0)]
        for t in range(len(TILES)):
            if t < last:
                steps.append(functools.partial(score, t + 1))
            steps += [functools.partial(soften, t, start, count) for start, count in TILES]
            if t:
                steps.append(functools.partial(output, t - 1))
        return steps + [
            functools.partial(output_part, last, slice(0, WSLOT)), functools.partial(output, last)
        ]

    def attend_back(w, u, exps, dqkv):
        kept = {}

        def differ(t):
            first, size = TILES[t]
            cols = slice(first, first + size)
            grad = nn(r.v[u], r.up[u, :, cols]) - r.inner[u, :, cols]
            r.diff[:, cols] = exps[:, cols] * grad.astype(BF16)

        def query(t):
            first, size = TILES[t]
            cols = slice(first, first + size)
            dqkv[:width, cols] = (nn(r.k_t[u], r.diff[:, cols]) * factor).astype(BF16)

        def value():
            kept["v"] = nt(exps[...], r.up[u])

        def key():
            kept["k"] = nt(r.diff[...], r.q_t[:, cols_at(w)]) * factor

        def turn_value():
            dqkv[2 * width :, :] = kept["v"].T.astype(BF16)

        def turn_key():
            dqkv[width : 2 * width, :] = kept["k"].T.astype(BF16)

        steps = [functools.partial(differ, 0)]
        for t in range(1, len(TILES)):
            steps += [functools.partial(differ, t), functools.partial(query, t - 1)]
        return steps + [
            value, functools.partial(query, len(TILES) - 1), key, turn_value, turn_key
        ]

    def prepare_self(w, u):
        def project():
            stacked = nt(r.self_qv_t[...], r.x[rows_at(w), :]).astype(BF16)
            r.q_t[:, cols_at(w)] = stacked[:width]
            r.v_aug[u, :width, :] = stacked[width:]

        def keys():
            r.k[u] = nn(r.x[rows_at(w), :], r.sk[...]).astype(BF16)

        return [project, keys]

    def conclude_self(w):
        kept = {}

        def merge():
            kept["m"] = nn(r.self_merge_t[...], r.out_one[:, cols_at(w)])
            kept["x"] = nt(r.eye[...], r.x[rows_at(w), :])

        def norm(start):
            cols = slice(start, start + CHUNK)
            hat, _ = norm_stats(kept["m"][:, cols])
            x1 = kept["x"][:, cols] + hat * vector("sgain") + vector("sbias")
            r.x1[:, cols_at(w, start, CHUNK)] = x1
            r.concat[:width, cols_at(w, start, CHUNK)] = x1.astype(BF16)
            r.send[pl.ds(pl.multiple_of(w * WSLOT + start, CHUNK), CHUNK), :] = x1.T.astype(BF16)

        chunks = [functools.partial(norm, start) for start in range(0, WSLOT, CHUNK)]
        return [merge] + chunks + [send_rows(w).start]

    def forward_self(p, carry):
        w = 2 * p
        weave(prepare_self(w, 0))
        weave(
            attend(w, 0, r.exps.at[w], r.out_one, r.inverse_one), (0.5, 1.0, prepare_self(w + 1, 1))
        )

        @pl.when(p == 0)
        def _():
            pl.semaphore_wait(barrier, peers)

        weave(
            attend(w + 1, 1, r.exps.at[w + 1], r.out_one, r.inverse_one), (0.0, 0.8, conclude_self(w))
        )
        weave(conclude_self(w + 1))
        return carry

    lax.fori_loop(0, windows // 2, forward_self, 0)

    r.cross_q_t[...] = flip(r.cq[...])
    r.cross_k_t[...] = flip(r.ck[...])
    r.cross_v_t[...] = flip(r.cv[...])
    r.cross_merge_t[...] = flip(r.cm[...])
    r.cross_kv[:, :width] = r.ck[...]
    r.cross_kv[:, width:] = r.cv[...]
    r.expand_t[...] = flip(r.we[...])
    r.shrink_t[...] = flip(r.ws[...])

    def prepare_cross(w, u):
        def queries():
            r.q_t[:, cols_at(w)] = nn(r.cross_q_t[...], r.concat[:width, cols_at(w)]).astype(BF16)

        def values():
            send_rows(w).wait()
            r.v_aug[u, :width, :] = nt(r.cross_v_t[...], r.other[rows_at(w), :]).astype(BF16)

        def keys():
            r.k[u] = nn(r.other[rows_at(w), :], r.ck[...]).astype(BF16)

        return [queries, values, keys]

    def conclude_cross(w):
        kept = {}

        def merge():
            kept["m"] = nn(r.cross_merge_t[...], r.out_two[:, cols_at(w)])

        def norm(start):
            hat, _ = norm_stats(kept["m"][:, start : start + CHUNK])
            r.concat[width:, cols_at(w, start, CHUNK)] = (
                hat * vector("cgain") + vector("cbias")
            ).astype(BF16)

        return [merge] + [functools.partial(norm, start) for start in range(0, WSLOT, CHUNK)]

    def forward_cross(w):
        weave(prepare_cross(w, 0))
        weave(
            attend(w, 0, r.exps_two.at[0], r.out_two, r.inverse_two), (0.6, 1.0, prepare_cross(w + 1, 1))
        )
        weave(
            attend(w + 1, 1, r.exps_two.at[1], r.out_two, r.inverse_two), (0.0, 0.8, conclude_cross(w))
        )
        weave(conclude_cross(w + 1))

    spans = sizes.rows // SPAN

    def span(i):
        return pl.ds(pl.multiple_of(i * SPAN, SPAN), SPAN)

    def norm_tile(i, b, branch, up_all, start):
        part = slice(start, start + CHUNK)
        here = pl.ds(pl.multiple_of(i * SPAN + start, CHUNK), CHUNK)
        alive = alive_at(i * SPAN + start, CHUNK)
        hat, inverse = norm_stats(branch[:, part])
        result = (r.x1[:, here] + hat * vector("fgain") + vector("fbias")) * alive
        r.result_stage[here, :] = result.T.astype(BF16)
        up = up_all[:, part] * alive
        r.x1[:, here] = up
        r.g_vec[4] += up * hat
        r.g_vec[5] += up
        r.branch[b, :, part] = norm_back(hat, inverse, vector("fgain"), up).astype(BF16)

    def settle(i, total):
        r.x1[:, span(i)] += total[:width]
        r.grad_normed[:, span(i)] = total[width:]

    parts = [slice(start, start + SPAN) for start in range(0, hidden, SPAN)]

    def expand(i):
        r.buf_a[:hidden, :] = nn(r.expand_t[...], r.concat[:, span(i)])

    def activate(b, rows):
        act, slope = gelu_both(r.buf_a[rows, :])
        r.act[b, rows, :] = act
        r.slope[b, rows, :] = slope

    def hide(b):
        r.hid[...] = r.slope[b] * nn(r.ws[...], r.branch[b]).astype(BF16)

    def add(total, part):
        return part if total is None else total + part

    per_half = 2 * WSLOT // SPAN

    def feed_forward(half):
        first = per_half * half
        for name in ("act", "slope", "branch"):
            getattr(r, name)[2] = jnp.zeros(getattr(r, name).shape[1:], BF16)
        expand(first)
        for rows in parts:
            activate(0, rows)

        def feed(j, carry):
            for b in range(3):
                i = first + 3 * j + b
                old = (b + 2) % 3
                before = jnp.maximum(i - 1, first)
                expand(jnp.minimum(i + 1, spans - 1))
                hide(old)
                branch, total = None, None
                for rows in parts:
                    branch = add(branch, nn(r.shrink_t[:, rows], r.act[b, rows, :]))
                    total = add(total, nn(r.we[:, rows], r.hid[rows, :]))
                    activate((b + 1) % 3, rows)
                settle(before, total)
                up_all = nt(r.eye[...], r.cot[span(i), :])
                for_shrink = nt(r.act[old], r.branch[old])
                norm_tile(i, b, branch, up_all, 0)
                for_expand = nt(r.hid[...], r.concat[:, span(before)])
                norm_tile(i, b, branch, up_all, CHUNK)
                r.g_ws[...] += for_shrink
                r.g_we[...] += for_expand
            return carry

        lax.fori_loop(0, per_half // 3, feed, 0)
        end = first + per_half - 1
        last = (per_half - 1) % 3
        hide(last)
        settle(end, nn(r.we[...], r.hid[...]))
        r.g_ws[...] += nt(r.act[last], r.branch[last])
        r.g_we[...] += nt(r.hid[...], r.concat[:, span(end)])

    def upstream(w, u, merge_t, grad_at, number, gain, out, gradient, merge, inverse):
        kept = {"sums": [jnp.zeros((width, CHUNK), F32)] * 2}

        def remake():
            kept["m"] = nn(merge_t[...], out[:, cols_at(w)])

        def back(start):
            hat, root = norm_stats(kept["m"][:, start : start + CHUNK])
            grad = grad_at(start)
            sums = kept["sums"]
            kept["sums"] = [sums[0] + grad * hat, sums[1] + grad]
            r.grad_merged[u, :, start : start + CHUNK] = norm_back(
                hat, root, vector(gain), grad
            ).astype(BF16)

        def add_up():
            r.g_vec[number] += kept["sums"][0]
            r.g_vec[number + 1] += kept["sums"][1]
            kept["up"] = nn(merge[...], r.grad_merged[u])

        def collect():
            gradient[...] += nt(out[:, cols_at(w)], r.grad_merged[u])

        def lift():
            up = (kept["up"] * inverse[:, cols_at(w)]).astype(BF16)
            r.up[u] = up
            r.inner[u] = jnp.sum(
                up.astype(F32) * out[:, cols_at(w)].astype(F32), axis=0, keepdims=True
            )

        chunks = [functools.partial(back, start) for start in range(0, WSLOT, CHUNK)]
        return [remake] + chunks + [add_up, collect, lift]

    def unfold_cross(w, u):
        def keys():
            r.k_t[u] = nt(r.cross_k_t[...], r.other[rows_at(w), :]).astype(BF16)

        def values():
            r.v[u] = nn(r.other[rows_at(w), :], r.cv[...]).astype(BF16)

        steps = upstream(
            w, u, r.cross_merge_t, lambda start: r.grad_normed[:, cols_at(w, start, CHUNK)],
            2, "cgain", r.out_two, r.g_cm, r.cm, r.inverse_two,
        )
        return [steps[0], keys, values] + steps[1:]

    def deliver_cross(w):
        def back():
            r.back[w] = nn(r.cross_kv[...], r.dqkv[w, width:, :]).astype(BF16)
            send_back(w).start()

        def queries():
            r.g_cqkv[:width] += nt(r.dqkv[w, :width, :], r.concat[:width, cols_at(w)])

        def others():
            r.g_cqkv[width:] += nn(r.dqkv[w, width:, :], r.other[rows_at(w), :])

        def inputs():
            r.x1[:, cols_at(w)] += nn(r.cq[...], r.dqkv[w, :width, :])

        return [back, queries, others, inputs]

    def backward_cross(w):
        weave(unfold_cross(w, 0))
        weave(
            attend_back(w, 0, r.exps_two.at[0], r.dqkv.at[w]), (0.0, 0.9, unfold_cross(w + 1, 1))
        )
        weave(attend_back(w + 1, 1, r.exps_two.at[1], r.dqkv.at[w + 1]), (0.0, 0.5, deliver_cross(w)))
        weave(deliver_cross(w + 1))

    def middle(half, carry):
        forward_cross(2 * half)
        feed_forward(half)
        for u in range(2):
            store_rows(r.result, r.result_stage, 2 * half + u, r.sem_result).start()
        backward_cross(2 * half)
        return carry

    lax.fori_loop(0, windows // 2, middle, 0)

    early = Reduction(r, sizes.plans["early"], "early", sizes.scale, sibling, peer, core, me)
    late = Reduction(r, sizes.plans["late"], "late", sizes.scale, sibling, peer, core, me)
    early.begin(
        [r.g_we.at[:, pl.ds(0, width)], r.g_we.at[:, pl.ds(width, width)], r.g_ws, r.g_cqkv, r.g_cm]
    )

    def unfold_self(w, u):
        def queries():
            r.q_t[:, cols_at(w)] = nt(r.self_qv_t[:width, :], r.x[rows_at(w), :]).astype(BF16)

        def keys():
            r.k_t[u] = nt(r.self_k_t[...], r.x[rows_at(w), :]).astype(BF16)

        def values():
            r.v[u] = nn(r.x[rows_at(w), :], r.sv[...]).astype(BF16)
            send_back(w).wait()

        def grad_at(start):
            here = cols_at(w, start, CHUNK)
            grad = r.x1[:, here] + r.received[w, :, start : start + CHUNK].astype(F32)
            r.x1[:, here] = grad
            return grad

        steps = upstream(
            w, u, r.self_merge_t, grad_at, 0, "sgain", r.out_one, r.g_sm, r.sm, r.inverse_one
        )
        return [steps[0], queries, keys, values] + steps[1:]

    def deliver_self(w):
        def all_three():
            r.g_sqkv[...] += nn(r.dqkv[w], r.x[rows_at(w), :])

        return [all_three]

    def backward_self(p, carry):
        w = 2 * p
        weave(unfold_self(w, 0))
        weave(attend_back(w, 0, r.exps.at[w], r.dqkv.at[w]), (0.0, 0.9, unfold_self(w + 1, 1)))

        @pl.when(p == 0)
        def _():
            early.scatter()

        @pl.when(p == 1)
        def _():
            early.gather()

        weave(
            attend_back(w + 1, 1, r.exps.at[w + 1], r.dqkv.at[w + 1]), (0.0, 0.5, deliver_self(w))
        )
        weave(deliver_self(w + 1))
        return carry

    lax.fori_loop(0, windows // 2, backward_self, 0)

    def finish(w):
        place = w % 2
        stage = r.grad_stage.at[pl.ds(place * WSLOT, WSLOT), :]
        if w >= 2:
            store_grad(w - 2).wait()
        stage[...] = (r.x1[:, cols_at(w)] + nn(r.self_qkv[...], r.dqkv[w])).T
        store_grad(w).start()

    def store_grad(w):
        place = w % 2
        return pltpu.make_async_copy(
            r.grad_stage.at[pl.ds(place * WSLOT, WSLOT), :], r.grad.at[pl.ds(w * WSLOT, WSLOT), :],
            r.sem_grad.at[w],
        )

    late.begin([r.g_sqkv, r.g_sm], r.g_vec)
    early.share()
    finish(0)
    late.scatter()
    early.finish()
    early.store(r.early_out).start()
    finish(1)
    late.gather()
    if late.full:
        r.totals[...] = late.vector_total()
    finish(2)
    late.share()
    finish(3)
    late.finish()
    late.store(r.late_out).start()
    if not late.full:
        r.totals[...] = late.total[0, 0, late.shard :].astype(F32)

    def drain(w, carry):
        store_rows(r.result, r.result_stage, w, r.sem_result).wait()
        return carry

    lax.fori_loop(0, windows, drain, 0)
    store_grad(2).wait()
    store_grad(3).wait()
    early.store(r.early_out).wait()
    late.store(r.late_out).wait()


class Reduction:
    def __init__(self, r, plan, name, scale, sibling, peer, core, me):
        self.sibling, self.peer, self.core, self.me = sibling, peer, core, me
        self.scale = scale
        self.peers, self.owners, self.shard, self.extra, self.kept = (
            plan.peers, plan.owners, plan.shard, plan.extra, plan.kept
        )
        self.half = self.owners * self.shard
        self.full = self.owners == self.peers
        for field in ("pack", "from_sibling", "inbox", "total", "sems"):
            setattr(self, field, getattr(r, name + "_" + field))

    def copy(self, source, target, number, device):
        return pltpu.make_async_remote_copy(
            src_ref=source, dst_ref=target, send_sem=self.sems.at[0, number],
            recv_sem=self.sems.at[1, number], device_id=device, device_id_type=MESH,
        )

    def owning(self, then, otherwise=None):
        if self.full:
            then()
        else:
            pl.when(self.me < self.owners)(then)
            if otherwise is not None:
                pl.when(self.me >= self.owners)(otherwise)

    def halves(self):
        return self.copy(self.pack.at[1 - self.core], self.from_sibling, 0, self.sibling)

    def begin(self, pieces, vec=None):
        at = 0
        width = self.pack.shape[3]
        for piece in pieces:
            taken = 0
            while taken < piece.shape[0]:
                which, inside = divmod(at, self.half)
                index, offset = divmod(inside, self.shard)
                left = piece.shape[0] - taken
                if offset or left < self.shard:
                    count = min(left, self.shard - offset)
                    self.pack[which, index, offset : offset + count] = piece[
                        taken : taken + count, :
                    ].astype(BF16)
                else:
                    blocks = min(left // self.shard, self.owners - index)
                    count = blocks * self.shard
                    self.pack[which, index : index + blocks, : self.shard] = (
                        piece[taken : taken + count, :].astype(BF16).reshape(blocks, self.shard, width)
                    )
                at += count
                taken += count
        while at < 2 * self.half:
            which, inside = divmod(at, self.half)
            index, offset = divmod(inside, self.shard)
            count = self.shard - offset
            self.pack[which, index, offset : self.shard] = jnp.zeros((count, width), BF16)
            at += count
        if self.extra:
            sums = jnp.concatenate([jnp.sum(vec[i].T, axis=0, keepdims=True) for i in range(vec.shape[0])])
            rows = jnp.concatenate([sums, jnp.zeros((self.extra - vec.shape[0], width), F32)]).astype(BF16)
            for which in range(2):
                self.pack[which, :, self.shard :] = jnp.broadcast_to(
                    rows[None], (self.owners, self.extra, width)
                )
        self.halves().start()

    def wait(self, number, sent, received):
        if sent is not None:
            self.copy(sent, sent, number, self.sibling).wait_send()
        if received is not None:
            self.copy(received, received, number, self.sibling).wait_recv()

    def scatter(self):
        self.halves().wait()
        mine = self.pack[self.core].astype(F32) + self.from_sibling[...].astype(F32)
        self.pack[self.core] = mine.astype(BF16)

        def send(step, carry):
            index, device = self.peer(step)

            def go():
                place = self.pack.at[self.core, index]
                self.copy(place, self.inbox.at[self.me], 1, device).start()

            go() if self.full else pl.when(index < self.owners)(go)
            return carry

        lax.fori_loop(1, self.peers, send, 0)

        def own():
            self.inbox[self.me] = self.pack[self.core, self.me]

        self.owning(own)

    def gather(self):
        def own():
            self.wait(
                1, self.pack.at[0, pl.ds(0, self.owners - 1)], self.inbox.at[pl.ds(0, self.peers - 1)]
            )
            total = jnp.sum(self.inbox[:, : self.kept].astype(F32), axis=0) * self.scale
            self.total[self.core, self.me] = total.astype(BF16)

            def send(step, carry):
                place = self.total.at[self.core, self.me]
                self.copy(place, place, 2, self.peer(step)[1]).start()
                return carry

            lax.fori_loop(1, self.peers, send, 0)

        self.owning(own, lambda: self.wait(1, self.pack.at[0], None))

    def vector_total(self):
        return jnp.sum(self.inbox[:, self.shard :].astype(F32), axis=0) * self.scale

    def share(self):
        def own():
            for count in (self.owners - 1,) * ((self.peers - 1) // (self.owners - 1)) + (
                (self.peers - 1) % (self.owners - 1),
            ):
                if count:
                    self.wait(2, self.total.at[0, pl.ds(0, count)], None)
            self.wait(2, None, self.total.at[0, pl.ds(0, self.owners - 1)])

        self.owning(own, lambda: self.wait(2, None, self.total.at[0]))
        self.copy(self.total.at[self.core], self.total.at[self.core], 3, self.sibling).start()

    def finish(self):
        self.copy(self.total.at[self.core], self.total.at[self.core], 3, self.sibling).wait()

    def store(self, target):
        return pltpu.make_async_copy(self.total, target, self.sems.at[0, 4])


def scratch_shapes(sizes):
    width, hidden, windows, rows, peers = sizes.width, sizes.hidden, sizes.windows, sizes.rows, sizes.peers
    vmem = pltpu.VMEM
    dma = pltpu.SemaphoreType.DMA
    square = vmem((width, width), F32)
    shapes = {
        "eye": vmem((width, width), BF16),
        "self_qv_t": vmem((2 * width, width), BF16),
        "self_k_t": vmem((width, width), BF16),
        "self_merge_t": vmem((width, width), BF16),
        "self_qkv": vmem((width, 3 * width), BF16),
        "vectors": vmem((len(VECTORS), width, CHUNK), F32),
        "cross_q_t": vmem((width, width), BF16),
        "cross_k_t": vmem((width, width), BF16),
        "cross_v_t": vmem((width, width), BF16),
        "cross_merge_t": vmem((width, width), BF16),
        "cross_kv": vmem((width, 2 * width), BF16),
        "expand_t": vmem((hidden, 2 * width), BF16),
        "shrink_t": vmem((width, hidden), BF16),
        "g_sqkv": vmem((3 * width, width), F32),
        "g_cqkv": vmem((3 * width, width), F32),
        "g_sm": square,
        "g_cm": square,
        "g_we": vmem((hidden, 2 * width), F32),
        "g_ws": vmem((hidden, width), F32),
        "g_vec": vmem((len(VECTORS), width, CHUNK), F32),
        "q_t": vmem((width, rows), BF16),
        "k": vmem((2, WSLOT, width), BF16),
        "v_aug": vmem((2, width + ONES, WSLOT), BF16),
        "out_one": vmem((width, rows), BF16),
        "out_two": vmem((width, rows), BF16),
        "inverse_one": vmem((1, rows), F32),
        "inverse_two": vmem((1, rows), F32),
        "x1": vmem((width, rows), F32),
        "concat": vmem((2 * width, rows), BF16),
        "send": vmem((rows, width), BF16),
        "other": vmem((rows, width), BF16),
        "back": vmem((windows, width, WSLOT), BF16),
        "received": vmem((windows, width, WSLOT), BF16),
        "grad_normed": vmem((width, rows), F32),
        "exps": vmem((windows, WSLOT, WSLOT), BF16),
        "exps_two": vmem((2, WSLOT, WSLOT), BF16),
        "diff": vmem((WSLOT, WSLOT), BF16),
        "act": vmem((3, hidden, SPAN), BF16),
        "slope": vmem((3, hidden, SPAN), BF16),
        "branch": vmem((3, width, SPAN), BF16),
        "hid": vmem((hidden, SPAN), BF16),
        "buf_a": vmem((max(WSLOT, hidden), SPAN), F32),
        "buf_b": vmem((WSLOT, SPAN), F32),
        "grad_merged": vmem((2, width, WSLOT), BF16),
        "k_t": vmem((2, width, WSLOT), BF16),
        "v": vmem((2, WSLOT, width), BF16),
        "up": vmem((2, width, WSLOT), BF16),
        "inner": vmem((2, 1, WSLOT), F32),
        "dqkv": vmem((windows, 3 * width, WSLOT), BF16),
        "result_stage": vmem((rows, width), BF16),
        "grad_stage": vmem((2 * WSLOT, width), F32),
        "sem_x": dma((2, windows)),
        "sem_b": dma((2, windows)),
        "sem_result": dma((windows,)),
        "sem_grad": dma((windows,)),
    }
    for name, plan in sizes.plans.items():
        part = plan.shard + plan.extra
        shapes[name + "_pack"] = vmem((2, plan.owners, part, width), BF16)
        shapes[name + "_from_sibling"] = vmem((plan.owners, part, width), BF16)
        shapes[name + "_inbox"] = vmem((peers, part, width), BF16)
        shapes[name + "_total"] = vmem((2, plan.owners, plan.kept, width), BF16)
        shapes[name + "_sems"] = dma((2, 5))
    return shapes


def total_rows(total, shard, start, count):
    _, peers, _, width = total.shape
    at = start
    found = []
    while at < start + count:
        which, inside = divmod(at, peers * shard)
        index, offset = divmod(inside, shard)
        left = start + count - at
        if offset or left < shard:
            take = min(shard - offset, left)
            found.append(total[which, index, offset : offset + take])
        else:
            blocks = min(left // shard, peers - index)
            take = blocks * shard
            found.append(total[which, index : index + blocks, :shard].reshape(take, width))
        at += take
    return found[0] if len(found) == 1 else jnp.concatenate(found, axis=0)


def hand_out(sizes, *refs):
    result_in, grad_in, early, late, totals, result, grad = refs[:7]
    (o_sq, o_sk, o_sv, o_sm, o_sgain, o_sbias, o_cq, o_ck, o_cv, o_cm, o_cgain, o_cbias,
     o_we, o_ws, o_fgain, o_fbias) = refs[7:23]
    width, hidden = sizes.width, sizes.hidden
    shards = [plan.shard for plan in sizes.plans.values()]
    result[...] = result_in[...]
    grad[...] = grad_in[...]

    step = pl.program_id(0)
    quarter = hidden // sizes.windows
    for w in range(sizes.windows):

        @pl.when(step == w)
        def _():
            at = w * quarter
            o_we[:width, :] = total_rows(early, shards[0], at, quarter).astype(F32).T
            o_we[width:, :] = total_rows(early, shards[0], hidden + at, quarter).astype(F32).T
            o_ws[...] = total_rows(early, shards[0], 2 * hidden + at, quarter).astype(F32)

    @pl.when(step == 0)
    def _():
        for source, shard, base, group in (
            (early, shards[0], 3 * hidden, (o_cq, o_ck, o_cv, o_cm)), (late, shards[1], 0, (o_sq, o_sk, o_sv, o_sm))
        ):
            for i, ref in enumerate(group):
                total = total_rows(source, shard, base + i * width, width).astype(F32)
                ref[...] = total if i == 3 else total.T
        for i, ref in enumerate((o_sgain, o_sbias, o_cgain, o_cbias, o_fgain, o_fbias)):
            ref[...] = totals[i : i + 1, :]


def local(features, cotangent, slot_pair, crop_size, *weights):
    rows, width = features.shape[1:]
    hidden = weights[12].shape[1]
    peers = lax.axis_size("pix")

    def plan(count, extra=0):
        shard = -(-count // (2 * peers * 16)) * 16
        owners = min(peers, -(-count // (2 * shard)))
        kept = shard + (extra if owners < peers else 0)
        return types.SimpleNamespace(peers=peers, owners=owners, shard=shard, extra=extra, kept=kept)

    sizes = types.SimpleNamespace(
        rows=rows, width=width, hidden=hidden, windows=rows // WSLOT, peers=peers,
        scale=1.0 / math.sqrt(2.0 * rows * peers),
        plans={"early": plan(3 * hidden + 4 * width), "late": plan(4 * width, 16)},
    )
    flat = lambda value: value.reshape(1, -1) if value.ndim == 1 else value
    shape = jax.ShapeDtypeStruct
    small = pl.BlockSpec(memory_space=pltpu.VMEM)
    large = pl.BlockSpec(memory_space=pl.ANY)
    scalar = pl.BlockSpec(memory_space=pltpu.SMEM)
    square = shape((width, width), F32)
    row = shape((1, width), F32)
    big = [shape((rows, width), BF16), shape((rows, width), F32)]
    middle = pl.pallas_call(
        functools.partial(layer_kernel, sizes),
        in_specs=[small, small, scalar, scalar] + [small] * 16,
        out_specs=[large] * 4 + [small],
        out_shape=big + [
            shape((2, plan.owners, plan.kept, width), BF16) for plan in sizes.plans.values()
        ] + [shape((16, width), F32)],
        scratch_shapes=list(scratch_shapes(sizes).values()),
        compiler_params=pltpu.CompilerParams(
            collective_id=0, has_side_effects=True, vmem_limit_bytes=63 * 2**20
        ),
        name="layer",
    )(features[0], cotangent[0], slot_pair, crop_size.T, *[flat(weight) for weight in weights])
    moved = [pl.BlockSpec((WSLOT, width), lambda w: (w, 0))] * 2
    whole = lambda shape: pl.BlockSpec(shape, lambda w: (0,) * len(shape))
    smalls = [
        square, square, square, square, row, row, square, square, square, square, row, row,
        shape((2 * width, hidden), F32), shape((hidden, width), F32), row, row,
    ]
    outs = pl.pallas_call(
        functools.partial(hand_out, sizes),
        grid=(sizes.windows,),
        in_specs=moved + [whole(value.shape) for value in middle[2:]],
        out_specs=moved + [whole(value.shape) for value in smalls[:12]] + [
            pl.BlockSpec((2 * width, hidden // sizes.windows), lambda w: (0, w)),
            pl.BlockSpec((hidden // sizes.windows, width), lambda w: (w, 0)),
            whole(row.shape), whole(row.shape),
        ],
        out_shape=big + smalls,
        compiler_params=pltpu.CompilerParams(vmem_limit_bytes=60 * 2**20),
        name="hand_out",
    )(*middle)
    result, grad = outs[:2]
    return (result[None], grad[None]) + tuple(
        out.reshape(-1) if out.shape[0] == 1 else out for out in outs[2:]
    )


def solution(mesh):
    split = P("frame", "pix", None)
    return jax.shard_map(
        local,
        mesh=mesh,
        in_specs=(split, split, P("pix")) + (P(),) * 17,
        out_specs=(split, split) + (P(),) * 16,
        check_vma=False,
    )
```

```python
import functools
import math
import types

import jax
import jax.numpy as jnp
from jax import lax
from jax.experimental import pallas as pl
from jax.experimental.pallas import tpu as pltpu
from jax.sharding import PartitionSpec as P

WSLOT = 1152
FEWEST = 704
NEGATIVE = -1e30
EPSILON = 1e-05
LOG2E = 1.4426950408889634
F32 = jnp.float32
BF16 = jnp.bfloat16
MESH = pl.DeviceIdType.MESH
TAIL_SHIFT = 2.7777777777777777
TAIL_POLY = (0.39765776262463953, 1.1594294101832299, 1.9333185594349698, 10.032517622923805, -5.2492700447308085, -9.371923274701059)
SPAN = 256
CHUNK = 128
TILES = ((0, 256), (256, 256), (512, 256), (768, 256), (1024, 128))
ONES = 16


def nn(left, right):
    return jnp.dot(left, right, preferred_element_type=F32)


def nt(left, right):
    return lax.dot_general(left, right, (((1,), (1,)), ((), ())), preferred_element_type=F32)


def norm_stats(values):
    centre = jnp.mean(values, axis=0, keepdims=True)
    shifted = values - centre
    spread = jnp.mean(shifted * shifted, axis=0, keepdims=True)
    inverse = lax.rsqrt(spread + EPSILON)
    return shifted * inverse, inverse


def norm_back(hat, inverse, gain, upstream):
    scaled = upstream * gain
    first = jnp.mean(scaled, axis=0, keepdims=True)
    second = jnp.mean(scaled * hat, axis=0, keepdims=True)
    return inverse * (scaled - first - hat * second)


def gelu_both(values):
    bell = jnp.exp2(values * (values * (-0.5 * LOG2E))).astype(BF16)
    t = (1.0 / (jnp.abs(values) + TAIL_SHIFT)).astype(BF16)
    low = values.astype(BF16)
    poly = t * BF16(TAIL_POLY[-1]) + BF16(TAIL_POLY[-2])
    for coefficient in TAIL_POLY[-3::-1]:
        poly = poly * t + BF16(coefficient)
    tail = poly * t * bell
    phi = jnp.where(low >= BF16(0.0), BF16(1.0) - tail, tail)
    return low * phi, phi + low * bell * BF16(1.0 / math.sqrt(2.0 * math.pi))


def weave(main, *others):
    order = [((i + 0.5) / len(main), step) for i, step in enumerate(main)]
    for first, last, steps in others:
        order += [(first + (last - first) * (i + 0.5) / len(steps), step) for i, step in enumerate(steps)]
    for _, step in sorted(order, key=lambda entry: entry[0]):
        step()


def flip(values):
    return values.astype(F32).T.astype(BF16)


INPUTS = (
    "x", "cot", "slot", "crop", "sq", "sk", "sv", "sm", "sgain", "sbias",
    "cq", "ck", "cv", "cm", "cgain", "cbias", "we", "ws", "fgain", "fbias",
)
OUTPUTS = ("result", "grad", "feed_out", "cross_out", "late_out", "totals")
VECTORS = ("sgain", "sbias", "cgain", "cbias", "fgain", "fbias")


def layer_kernel(sizes, *refs):
    names = INPUTS + OUTPUTS + tuple(scratch_shapes(sizes))
    r = types.SimpleNamespace(**dict(zip(names, refs, strict=True)))
    width, hidden, windows, peers = sizes.width, sizes.hidden, sizes.windows, sizes.peers
    factor = 1.0 / math.sqrt(width)
    scale = factor * LOG2E
    frame = lax.axis_index("frame")
    pix = lax.axis_index("pix")
    core = lax.rem(pix, 2)
    me = frame * (peers // 2) + lax.div(pix, 2)
    partner = (1 - frame, pix)
    sibling = (frame, pix + 1 - 2 * core)

    def peer(step):
        index = lax.rem(me + step, peers)
        return index, (lax.div(index, peers // 2), lax.rem(index, peers // 2) * 2 + core)

    barrier = pltpu.get_barrier_semaphore()
    pl.semaphore_signal(barrier, inc=1, device_id=sibling, device_id_type=MESH)

    def greet(step, carry):
        pl.semaphore_signal(barrier, inc=1, device_id=peer(step)[1], device_id_type=MESH)
        return carry

    lax.fori_loop(1, peers, greet, 0)

    slot = r.slot[0]
    live = lax.shift_right_logical(r.crop[0, slot], 1) * lax.shift_right_logical(r.crop[1, slot], 1)

    r.eye[...] = jnp.where(
        lax.broadcasted_iota(jnp.int32, (width, width), 0)
        == lax.broadcasted_iota(jnp.int32, (width, width), 1),
        1.0, 0.0,
    ).astype(BF16)
    r.self_qv_t[:width] = flip(r.sq[...])
    r.self_qv_t[width:] = flip(r.sv[...])
    r.self_k_t[...] = flip(r.sk[...])
    r.self_merge_t[...] = flip(r.sm[...])
    r.self_qkv[:, :width] = r.sq[...]
    r.self_qkv[:, width : 2 * width] = r.sk[...]
    r.self_qkv[:, 2 * width :] = r.sv[...]
    for i, name in enumerate(VECTORS):
        r.vectors[i] = jnp.broadcast_to(getattr(r, name)[...], (width, CHUNK)).T
    vector = lambda name: r.vectors[VECTORS.index(name)]
    for name in ("g_sqkv", "g_sm", "g_cqkv", "g_cm", "g_we", "g_ws", "g_vec"):
        getattr(r, name)[...] = jnp.zeros_like(getattr(r, name))
    r.v_aug[:, width:, :] = jnp.ones((2, ONES, WSLOT), BF16)

    def alive_at(start, size):
        token = lax.broadcasted_iota(jnp.int32, (1, size), 1) + lax.rem(start, WSLOT)
        return jnp.where(token < live, 1.0, 0.0)

    def rows_at(w):
        return pl.ds(pl.multiple_of(w * WSLOT, WSLOT), WSLOT)

    def cols_at(w, start=0, size=WSLOT):
        return pl.ds(pl.multiple_of(w * WSLOT + start, 128), size)

    def send_rows(w):
        return pltpu.make_async_remote_copy(
            src_ref=r.send.at[rows_at(w), :], dst_ref=r.other.at[rows_at(w), :],
            send_sem=r.sem_x.at[0, w], recv_sem=r.sem_x.at[1, w], device_id=partner, device_id_type=MESH,
        )

    def send_back(w):
        return pltpu.make_async_remote_copy(
            src_ref=r.back.at[w], dst_ref=r.received.at[w],
            send_sem=r.sem_b.at[0, w], recv_sem=r.sem_b.at[1, w], device_id=partner, device_id_type=MESH,
        )

    def store_rows(target, stage, w, sem):
        return pltpu.make_async_copy(stage.at[rows_at(w), :], target.at[rows_at(w), :], sem.at[w])

    def attend(w, u, exps, out, inverse):
        bufs = (r.buf_a, r.buf_b)
        tops, sums = {}, {}

        def score(t):
            first, size = TILES[t]
            got = nn(r.k[u], r.q_t[:, cols_at(w, first, size)])
            rest = got[FEWEST:]
            row = lax.broadcasted_iota(jnp.int32, rest.shape, 0) + FEWEST
            rest = jnp.where(row < live, rest, NEGATIVE)
            bufs[t % 2][:FEWEST, :size] = got[:FEWEST]
            bufs[t % 2][FEWEST:, :size] = rest
            tops[t] = scale * jnp.maximum(
                jnp.max(got[:FEWEST], axis=0, keepdims=True), jnp.max(rest, axis=0, keepdims=True)
            )

        def output_part(t, rows):
            first, size = TILES[t]
            part = nn(r.v_aug[u, :, rows], exps[rows, first : first + size])
            sums[t] = part if t not in sums else sums[t] + part

        def output(t):
            first, size = TILES[t]
            both = sums[t]
            share = 1.0 / both[width : width + 1]
            inverse[:, cols_at(w, first, size)] = share
            out[:, cols_at(w, first, size)] = (both[:width] * share).astype(BF16)

        def soften(t, start, count):
            first, size = TILES[t]
            rows = slice(start, start + count)
            if t:
                output_part(t - 1, rows)
            exps[rows, first : first + size] = jnp.exp2(
                bufs[t % 2][rows, :size] * scale - tops[t]
            ).astype(BF16)

        last = len(TILES) - 1
        steps = [functools.partial(score, 0)]
        for t in range(len(TILES)):
            if t < last:
                steps.append(functools.partial(score, t + 1))
            steps += [functools.partial(soften, t, start, count) for start, count in TILES]
            if t:
                steps.append(functools.partial(output, t - 1))
        return steps + [
            functools.partial(output_part, last, slice(0, WSLOT)), functools.partial(output, last)
        ]

    def attend_back(w, u, exps, dqkv):
        kept = {}

        def differ(t):
            first, size = TILES[t]
            cols = slice(first, first + size)
            grad = nn(r.v[u], r.up[u, :, cols]) - r.inner[u, :, cols]
            r.diff[:, cols] = exps[:, cols] * grad.astype(BF16)

        def query(t):
            first, size = TILES[t]
            cols = slice(first, first + size)
            dqkv[:width, cols] = (nn(r.k_t[u], r.diff[:, cols]) * factor).astype(BF16)

        def value():
            kept["v"] = nt(exps[...], r.up[u])

        def key():
            kept["k"] = nt(r.diff[...], r.q_t[:, cols_at(w)]) * factor

        def turn_value():
            dqkv[2 * width :, :] = kept["v"].T.astype(BF16)

        def turn_key():
            dqkv[width : 2 * width, :] = kept["k"].T.astype(BF16)

        steps = [functools.partial(differ, 0)]
        for t in range(1, len(TILES)):
            steps += [functools.partial(differ, t), functools.partial(query, t - 1)]
        return steps + [
            value, functools.partial(query, len(TILES) - 1), key, turn_value, turn_key
        ]

    def prepare_self(w, u):
        def project():
            stacked = nt(r.self_qv_t[...], r.x[rows_at(w), :]).astype(BF16)
            r.q_t[:, cols_at(w)] = stacked[:width]
            r.v_aug[u, :width, :] = stacked[width:]

        def keys():
            r.k[u] = nn(r.x[rows_at(w), :], r.sk[...]).astype(BF16)

        return [project, keys]

    def conclude_self(w):
        kept = {}

        def merge():
            kept["m"] = nn(r.self_merge_t[...], r.out_one[:, cols_at(w)])
            kept["x"] = nt(r.eye[...], r.x[rows_at(w), :])

        def norm(start):
            cols = slice(start, start + CHUNK)
            hat, _ = norm_stats(kept["m"][:, cols])
            x1 = kept["x"][:, cols] + hat * vector("sgain") + vector("sbias")
            r.x1[:, cols_at(w, start, CHUNK)] = x1
            r.concat[:width, cols_at(w, start, CHUNK)] = x1.astype(BF16)
            r.send[pl.ds(pl.multiple_of(w * WSLOT + start, CHUNK), CHUNK), :] = x1.T.astype(BF16)

        chunks = [functools.partial(norm, start) for start in range(0, WSLOT, CHUNK)]
        return [merge] + chunks + [send_rows(w).start]

    def forward_self(p, carry):
        w = 2 * p
        weave(prepare_self(w, 0))
        weave(
            attend(w, 0, r.exps.at[w], r.out_one, r.inverse_one), (0.5, 1.0, prepare_self(w + 1, 1))
        )

        @pl.when(p == 0)
        def _():
            pl.semaphore_wait(barrier, peers)

        weave(
            attend(w + 1, 1, r.exps.at[w + 1], r.out_one, r.inverse_one), (0.0, 0.8, conclude_self(w))
        )
        weave(conclude_self(w + 1))
        return carry

    lax.fori_loop(0, windows // 2, forward_self, 0)

    r.cross_q_t[...] = flip(r.cq[...])
    r.cross_k_t[...] = flip(r.ck[...])
    r.cross_v_t[...] = flip(r.cv[...])
    r.cross_merge_t[...] = flip(r.cm[...])
    r.cross_kv[:, :width] = r.ck[...]
    r.cross_kv[:, width:] = r.cv[...]
    r.expand_t[...] = flip(r.we[...])
    r.shrink_t[...] = flip(r.ws[...])

    def prepare_cross(w, u):
        def queries():
            r.q_t[:, cols_at(w)] = nn(r.cross_q_t[...], r.concat[:width, cols_at(w)]).astype(BF16)

        def values():
            send_rows(w).wait()
            r.v_aug[u, :width, :] = nt(r.cross_v_t[...], r.other[rows_at(w), :]).astype(BF16)

        def keys():
            r.k[u] = nn(r.other[rows_at(w), :], r.ck[...]).astype(BF16)

        return [queries, values, keys]

    def conclude_cross(w):
        kept = {}

        def merge():
            kept["m"] = nn(r.cross_merge_t[...], r.out_two[:, cols_at(w)])

        def norm(start):
            hat, _ = norm_stats(kept["m"][:, start : start + CHUNK])
            r.concat[width:, cols_at(w, start, CHUNK)] = (
                hat * vector("cgain") + vector("cbias")
            ).astype(BF16)

        return [merge] + [functools.partial(norm, start) for start in range(0, WSLOT, CHUNK)]

    def forward_cross(w):
        weave(prepare_cross(w, 0))
        weave(
            attend(w, 0, r.exps_two.at[0], r.out_two, r.inverse_two), (0.6, 1.0, prepare_cross(w + 1, 1))
        )
        weave(
            attend(w + 1, 1, r.exps_two.at[1], r.out_two, r.inverse_two), (0.0, 0.8, conclude_cross(w))
        )
        weave(conclude_cross(w + 1))

    spans = sizes.rows // SPAN

    def span(i):
        return pl.ds(pl.multiple_of(i * SPAN, SPAN), SPAN)

    def norm_tile(i, b, branch, up_all, start):
        part = slice(start, start + CHUNK)
        here = pl.ds(pl.multiple_of(i * SPAN + start, CHUNK), CHUNK)
        alive = alive_at(i * SPAN + start, CHUNK)
        hat, inverse = norm_stats(branch[:, part])
        result = (r.x1[:, here] + hat * vector("fgain") + vector("fbias")) * alive
        r.result_stage[here, :] = result.T.astype(BF16)
        up = up_all[:, part] * alive
        r.x1[:, here] = up
        r.g_vec[4] += up * hat
        r.g_vec[5] += up
        r.branch[b, :, part] = norm_back(hat, inverse, vector("fgain"), up).astype(BF16)

    def settle(i, total):
        r.x1[:, span(i)] += total[:width]
        r.grad_normed[:, span(i)] = total[width:]

    parts = [slice(start, start + SPAN) for start in range(0, hidden, SPAN)]

    def expand(i):
        r.buf_a[:hidden, :] = nn(r.expand_t[...], r.concat[:, span(i)])

    def activate(b, rows):
        act, slope = gelu_both(r.buf_a[rows, :])
        r.act[b, rows, :] = act
        r.slope[b, rows, :] = slope

    def hide(b):
        r.hid[...] = r.slope[b] * nn(r.ws[...], r.branch[b]).astype(BF16)

    def add(total, part):
        return part if total is None else total + part

    per_half = 2 * WSLOT // SPAN

    def feed_forward(half):
        first = per_half * half
        for name in ("act", "slope", "branch"):
            getattr(r, name)[2] = jnp.zeros(getattr(r, name).shape[1:], BF16)
        expand(first)
        for rows in parts:
            activate(0, rows)

        def feed(j, carry):
            for b in range(3):
                i = first + 3 * j + b
                old = (b + 2) % 3
                before = jnp.maximum(i - 1, first)
                expand(jnp.minimum(i + 1, spans - 1))
                hide(old)
                branch, total = None, None
                for rows in parts:
                    branch = add(branch, nn(r.shrink_t[:, rows], r.act[b, rows, :]))
                    total = add(total, nn(r.we[:, rows], r.hid[rows, :]))
                    activate((b + 1) % 3, rows)
                settle(before, total)
                up_all = nt(r.eye[...], r.cot[span(i), :])
                for_shrink = nt(r.act[old], r.branch[old])
                norm_tile(i, b, branch, up_all, 0)
                for_expand = nt(r.hid[...], r.concat[:, span(before)])
                norm_tile(i, b, branch, up_all, CHUNK)
                r.g_ws[...] += for_shrink
                r.g_we[...] += for_expand
            return carry

        lax.fori_loop(0, per_half // 3, feed, 0)
        end = first + per_half - 1
        last = (per_half - 1) % 3
        hide(last)
        settle(end, nn(r.we[...], r.hid[...]))
        r.g_ws[...] += nt(r.act[last], r.branch[last])
        r.g_we[...] += nt(r.hid[...], r.concat[:, span(end)])

    def upstream(w, u, merge_t, grad_at, number, gain, out, gradient, merge, inverse):
        kept = {"sums": [jnp.zeros((width, CHUNK), F32)] * 2}

        def remake():
            kept["m"] = nn(merge_t[...], out[:, cols_at(w)])

        def back(start):
            hat, root = norm_stats(kept["m"][:, start : start + CHUNK])
            grad = grad_at(start)
            sums = kept["sums"]
            kept["sums"] = [sums[0] + grad * hat, sums[1] + grad]
            r.grad_merged[u, :, start : start + CHUNK] = norm_back(
                hat, root, vector(gain), grad
            ).astype(BF16)

        def add_up():
            r.g_vec[number] += kept["sums"][0]
            r.g_vec[number + 1] += kept["sums"][1]
            kept["up"] = nn(merge[...], r.grad_merged[u])

        def collect():
            gradient[...] += nt(out[:, cols_at(w)], r.grad_merged[u])

        def lift():
            up = (kept["up"] * inverse[:, cols_at(w)]).astype(BF16)
            r.up[u] = up
            r.inner[u] = jnp.sum(
                up.astype(F32) * out[:, cols_at(w)].astype(F32), axis=0, keepdims=True
            )

        chunks = [functools.partial(back, start) for start in range(0, WSLOT, CHUNK)]
        return [remake] + chunks + [add_up, collect, lift]

    def unfold_cross(w, u):
        def keys():
            r.k_t[u] = nt(r.cross_k_t[...], r.other[rows_at(w), :]).astype(BF16)

        def values():
            r.v[u] = nn(r.other[rows_at(w), :], r.cv[...]).astype(BF16)

        steps = upstream(
            w, u, r.cross_merge_t, lambda start: r.grad_normed[:, cols_at(w, start, CHUNK)],
            2, "cgain", r.out_two, r.g_cm, r.cm, r.inverse_two,
        )
        return [steps[0], keys, values] + steps[1:]

    def deliver_cross(w):
        def back():
            r.back[w] = nn(r.cross_kv[...], r.dqkv[w, width:, :]).astype(BF16)
            send_back(w).start()

        def queries():
            r.g_cqkv[:width] += nt(r.dqkv[w, :width, :], r.concat[:width, cols_at(w)])

        def others():
            r.g_cqkv[width:] += nn(r.dqkv[w, width:, :], r.other[rows_at(w), :])

        def inputs():
            r.x1[:, cols_at(w)] += nn(r.cq[...], r.dqkv[w, :width, :])

        return [back, queries, others, inputs]

    def backward_cross(w):
        weave(unfold_cross(w, 0))
        weave(
            attend_back(w, 0, r.exps_two.at[0], r.dqkv.at[w]), (0.0, 0.9, unfold_cross(w + 1, 1))
        )

        @pl.when(w == windows - 2)
        def _():
            feed_sum.scatter()

        weave(attend_back(w + 1, 1, r.exps_two.at[1], r.dqkv.at[w + 1]), (0.0, 0.5, deliver_cross(w)))
        weave(deliver_cross(w + 1))

    feed_sum = Reduction(r, sizes.plans["feed"], "feed", sizes.scale, sibling, peer, core, me)
    cross_sum = Reduction(r, sizes.plans["cross"], "cross", sizes.scale, sibling, peer, core, me)
    late = Reduction(r, sizes.plans["late"], "late", sizes.scale, sibling, peer, core, me)

    def middle(half, carry):
        forward_cross(2 * half)
        feed_forward(half)
        for u in range(2):
            store_rows(r.result, r.result_stage, 2 * half + u, r.sem_result).start()

        @pl.when(half == windows // 2 - 1)
        def _():
            feed_sum.begin([r.g_we.at[:, pl.ds(0, width)], r.g_we.at[:, pl.ds(width, width)], r.g_ws])

        backward_cross(2 * half)
        return carry

    lax.fori_loop(0, windows // 2, middle, 0)

    cross_sum.begin([r.g_cqkv, r.g_cm])

    def unfold_self(w, u):
        def queries():
            r.q_t[:, cols_at(w)] = nt(r.self_qv_t[:width, :], r.x[rows_at(w), :]).astype(BF16)

        def keys():
            r.k_t[u] = nt(r.self_k_t[...], r.x[rows_at(w), :]).astype(BF16)

        def values():
            r.v[u] = nn(r.x[rows_at(w), :], r.sv[...]).astype(BF16)
            send_back(w).wait()

        def grad_at(start):
            here = cols_at(w, start, CHUNK)
            grad = r.x1[:, here] + r.received[w, :, start : start + CHUNK].astype(F32)
            r.x1[:, here] = grad
            return grad

        steps = upstream(
            w, u, r.self_merge_t, grad_at, 0, "sgain", r.out_one, r.g_sm, r.sm, r.inverse_one
        )
        return [steps[0], queries, keys, values] + steps[1:]

    def deliver_self(w):
        def all_three():
            r.g_sqkv[...] += nn(r.dqkv[w], r.x[rows_at(w), :])

        return [all_three]

    def backward_self(p, carry):
        w = 2 * p
        weave(unfold_self(w, 0))
        weave(attend_back(w, 0, r.exps.at[w], r.dqkv.at[w]), (0.0, 0.9, unfold_self(w + 1, 1)))

        @pl.when(p == 0)
        def _():
            feed_sum.gather()
            cross_sum.scatter()

        @pl.when(p == 1)
        def _():
            cross_sum.gather()
            feed_sum.share()

        weave(
            attend_back(w + 1, 1, r.exps.at[w + 1], r.dqkv.at[w + 1]), (0.0, 0.5, deliver_self(w))
        )
        weave(deliver_self(w + 1))
        return carry

    lax.fori_loop(0, windows // 2, backward_self, 0)

    def finish(w):
        place = w % 2
        stage = r.grad_stage.at[pl.ds(place * WSLOT, WSLOT), :]
        if w >= 2:
            store_grad(w - 2).wait()
        stage[...] = (r.x1[:, cols_at(w)] + nn(r.self_qkv[...], r.dqkv[w])).T
        store_grad(w).start()

    def store_grad(w):
        place = w % 2
        return pltpu.make_async_copy(
            r.grad_stage.at[pl.ds(place * WSLOT, WSLOT), :], r.grad.at[pl.ds(w * WSLOT, WSLOT), :],
            r.sem_grad.at[w],
        )

    late.begin([r.g_sqkv, r.g_sm], r.g_vec)
    finish(0)
    late.scatter()
    cross_sum.share()
    finish(1)
    feed_sum.finish()
    feed_sum.store(r.feed_out).start()
    late.gather()
    if late.full:
        r.totals[...] = late.vector_total()
    finish(2)
    cross_sum.finish()
    cross_sum.store(r.cross_out).start()
    late.share()
    finish(3)
    late.finish()
    late.store(r.late_out).start()
    if not late.full:
        r.totals[...] = late.total[0, 0, late.shard :].astype(F32)

    def drain(w, carry):
        store_rows(r.result, r.result_stage, w, r.sem_result).wait()
        return carry

    lax.fori_loop(0, windows, drain, 0)
    store_grad(2).wait()
    store_grad(3).wait()
    feed_sum.store(r.feed_out).wait()
    cross_sum.store(r.cross_out).wait()
    late.store(r.late_out).wait()


class Reduction:
    def __init__(self, r, plan, name, scale, sibling, peer, core, me):
        self.sibling, self.peer, self.core, self.me = sibling, peer, core, me
        self.scale = scale
        self.peers, self.owners, self.shard, self.extra, self.kept = (
            plan.peers, plan.owners, plan.shard, plan.extra, plan.kept
        )
        self.half = self.owners * self.shard
        self.full = self.owners == self.peers
        for field in ("pack", "from_sibling", "inbox", "total", "sems"):
            setattr(self, field, getattr(r, name + "_" + field))

    def copy(self, source, target, number, device):
        return pltpu.make_async_remote_copy(
            src_ref=source, dst_ref=target, send_sem=self.sems.at[0, number],
            recv_sem=self.sems.at[1, number], device_id=device, device_id_type=MESH,
        )

    def owning(self, then, otherwise=None):
        if self.full:
            then()
        else:
            pl.when(self.me < self.owners)(then)
            if otherwise is not None:
                pl.when(self.me >= self.owners)(otherwise)

    def halves(self):
        return self.copy(self.pack.at[1 - self.core], self.from_sibling, 0, self.sibling)

    def begin(self, pieces, vec=None):
        at = 0
        width = self.pack.shape[3]
        for piece in pieces:
            taken = 0
            while taken < piece.shape[0]:
                which, inside = divmod(at, self.half)
                index, offset = divmod(inside, self.shard)
                left = piece.shape[0] - taken
                if offset or left < self.shard:
                    count = min(left, self.shard - offset)
                    self.pack[which, index, offset : offset + count] = piece[
                        taken : taken + count, :
                    ].astype(BF16)
                else:
                    blocks = min(left // self.shard, self.owners - index)
                    count = blocks * self.shard
                    self.pack[which, index : index + blocks, : self.shard] = (
                        piece[taken : taken + count, :].astype(BF16).reshape(blocks, self.shard, width)
                    )
                at += count
                taken += count
        while at < 2 * self.half:
            which, inside = divmod(at, self.half)
            index, offset = divmod(inside, self.shard)
            count = self.shard - offset
            self.pack[which, index, offset : self.shard] = jnp.zeros((count, width), BF16)
            at += count
        if self.extra:
            sums = jnp.concatenate([jnp.sum(vec[i].T, axis=0, keepdims=True) for i in range(vec.shape[0])])
            rows = jnp.concatenate([sums, jnp.zeros((self.extra - vec.shape[0], width), F32)]).astype(BF16)
            for which in range(2):
                self.pack[which, :, self.shard :] = jnp.broadcast_to(
                    rows[None], (self.owners, self.extra, width)
                )
        self.halves().start()

    def wait(self, number, sent, received):
        if sent is not None:
            self.copy(sent, sent, number, self.sibling).wait_send()
        if received is not None:
            self.copy(received, received, number, self.sibling).wait_recv()

    def scatter(self):
        self.halves().wait()
        mine = self.pack[self.core].astype(F32) + self.from_sibling[...].astype(F32)
        self.pack[self.core] = mine.astype(BF16)

        def send(step, carry):
            index, device = self.peer(step)

            def go():
                place = self.pack.at[self.core, index]
                self.copy(place, self.inbox.at[self.me], 1, device).start()

            go() if self.full else pl.when(index < self.owners)(go)
            return carry

        lax.fori_loop(1, self.peers, send, 0)

        def own():
            self.inbox[self.me] = self.pack[self.core, self.me]

        self.owning(own)

    def gather(self):
        def own():
            self.wait(
                1, self.pack.at[0, pl.ds(0, self.owners - 1)], self.inbox.at[pl.ds(0, self.peers - 1)]
            )
            total = jnp.sum(self.inbox[:, : self.kept].astype(F32), axis=0) * self.scale
            self.total[self.core, self.me] = total.astype(BF16)

            def send(step, carry):
                place = self.total.at[self.core, self.me]
                self.copy(place, place, 2, self.peer(step)[1]).start()
                return carry

            lax.fori_loop(1, self.peers, send, 0)

        self.owning(own, lambda: self.wait(1, self.pack.at[0], None))

    def vector_total(self):
        return jnp.sum(self.inbox[:, self.shard :].astype(F32), axis=0) * self.scale

    def share(self):
        def own():
            for count in (self.owners - 1,) * ((self.peers - 1) // (self.owners - 1)) + (
                (self.peers - 1) % (self.owners - 1),
            ):
                if count:
                    self.wait(2, self.total.at[0, pl.ds(0, count)], None)
            self.wait(2, None, self.total.at[0, pl.ds(0, self.owners - 1)])

        self.owning(own, lambda: self.wait(2, None, self.total.at[0]))
        self.copy(self.total.at[self.core], self.total.at[self.core], 3, self.sibling).start()

    def finish(self):
        self.copy(self.total.at[self.core], self.total.at[self.core], 3, self.sibling).wait()

    def store(self, target):
        return pltpu.make_async_copy(self.total, target, self.sems.at[0, 4])


def scratch_shapes(sizes):
    width, hidden, windows, rows, peers = sizes.width, sizes.hidden, sizes.windows, sizes.rows, sizes.peers
    vmem = pltpu.VMEM
    dma = pltpu.SemaphoreType.DMA
    square = vmem((width, width), F32)
    shapes = {
        "eye": vmem((width, width), BF16),
        "self_qv_t": vmem((2 * width, width), BF16),
        "self_k_t": vmem((width, width), BF16),
        "self_merge_t": vmem((width, width), BF16),
        "self_qkv": vmem((width, 3 * width), BF16),
        "vectors": vmem((len(VECTORS), width, CHUNK), F32),
        "cross_q_t": vmem((width, width), BF16),
        "cross_k_t": vmem((width, width), BF16),
        "cross_v_t": vmem((width, width), BF16),
        "cross_merge_t": vmem((width, width), BF16),
        "cross_kv": vmem((width, 2 * width), BF16),
        "expand_t": vmem((hidden, 2 * width), BF16),
        "shrink_t": vmem((width, hidden), BF16),
        "g_sqkv": vmem((3 * width, width), F32),
        "g_cqkv": vmem((3 * width, width), F32),
        "g_sm": square,
        "g_cm": square,
        "g_we": vmem((hidden, 2 * width), F32),
        "g_ws": vmem((hidden, width), F32),
        "g_vec": vmem((len(VECTORS), width, CHUNK), F32),
        "q_t": vmem((width, rows), BF16),
        "k": vmem((2, WSLOT, width), BF16),
        "v_aug": vmem((2, width + ONES, WSLOT), BF16),
        "out_one": vmem((width, rows), BF16),
        "out_two": vmem((width, rows), BF16),
        "inverse_one": vmem((1, rows), F32),
        "inverse_two": vmem((1, rows), F32),
        "x1": vmem((width, rows), F32),
        "concat": vmem((2 * width, rows), BF16),
        "send": vmem((rows, width), BF16),
        "other": vmem((rows, width), BF16),
        "back": vmem((windows, width, WSLOT), BF16),
        "received": vmem((windows, width, WSLOT), BF16),
        "grad_normed": vmem((width, rows), F32),
        "exps": vmem((windows, WSLOT, WSLOT), BF16),
        "exps_two": vmem((2, WSLOT, WSLOT), BF16),
        "diff": vmem((WSLOT, WSLOT), BF16),
        "act": vmem((3, hidden, SPAN), BF16),
        "slope": vmem((3, hidden, SPAN), BF16),
        "branch": vmem((3, width, SPAN), BF16),
        "hid": vmem((hidden, SPAN), BF16),
        "buf_a": vmem((max(WSLOT, hidden), SPAN), F32),
        "buf_b": vmem((WSLOT, SPAN), F32),
        "grad_merged": vmem((2, width, WSLOT), BF16),
        "k_t": vmem((2, width, WSLOT), BF16),
        "v": vmem((2, WSLOT, width), BF16),
        "up": vmem((2, width, WSLOT), BF16),
        "inner": vmem((2, 1, WSLOT), F32),
        "dqkv": vmem((windows, 3 * width, WSLOT), BF16),
        "result_stage": vmem((rows, width), BF16),
        "grad_stage": vmem((2 * WSLOT, width), F32),
        "sem_x": dma((2, windows)),
        "sem_b": dma((2, windows)),
        "sem_result": dma((windows,)),
        "sem_grad": dma((windows,)),
    }
    for name, plan in sizes.plans.items():
        part = plan.shard + plan.extra
        shapes[name + "_pack"] = vmem((2, plan.owners, part, width), BF16)
        shapes[name + "_from_sibling"] = vmem((plan.owners, part, width), BF16)
        shapes[name + "_inbox"] = vmem((peers, part, width), BF16)
        shapes[name + "_total"] = vmem((2, plan.owners, plan.kept, width), BF16)
        shapes[name + "_sems"] = dma((2, 5))
    return shapes


def total_rows(total, shard, start, count):
    _, peers, _, width = total.shape
    at = start
    found = []
    while at < start + count:
        which, inside = divmod(at, peers * shard)
        index, offset = divmod(inside, shard)
        left = start + count - at
        if offset or left < shard:
            take = min(shard - offset, left)
            found.append(total[which, index, offset : offset + take])
        else:
            blocks = min(left // shard, peers - index)
            take = blocks * shard
            found.append(total[which, index : index + blocks, :shard].reshape(take, width))
        at += take
    return found[0] if len(found) == 1 else jnp.concatenate(found, axis=0)


def hand_out(sizes, *refs):
    result_in, grad_in, feed, cross, late, totals, result, grad = refs[:8]
    (o_sq, o_sk, o_sv, o_sm, o_sgain, o_sbias, o_cq, o_ck, o_cv, o_cm, o_cgain, o_cbias,
     o_we, o_ws, o_fgain, o_fbias) = refs[8:24]
    result_stage, grad_stage, sems = refs[24:]
    width, hidden = sizes.width, sizes.hidden
    shards = [plan.shard for plan in sizes.plans.values()]
    loads, stores = [], []
    for kind, (source, stage, target) in enumerate(
        ((grad_in, grad_stage, grad), (result_in, result_stage, result))
    ):
        for w in range(sizes.windows):
            rows = pl.ds(w * WSLOT, WSLOT)
            loads.append(pltpu.make_async_copy(source.at[rows, :], stage.at[rows, :], sems.at[0, kind, w]))
            stores.append(pltpu.make_async_copy(stage.at[rows, :], target.at[rows, :], sems.at[1, kind, w]))
            loads[-1].start()
    half = hidden // 2

    def unpack_expand(at):
        o_we[:width, at : at + half] = total_rows(feed, shards[0], at, half).astype(F32).T
        o_we[width:, at : at + half] = total_rows(feed, shards[0], hidden + at, half).astype(F32).T

    def unpack_rest():
        o_ws[...] = total_rows(feed, shards[0], 2 * hidden, hidden).astype(F32)
        for source, shard, base, group in (
            (cross, shards[1], 0, (o_cq, o_ck, o_cv, o_cm)), (late, shards[2], 0, (o_sq, o_sk, o_sv, o_sm))
        ):
            for i, ref in enumerate(group):
                total = total_rows(source, shard, base + i * width, width).astype(F32)
                ref[...] = total if i == 3 else total.T
        for i, ref in enumerate((o_sgain, o_sbias, o_cgain, o_cbias, o_fgain, o_fbias)):
            ref[...] = totals[i : i + 1, :]

    between = [functools.partial(unpack_expand, 0), functools.partial(unpack_expand, half), unpack_rest]
    for number, (load, store) in enumerate(zip(loads, stores, strict=True)):
        load.wait()
        store.start()
        if number % 2 == 1 and between:
            between.pop(0)()
    for store in stores:
        store.wait()


def local(features, cotangent, slot_pair, crop_size, *weights):
    rows, width = features.shape[1:]
    hidden = weights[12].shape[1]
    peers = lax.axis_size("pix")

    def plan(count, extra=0):
        shard = -(-count // (2 * peers * 16)) * 16
        owners = min(peers, -(-count // (2 * shard)))
        kept = shard + (extra if owners < peers else 0)
        return types.SimpleNamespace(peers=peers, owners=owners, shard=shard, extra=extra, kept=kept)

    sizes = types.SimpleNamespace(
        rows=rows, width=width, hidden=hidden, windows=rows // WSLOT, peers=peers,
        scale=1.0 / math.sqrt(2.0 * rows * peers),
        plans={"feed": plan(3 * hidden), "cross": plan(4 * width), "late": plan(4 * width, 16)},
    )
    flat = lambda value: value.reshape(1, -1) if value.ndim == 1 else value
    shape = jax.ShapeDtypeStruct
    small = pl.BlockSpec(memory_space=pltpu.VMEM)
    large = pl.BlockSpec(memory_space=pl.ANY)
    scalar = pl.BlockSpec(memory_space=pltpu.SMEM)
    square = shape((width, width), F32)
    row = shape((1, width), F32)
    big = [shape((rows, width), BF16), shape((rows, width), F32)]
    middle = pl.pallas_call(
        functools.partial(layer_kernel, sizes),
        in_specs=[small, small, scalar, scalar] + [small] * 16,
        out_specs=[large] * 5 + [small],
        out_shape=big + [
            shape((2, plan.owners, plan.kept, width), BF16) for plan in sizes.plans.values()
        ] + [shape((16, width), F32)],
        scratch_shapes=list(scratch_shapes(sizes).values()),
        compiler_params=pltpu.CompilerParams(
            collective_id=0, has_side_effects=True, vmem_limit_bytes=63 * 2**20
        ),
        name="layer",
    )(features[0], cotangent[0], slot_pair, crop_size.T, *[flat(weight) for weight in weights])
    smalls = [
        square, square, square, square, row, row, square, square, square, square, row, row,
        shape((2 * width, hidden), F32), shape((hidden, width), F32), row, row,
    ]
    moved = [pl.BlockSpec((WSLOT, width), lambda w: (w, 0))] * 2
    whole = lambda shape: pl.BlockSpec(shape, lambda w: (0,) * len(shape))
    smalls = [
        square, square, square, square, row, row, square, square, square, square, row, row,
        shape((2 * width, hidden), F32), shape((hidden, width), F32), row, row,
    ]
    outs = pl.pallas_call(
        functools.partial(hand_out, sizes),
        in_specs=[large, large] + [small] * 4,
        out_specs=[large, large] + [small] * 16,
        out_shape=big + smalls,
        scratch_shapes=[
            pltpu.VMEM((rows, width), BF16), pltpu.VMEM((rows, width), F32),
            pltpu.SemaphoreType.DMA((2, 2, sizes.windows)),
        ],
        compiler_params=pltpu.CompilerParams(vmem_limit_bytes=60 * 2**20),
        name="hand_out",
    )(*middle)
    result, grad = outs[:2]
    return (result[None], grad[None]) + tuple(
        out.reshape(-1) if out.shape[0] == 1 else out for out in outs[2:]
    )


def solution(mesh):
    split = P("frame", "pix", None)
    return jax.shard_map(
        local,
        mesh=mesh,
        in_specs=(split, split, P("pix")) + (P(),) * 17,
        out_specs=(split, split) + (P(),) * 16,
        check_vma=False,
    )
```

```python
import functools
import math
import types

import jax
import jax.numpy as jnp
from jax import lax
from jax.experimental import pallas as pl
from jax.experimental.pallas import tpu as pltpu
from jax.sharding import PartitionSpec as P

WSLOT = 1152
FEWEST = 704
NEGATIVE = -1e30
EPSILON = 1e-05
LOG2E = 1.4426950408889634
F32 = jnp.float32
BF16 = jnp.bfloat16
MESH = pl.DeviceIdType.MESH
TAIL_SHIFT = 2.7777777777777777
TAIL_POLY = (0.39765776262463953, 1.1594294101832299, 1.9333185594349698, 10.032517622923805, -5.2492700447308085, -9.371923274701059)
SPAN = 384
CHUNK = 128
TILES = ((0, 512), (512, 512), (1024, 128))
WIDE = 512
BLOCK = 256
ONES = 16


def nn(left, right):
    return jnp.dot(left, right, preferred_element_type=F32)


def nt(left, right):
    return lax.dot_general(left, right, (((1,), (1,)), ((), ())), preferred_element_type=F32)


def norm_stats(values):
    centre = jnp.mean(values, axis=0, keepdims=True)
    shifted = values - centre
    spread = jnp.mean(shifted * shifted, axis=0, keepdims=True)
    inverse = lax.rsqrt(spread + EPSILON)
    return shifted * inverse, inverse


def norm_back(hat, inverse, gain, upstream):
    scaled = upstream * gain
    first = jnp.mean(scaled, axis=0, keepdims=True)
    second = jnp.mean(scaled * hat, axis=0, keepdims=True)
    return inverse * (scaled - first - hat * second)


def gelu_both(values):
    bell = jnp.exp2(values * (values * (-0.5 * LOG2E))).astype(BF16)
    t = (1.0 / (jnp.abs(values) + TAIL_SHIFT)).astype(BF16)
    low = values.astype(BF16)
    poly = t * BF16(TAIL_POLY[-1]) + BF16(TAIL_POLY[-2])
    for coefficient in TAIL_POLY[-3::-1]:
        poly = poly * t + BF16(coefficient)
    tail = poly * t * bell
    phi = jnp.where(low >= BF16(0.0), BF16(1.0) - tail, tail)
    return low * phi, phi + low * bell * BF16(1.0 / math.sqrt(2.0 * math.pi))


def flip(values):
    return values.astype(F32).T.astype(BF16)


INPUTS = (
    "x", "cot", "slot", "crop", "sq", "sk", "sv", "sm", "sgain", "sbias",
    "cq", "ck", "cv", "cm", "cgain", "cbias", "we", "ws", "fgain", "fbias",
)
OUTPUTS = ("result", "grad", "early_out", "late_out", "totals")
VECTORS = ("sgain", "sbias", "cgain", "cbias", "fgain", "fbias")


def layer_kernel(sizes, *refs):
    names = INPUTS + OUTPUTS + tuple(scratch_shapes(sizes))
    r = types.SimpleNamespace(**dict(zip(names, refs, strict=True)))
    width, hidden, windows, peers = sizes.width, sizes.hidden, sizes.windows, sizes.peers
    factor = 1.0 / math.sqrt(width)
    scale = factor * LOG2E
    frame = lax.axis_index("frame")
    pix = lax.axis_index("pix")
    core = lax.rem(pix, 2)
    me = frame * (peers // 2) + lax.div(pix, 2)
    partner = (1 - frame, pix)
    sibling = (frame, pix + 1 - 2 * core)

    def peer(step):
        index = lax.rem(me + step, peers)
        return index, (lax.div(index, peers // 2), lax.rem(index, peers // 2) * 2 + core)

    barrier = pltpu.get_barrier_semaphore()
    pl.semaphore_signal(barrier, inc=1, device_id=sibling, device_id_type=MESH)

    def greet(step, carry):
        pl.semaphore_signal(barrier, inc=1, device_id=peer(step)[1], device_id_type=MESH)
        return carry

    lax.fori_loop(1, peers, greet, 0)

    slot = r.slot[0]
    live = lax.shift_right_logical(r.crop[0, slot], 1) * lax.shift_right_logical(r.crop[1, slot], 1)

    r.eye[...] = jnp.where(
        lax.broadcasted_iota(jnp.int32, (width, width), 0)
        == lax.broadcasted_iota(jnp.int32, (width, width), 1),
        1.0, 0.0,
    ).astype(BF16)
    r.self_qv_t[:width] = flip(r.sq[...])
    r.self_qv_t[width:] = flip(r.sv[...])
    r.self_k_t[...] = flip(r.sk[...])
    r.self_merge_t[...] = flip(r.sm[...])
    r.self_qkv[:, :width] = r.sq[...]
    r.self_qkv[:, width : 2 * width] = r.sk[...]
    r.self_qkv[:, 2 * width :] = r.sv[...]
    for i, name in enumerate(VECTORS):
        r.vectors[i] = jnp.broadcast_to(getattr(r, name)[...], (width, CHUNK)).T
    vector = lambda name: r.vectors[VECTORS.index(name)]
    for name in ("g_sqkv", "g_sm", "g_cqkv", "g_cm", "g_we", "g_ws", "g_vec"):
        getattr(r, name)[...] = jnp.zeros_like(getattr(r, name))
    r.v_aug[width:, :] = jnp.ones((ONES, WSLOT), BF16)

    def alive_at(start, size):
        token = lax.broadcasted_iota(jnp.int32, (1, size), 1) + lax.rem(start, WSLOT)
        return jnp.where(token < live, 1.0, 0.0)

    def rows_at(w):
        return pl.ds(pl.multiple_of(w * WSLOT, WSLOT), WSLOT)

    def cols_at(w, start=0, size=WSLOT):
        return pl.ds(pl.multiple_of(w * WSLOT + start, 128), size)

    def send_rows(w):
        return pltpu.make_async_remote_copy(
            src_ref=r.send.at[rows_at(w), :], dst_ref=r.other.at[rows_at(w), :],
            send_sem=r.sem_x.at[0, w], recv_sem=r.sem_x.at[1, w], device_id=partner, device_id_type=MESH,
        )

    def send_back(w):
        return pltpu.make_async_remote_copy(
            src_ref=r.back.at[w], dst_ref=r.received.at[w],
            send_sem=r.sem_b.at[0, w], recv_sem=r.sem_b.at[1, w], device_id=partner, device_id_type=MESH,
        )

    def store_rows(target, stage, w, sem):
        return pltpu.make_async_copy(stage.at[rows_at(w), :], target.at[rows_at(w), :], sem.at[w])

    def attend(w, exps, out, inverse):
        bufs = (r.buf_a, r.buf_b)

        def score(t):
            first, size = TILES[t]
            got = nn(r.k[...], r.q_t[:, cols_at(w, first, size)])
            rest = got[FEWEST:]
            row = lax.broadcasted_iota(jnp.int32, rest.shape, 0) + FEWEST
            rest = jnp.where(row < live, rest, NEGATIVE)
            bufs[t % 2][:FEWEST, :size] = got[:FEWEST]
            bufs[t % 2][FEWEST:, :size] = rest
            return scale * jnp.maximum(
                jnp.max(got[:FEWEST], axis=0, keepdims=True), jnp.max(rest, axis=0, keepdims=True)
            )

        def output_part(t, rows, total):
            first, size = TILES[t]
            part = nn(r.v_aug[:, rows], exps[rows, first : first + size])
            return part if total is None else total + part

        def output(t, both):
            first, size = TILES[t]
            share = 1.0 / both[width : width + 1]
            inverse[:, cols_at(w, first, size)] = share
            out[:, cols_at(w, first, size)] = (both[:width] * share).astype(BF16)

        top = score(0)
        for t, (first, size) in enumerate(TILES):
            after = score(t + 1) if t + 1 < len(TILES) else None
            total = None
            for start, count in TILES:
                rows = slice(start, start + count)
                if t:
                    total = output_part(t - 1, rows, total)
                exps[rows, first : first + size] = jnp.exp2(
                    bufs[t % 2][rows, :size] * scale - top
                ).astype(BF16)
            if t:
                output(t - 1, total)
            top = after
        last = len(TILES) - 1
        output(last, output_part(last, slice(0, WSLOT), None))

    def attend_back(w, exps, dqkv):
        def query(t):
            first, size = TILES[t]
            cols = slice(first, first + size)
            dqkv[:width, cols] = (nn(r.k_t[...], r.diff[:, cols]) * factor).astype(BF16)

        for t, (first, size) in enumerate(TILES):
            cols = slice(first, first + size)
            grad = nn(r.v[...], r.up[:, cols]) - r.inner[:, cols]
            r.diff[:, cols] = exps[:, cols] * grad.astype(BF16)
            if t:
                query(t - 1)
        grad_value = nt(exps[...], r.up[...])
        query(len(TILES) - 1)
        grad_key = nt(r.diff[...], r.q_t[:, cols_at(w)]) * factor
        dqkv[2 * width :, :] = grad_value.T.astype(BF16)
        dqkv[width : 2 * width, :] = grad_key.T.astype(BF16)

    def forward_self(w, carry):
        x = r.x[rows_at(w), :]
        stacked = nt(r.self_qv_t[...], x).astype(BF16)
        r.q_t[:, cols_at(w)] = stacked[:width]
        r.v_aug[:width, :] = stacked[width:]
        r.k[...] = nn(x, r.sk[...]).astype(BF16)
        attend(w, r.exps.at[w], r.out_one, r.inverse_one)
        merged = nn(r.self_merge_t[...], r.out_one[:, cols_at(w)])
        x_t = nt(r.eye[...], r.x[rows_at(w), :])
        for start in range(0, WSLOT, CHUNK):
            cols = slice(start, start + CHUNK)
            hat, _ = norm_stats(merged[:, cols])
            x1 = x_t[:, cols] + hat * vector("sgain") + vector("sbias")
            r.x1[:, cols_at(w, start, CHUNK)] = x1
            r.concat[:width, cols_at(w, start, CHUNK)] = x1.astype(BF16)
            r.send[pl.ds(pl.multiple_of(w * WSLOT + start, CHUNK), CHUNK), :] = x1.T.astype(BF16)

        @pl.when(w == 0)
        def _():
            pl.semaphore_wait(barrier, peers)

        send_rows(w).start()
        return carry

    lax.fori_loop(0, windows, forward_self, 0)

    r.cross_q_t[...] = flip(r.cq[...])
    r.cross_k_t[...] = flip(r.ck[...])
    r.cross_v_t[...] = flip(r.cv[...])
    r.cross_merge_t[...] = flip(r.cm[...])
    r.cross_kv[:, :width] = r.ck[...]
    r.cross_kv[:, width:] = r.cv[...]
    r.expand_t[...] = flip(r.we[...])
    r.shrink_t[...] = flip(r.ws[...])

    def forward_cross(w):
        r.q_t[:, cols_at(w)] = nn(r.cross_q_t[...], r.concat[:width, cols_at(w)]).astype(BF16)
        send_rows(w).wait()
        other = r.other[rows_at(w), :]
        r.v_aug[:width, :] = nt(r.cross_v_t[...], other).astype(BF16)
        r.k[...] = nn(other, r.ck[...]).astype(BF16)
        attend(w, r.exps_two.at[lax.rem(w, 2)], r.out_two, r.inverse_two)
        merged = nn(r.cross_merge_t[...], r.out_two[:, cols_at(w)])
        for start in range(0, WSLOT, CHUNK):
            hat, _ = norm_stats(merged[:, start : start + CHUNK])
            r.concat[width:, cols_at(w, start, CHUNK)] = (
                hat * vector("cgain") + vector("cbias")
            ).astype(BF16)

    spans = sizes.rows // SPAN

    def span(i):
        return pl.ds(pl.multiple_of(i * SPAN, SPAN), SPAN)

    def norm_tile(i, b, branch, up_all, start):
        part = slice(start, start + CHUNK)
        here = pl.ds(pl.multiple_of(i * SPAN + start, CHUNK), CHUNK)
        alive = alive_at(i * SPAN + start, CHUNK)
        hat, inverse = norm_stats(branch[:, part])
        result = (r.x1[:, here] + hat * vector("fgain") + vector("fbias")) * alive
        r.result_stage[here, :] = result.T.astype(BF16)
        up = up_all[:, part] * alive
        r.x1[:, here] = up
        r.g_vec[4] += up * hat
        r.g_vec[5] += up
        r.branch[b, :, part] = norm_back(hat, inverse, vector("fgain"), up).astype(BF16)

    def settle(i, total):
        r.x1[:, span(i)] += total[:width]
        r.grad_normed[:, span(lax.rem(i, per_half))] = total[width:]

    parts = [slice(start, start + BLOCK) for start in range(0, hidden, BLOCK)]

    def expand(i):
        r.buf_a[:hidden, :SPAN] = nn(r.expand_t[...], r.concat[:, span(i)])

    def activate(b, rows):
        act, slope = gelu_both(r.buf_a[rows, :SPAN])
        r.act[b, rows, :] = act
        r.slope[b, rows, :] = slope

    def hide(b):
        r.hid[...] = r.slope[b] * nn(r.ws[...], r.branch[b]).astype(BF16)

    def add(total, part):
        return part if total is None else total + part

    per_half = 2 * WSLOT // SPAN

    def feed_forward(half):
        first = per_half * half
        for name in ("act", "slope", "branch"):
            getattr(r, name)[2] = jnp.zeros(getattr(r, name).shape[1:], BF16)
        expand(first)
        for rows in parts:
            activate(0, rows)

        def feed(j, carry):
            for b in range(3):
                i = first + 3 * j + b
                old = (b + 2) % 3
                before = jnp.maximum(i - 1, first)
                expand(jnp.minimum(i + 1, spans - 1))
                hide(old)
                branch, total = None, None
                for rows in parts:
                    branch = add(branch, nn(r.shrink_t[:, rows], r.act[b, rows, :]))
                    total = add(total, nn(r.we[:, rows], r.hid[rows, :]))
                    activate((b + 1) % 3, rows)
                settle(before, total)
                up_all = nt(r.eye[...], r.cot[span(i), :])
                for_shrink = nt(r.act[old], r.branch[old])
                norm_tile(i, b, branch, up_all, 0)
                for_expand = nt(r.hid[...], r.concat[:, span(before)])
                for start in range(CHUNK, SPAN, CHUNK):
                    norm_tile(i, b, branch, up_all, start)
                r.g_ws[...] += for_shrink
                r.g_we[...] += for_expand
            return carry

        lax.fori_loop(0, per_half // 3, feed, 0)
        end = first + per_half - 1
        last = (per_half - 1) % 3
        hide(last)
        settle(end, nn(r.we[...], r.hid[...]))
        r.g_ws[...] += nt(r.act[last], r.branch[last])
        r.g_we[...] += nt(r.hid[...], r.concat[:, span(end)])

    def upstream(w, merged, grad_at, number, gain, out, gradient, merge, inverse):
        sums = [jnp.zeros((width, CHUNK), F32)] * 2
        for start in range(0, WSLOT, CHUNK):
            hat, root = norm_stats(merged[:, start : start + CHUNK])
            grad = grad_at(start)
            sums = [sums[0] + grad * hat, sums[1] + grad]
            r.grad_merged[:, start : start + CHUNK] = norm_back(hat, root, vector(gain), grad).astype(BF16)
        r.g_vec[number] += sums[0]
        r.g_vec[number + 1] += sums[1]
        out = out[:, cols_at(w)]
        gradient[...] += nt(out, r.grad_merged[...])
        up = (nn(merge[...], r.grad_merged[...]) * inverse[:, cols_at(w)]).astype(BF16)
        r.up[...] = up
        r.inner[...] = jnp.sum(up.astype(F32) * out.astype(F32), axis=0, keepdims=True)

    def backward_cross(w):
        exps = r.exps_two.at[lax.rem(w, 2)]
        dqkv = r.dqkv.at[w]
        upstream(
            w, nn(r.cross_merge_t[...], r.out_two[:, cols_at(w)]),
            lambda start: r.grad_normed[:, cols_at(lax.rem(w, 2), start, CHUNK)],
            2, "cgain", r.out_two, r.g_cm, r.cm, r.inverse_two,
        )
        other = r.other[rows_at(w), :]
        r.k_t[...] = nt(r.cross_k_t[...], other).astype(BF16)
        r.v[...] = nn(other, r.cv[...]).astype(BF16)
        attend_back(w, exps, dqkv)
        r.back[w] = nn(r.cross_kv[...], dqkv[width:, :]).astype(BF16)
        send_back(w).start()
        r.g_cqkv[:width] += nt(dqkv[:width, :], r.concat[:width, cols_at(w)])
        r.g_cqkv[width:] += nn(dqkv[width:, :], r.other[rows_at(w), :])
        r.x1[:, cols_at(w)] += nn(r.cq[...], dqkv[:width, :])

    def middle(half, carry):
        def before(u, carry):
            forward_cross(2 * half + u)
            return carry

        lax.fori_loop(0, 2, before, 0)
        feed_forward(half)

        def after(u, carry):
            store_rows(r.result, r.result_stage, 2 * half + u, r.sem_result).start()
            backward_cross(2 * half + u)
            return carry

        lax.fori_loop(0, 2, after, 0)
        return carry

    lax.fori_loop(0, windows // 2, middle, 0)

    early = Reduction(r, sizes.plans["early"], "early", sizes.scale, sibling, peer, core, me)
    late = Reduction(r, sizes.plans["late"], "late", sizes.scale, sibling, peer, core, me)
    early.begin(
        [r.g_we.at[:, pl.ds(0, width)], r.g_we.at[:, pl.ds(width, width)], r.g_ws, r.g_cqkv, r.g_cm]
    )

    def backward_self(w, carry):
        @pl.when(w == 1)
        def _():
            early.scatter()

        @pl.when(w == windows - 1)
        def _():
            early.gather()

        exps = r.exps.at[w]
        dqkv = r.dqkv.at[w]
        x = r.x[rows_at(w), :]
        r.q_t[:, cols_at(w)] = nt(r.self_qv_t[:width, :], x).astype(BF16)
        r.k_t[...] = nt(r.self_k_t[...], x).astype(BF16)
        r.v[...] = nn(x, r.sv[...]).astype(BF16)
        send_back(w).wait()

        def grad_at(start):
            here = cols_at(w, start, CHUNK)
            grad = r.x1[:, here] + r.received[w, :, start : start + CHUNK].astype(F32)
            r.x1[:, here] = grad
            return grad

        upstream(
            w, nn(r.self_merge_t[...], r.out_one[:, cols_at(w)]), grad_at,
            0, "sgain", r.out_one, r.g_sm, r.sm, r.inverse_one,
        )
        attend_back(w, exps, dqkv)
        r.g_sqkv[...] += nn(dqkv[...], r.x[rows_at(w), :])
        return carry

    lax.fori_loop(0, windows, backward_self, 0)

    def finish(w):
        place = w % 2
        stage = r.grad_stage.at[pl.ds(place * WSLOT, WSLOT), :]
        if w >= 2:
            store_grad(w - 2).wait()
        stage[...] = (r.x1[:, cols_at(w)] + nn(r.self_qkv[...], r.dqkv[w])).T
        store_grad(w).start()

    def store_grad(w):
        place = w % 2
        return pltpu.make_async_copy(
            r.grad_stage.at[pl.ds(place * WSLOT, WSLOT), :], r.grad.at[pl.ds(w * WSLOT, WSLOT), :],
            r.sem_grad.at[w],
        )

    late.begin([r.g_sqkv, r.g_sm], r.g_vec)
    early.share()
    finish(0)
    late.scatter()
    early.finish()
    early.store(r.early_out).start()
    finish(1)
    late.gather()
    if late.full:
        r.totals[...] = late.vector_total()
    finish(2)
    late.share()
    finish(3)
    late.finish()
    late.store(r.late_out).start()
    if not late.full:
        r.totals[...] = late.total[0, 0, late.shard :].astype(F32)

    def drain(w, carry):
        store_rows(r.result, r.result_stage, w, r.sem_result).wait()
        return carry

    lax.fori_loop(0, windows, drain, 0)
    store_grad(2).wait()
    store_grad(3).wait()
    early.store(r.early_out).wait()
    late.store(r.late_out).wait()


class Reduction:
    def __init__(self, r, plan, name, scale, sibling, peer, core, me):
        self.sibling, self.peer, self.core, self.me = sibling, peer, core, me
        self.scale = scale
        self.peers, self.owners, self.shard, self.extra, self.kept = (
            plan.peers, plan.owners, plan.shard, plan.extra, plan.kept
        )
        self.half = self.owners * self.shard
        self.full = self.owners == self.peers
        for field in ("pack", "from_sibling", "inbox", "total", "sems"):
            setattr(self, field, getattr(r, name + "_" + field))

    def copy(self, source, target, number, device):
        return pltpu.make_async_remote_copy(
            src_ref=source, dst_ref=target, send_sem=self.sems.at[0, number],
            recv_sem=self.sems.at[1, number], device_id=device, device_id_type=MESH,
        )

    def owning(self, then, otherwise=None):
        if self.full:
            then()
        else:
            pl.when(self.me < self.owners)(then)
            if otherwise is not None:
                pl.when(self.me >= self.owners)(otherwise)

    def halves(self):
        return self.copy(self.pack.at[1 - self.core], self.from_sibling, 0, self.sibling)

    def begin(self, pieces, vec=None):
        at = 0
        width = self.pack.shape[3]
        for piece in pieces:
            taken = 0
            while taken < piece.shape[0]:
                which, inside = divmod(at, self.half)
                index, offset = divmod(inside, self.shard)
                left = piece.shape[0] - taken
                if offset or left < self.shard:
                    count = min(left, self.shard - offset)
                    self.pack[which, index, offset : offset + count] = piece[
                        taken : taken + count, :
                    ].astype(BF16)
                else:
                    blocks = min(left // self.shard, self.owners - index)
                    count = blocks * self.shard
                    self.pack[which, index : index + blocks, : self.shard] = (
                        piece[taken : taken + count, :].astype(BF16).reshape(blocks, self.shard, width)
                    )
                at += count
                taken += count
        while at < 2 * self.half:
            which, inside = divmod(at, self.half)
            index, offset = divmod(inside, self.shard)
            count = self.shard - offset
            self.pack[which, index, offset : self.shard] = jnp.zeros((count, width), BF16)
            at += count
        if self.extra:
            sums = jnp.concatenate([jnp.sum(vec[i].T, axis=0, keepdims=True) for i in range(vec.shape[0])])
            rows = jnp.concatenate([sums, jnp.zeros((self.extra - vec.shape[0], width), F32)]).astype(BF16)
            for which in range(2):
                self.pack[which, :, self.shard :] = jnp.broadcast_to(
                    rows[None], (self.owners, self.extra, width)
                )
        self.halves().start()

    def wait(self, number, sent, received):
        if sent is not None:
            self.copy(sent, sent, number, self.sibling).wait_send()
        if received is not None:
            self.copy(received, received, number, self.sibling).wait_recv()

    def scatter(self):
        self.halves().wait()
        mine = self.pack[self.core].astype(F32) + self.from_sibling[...].astype(F32)
        self.pack[self.core] = mine.astype(BF16)

        def send(step, carry):
            index, device = self.peer(step)

            def go():
                place = self.pack.at[self.core, index]
                self.copy(place, self.inbox.at[self.me], 1, device).start()

            go() if self.full else pl.when(index < self.owners)(go)
            return carry

        lax.fori_loop(1, self.peers, send, 0)

        def own():
            self.inbox[self.me] = self.pack[self.core, self.me]

        self.owning(own)

    def gather(self):
        def own():
            self.wait(
                1, self.pack.at[0, pl.ds(0, self.owners - 1)], self.inbox.at[pl.ds(0, self.peers - 1)]
            )
            total = jnp.sum(self.inbox[:, : self.kept].astype(F32), axis=0) * self.scale
            self.total[self.core, self.me] = total.astype(BF16)

            def send(step, carry):
                place = self.total.at[self.core, self.me]
                self.copy(place, place, 2, self.peer(step)[1]).start()
                return carry

            lax.fori_loop(1, self.peers, send, 0)

        self.owning(own, lambda: self.wait(1, self.pack.at[0], None))

    def vector_total(self):
        return jnp.sum(self.inbox[:, self.shard :].astype(F32), axis=0) * self.scale

    def share(self):
        def own():
            for count in (self.owners - 1,) * ((self.peers - 1) // (self.owners - 1)) + (
                (self.peers - 1) % (self.owners - 1),
            ):
                if count:
                    self.wait(2, self.total.at[0, pl.ds(0, count)], None)
            self.wait(2, None, self.total.at[0, pl.ds(0, self.owners - 1)])

        self.owning(own, lambda: self.wait(2, None, self.total.at[0]))
        self.copy(self.total.at[self.core], self.total.at[self.core], 3, self.sibling).start()

    def finish(self):
        self.copy(self.total.at[self.core], self.total.at[self.core], 3, self.sibling).wait()

    def store(self, target):
        return pltpu.make_async_copy(self.total, target, self.sems.at[0, 4])


def scratch_shapes(sizes):
    width, hidden, windows, rows, peers = sizes.width, sizes.hidden, sizes.windows, sizes.rows, sizes.peers
    vmem = pltpu.VMEM
    dma = pltpu.SemaphoreType.DMA
    square = vmem((width, width), F32)
    shapes = {
        "eye": vmem((width, width), BF16),
        "self_qv_t": vmem((2 * width, width), BF16),
        "self_k_t": vmem((width, width), BF16),
        "self_merge_t": vmem((width, width), BF16),
        "self_qkv": vmem((width, 3 * width), BF16),
        "vectors": vmem((len(VECTORS), width, CHUNK), F32),
        "cross_q_t": vmem((width, width), BF16),
        "cross_k_t": vmem((width, width), BF16),
        "cross_v_t": vmem((width, width), BF16),
        "cross_merge_t": vmem((width, width), BF16),
        "cross_kv": vmem((width, 2 * width), BF16),
        "expand_t": vmem((hidden, 2 * width), BF16),
        "shrink_t": vmem((width, hidden), BF16),
        "g_sqkv": vmem((3 * width, width), F32),
        "g_cqkv": vmem((3 * width, width), F32),
        "g_sm": square,
        "g_cm": square,
        "g_we": vmem((hidden, 2 * width), F32),
        "g_ws": vmem((hidden, width), F32),
        "g_vec": vmem((len(VECTORS), width, CHUNK), F32),
        "q_t": vmem((width, rows), BF16),
        "k": vmem((WSLOT, width), BF16),
        "v_aug": vmem((width + ONES, WSLOT), BF16),
        "out_one": vmem((width, rows), BF16),
        "out_two": vmem((width, rows), BF16),
        "inverse_one": vmem((1, rows), F32),
        "inverse_two": vmem((1, rows), F32),
        "x1": vmem((width, rows), F32),
        "concat": vmem((2 * width, rows), BF16),
        "send": vmem((rows, width), BF16),
        "other": vmem((rows, width), BF16),
        "back": vmem((windows, width, WSLOT), BF16),
        "received": vmem((windows, width, WSLOT), BF16),
        "grad_normed": vmem((width, 2 * WSLOT), F32),
        "exps": vmem((windows, WSLOT, WSLOT), BF16),
        "exps_two": vmem((2, WSLOT, WSLOT), BF16),
        "diff": vmem((WSLOT, WSLOT), BF16),
        "act": vmem((3, hidden, SPAN), BF16),
        "slope": vmem((3, hidden, SPAN), BF16),
        "branch": vmem((3, width, SPAN), BF16),
        "hid": vmem((hidden, SPAN), BF16),
        "buf_a": vmem((max(WSLOT, hidden), WIDE), F32),
        "buf_b": vmem((WSLOT, WIDE), F32),
        "grad_merged": vmem((width, WSLOT), BF16),
        "k_t": vmem((width, WSLOT), BF16),
        "v": vmem((WSLOT, width), BF16),
        "up": vmem((width, WSLOT), BF16),
        "inner": vmem((1, WSLOT), F32),
        "dqkv": vmem((windows, 3 * width, WSLOT), BF16),
        "result_stage": vmem((rows, width), BF16),
        "grad_stage": vmem((2 * WSLOT, width), F32),
        "sem_x": dma((2, windows)),
        "sem_b": dma((2, windows)),
        "sem_result": dma((windows,)),
        "sem_grad": dma((windows,)),
    }
    for name, plan in sizes.plans.items():
        part = plan.shard + plan.extra
        shapes[name + "_pack"] = vmem((2, plan.owners, part, width), BF16)
        shapes[name + "_from_sibling"] = vmem((plan.owners, part, width), BF16)
        shapes[name + "_inbox"] = vmem((peers, part, width), BF16)
        shapes[name + "_total"] = vmem((2, plan.owners, plan.kept, width), BF16)
        shapes[name + "_sems"] = dma((2, 5))
    return shapes


def total_rows(total, shard, start, count):
    _, peers, _, width = total.shape
    at = start
    found = []
    while at < start + count:
        which, inside = divmod(at, peers * shard)
        index, offset = divmod(inside, shard)
        left = start + count - at
        if offset or left < shard:
            take = min(shard - offset, left)
            found.append(total[which, index, offset : offset + take])
        else:
            blocks = min(left // shard, peers - index)
            take = blocks * shard
            found.append(total[which, index : index + blocks, :shard].reshape(take, width))
        at += take
    return found[0] if len(found) == 1 else jnp.concatenate(found, axis=0)


def hand_out(sizes, *refs):
    result_in, grad_in, early, late, totals, result, grad = refs[:7]
    (o_sq, o_sk, o_sv, o_sm, o_sgain, o_sbias, o_cq, o_ck, o_cv, o_cm, o_cgain, o_cbias,
     o_we, o_ws, o_fgain, o_fbias) = refs[7:23]
    result_stage, grad_stage, sems = refs[23:]
    width, hidden = sizes.width, sizes.hidden
    shards = [plan.shard for plan in sizes.plans.values()]
    loads, stores = [], []
    for kind, (source, stage, target) in enumerate(
        ((grad_in, grad_stage, grad), (result_in, result_stage, result))
    ):
        for w in range(sizes.windows):
            rows = pl.ds(w * WSLOT, WSLOT)
            loads.append(pltpu.make_async_copy(source.at[rows, :], stage.at[rows, :], sems.at[0, kind, w]))
            stores.append(pltpu.make_async_copy(stage.at[rows, :], target.at[rows, :], sems.at[1, kind, w]))
            loads[-1].start()
    half = hidden // 2

    def unpack_expand(at):
        o_we[:width, at : at + half] = total_rows(early, shards[0], at, half).astype(F32).T
        o_we[width:, at : at + half] = total_rows(early, shards[0], hidden + at, half).astype(F32).T

    def unpack_rest():
        o_ws[...] = total_rows(early, shards[0], 2 * hidden, hidden).astype(F32)
        for source, shard, base, group in (
            (early, shards[0], 3 * hidden, (o_cq, o_ck, o_cv, o_cm)), (late, shards[1], 0, (o_sq, o_sk, o_sv, o_sm))
        ):
            for i, ref in enumerate(group):
                total = total_rows(source, shard, base + i * width, width).astype(F32)
                ref[...] = total if i == 3 else total.T
        for i, ref in enumerate((o_sgain, o_sbias, o_cgain, o_cbias, o_fgain, o_fbias)):
            ref[...] = totals[i : i + 1, :]

    between = [functools.partial(unpack_expand, 0), functools.partial(unpack_expand, half), unpack_rest]
    for number, (load, store) in enumerate(zip(loads, stores, strict=True)):
        load.wait()
        store.start()
        if number % 2 == 1 and between:
            between.pop(0)()
    for store in stores:
        store.wait()


def local(features, cotangent, slot_pair, crop_size, *weights):
    rows, width = features.shape[1:]
    hidden = weights[12].shape[1]
    peers = lax.axis_size("pix")

    def plan(count, extra=0):
        shard = -(-count // (2 * peers * 16)) * 16
        owners = min(peers, -(-count // (2 * shard)))
        kept = shard + (extra if owners < peers else 0)
        return types.SimpleNamespace(peers=peers, owners=owners, shard=shard, extra=extra, kept=kept)

    sizes = types.SimpleNamespace(
        rows=rows, width=width, hidden=hidden, windows=rows // WSLOT, peers=peers,
        scale=1.0 / math.sqrt(2.0 * rows * peers),
        plans={"early": plan(3 * hidden + 4 * width), "late": plan(4 * width, 16)},
    )
    flat = lambda value: value.reshape(1, -1) if value.ndim == 1 else value
    shape = jax.ShapeDtypeStruct
    small = pl.BlockSpec(memory_space=pltpu.VMEM)
    large = pl.BlockSpec(memory_space=pl.ANY)
    scalar = pl.BlockSpec(memory_space=pltpu.SMEM)
    square = shape((width, width), F32)
    row = shape((1, width), F32)
    big = [shape((rows, width), BF16), shape((rows, width), F32)]
    middle = pl.pallas_call(
        functools.partial(layer_kernel, sizes),
        in_specs=[small, small, scalar, scalar] + [small] * 16,
        out_specs=[large] * 4 + [small],
        out_shape=big + [
            shape((2, plan.owners, plan.kept, width), BF16) for plan in sizes.plans.values()
        ] + [shape((16, width), F32)],
        scratch_shapes=list(scratch_shapes(sizes).values()),
        compiler_params=pltpu.CompilerParams(
            collective_id=0, has_side_effects=True, vmem_limit_bytes=63 * 2**20
        ),
        name="layer",
    )(features[0], cotangent[0], slot_pair, crop_size.T, *[flat(weight) for weight in weights])
    smalls = [
        square, square, square, square, row, row, square, square, square, square, row, row,
        shape((2 * width, hidden), F32), shape((hidden, width), F32), row, row,
    ]
    moved = [pl.BlockSpec((WSLOT, width), lambda w: (w, 0))] * 2
    whole = lambda shape: pl.BlockSpec(shape, lambda w: (0,) * len(shape))
    smalls = [
        square, square, square, square, row, row, square, square, square, square, row, row,
        shape((2 * width, hidden), F32), shape((hidden, width), F32), row, row,
    ]
    outs = pl.pallas_call(
        functools.partial(hand_out, sizes),
        in_specs=[large, large] + [small] * 3,
        out_specs=[large, large] + [small] * 16,
        out_shape=big + smalls,
        scratch_shapes=[
            pltpu.VMEM((rows, width), BF16), pltpu.VMEM((rows, width), F32),
            pltpu.SemaphoreType.DMA((2, 2, sizes.windows)),
        ],
        compiler_params=pltpu.CompilerParams(vmem_limit_bytes=60 * 2**20),
        name="hand_out",
    )(*middle)
    result, grad = outs[:2]
    return (result[None], grad[None]) + tuple(
        out.reshape(-1) if out.shape[0] == 1 else out for out in outs[2:]
    )


def solution(mesh):
    split = P("frame", "pix", None)
    return jax.shard_map(
        local,
        mesh=mesh,
        in_specs=(split, split, P("pix")) + (P(),) * 17,
        out_specs=(split, split) + (P(),) * 16,
        check_vma=False,
    )
```
